256 devices in a mesh: dp: 32 (over z_hi, x, y), graph: 8 (over z_lo, core).
Axes of the slice: x: 4, y: 4, z: 8 (z_hi: 2, z_lo: 4; z = z_hi * 4 + z_lo), core: 2. Of those that a mesh axis runs over, the one named last changes fastest.
Arguments:
- node_features: bfloat16 [32, 128, 49, 128], P('dp', 'graph'), may hold values from -6 to 6
- edge_embed: bfloat16 [32, 1024, 128], P('dp', 'graph'), may hold values from -6 to 6
- sources: int32 [32, 1024], P('dp', 'graph'), may hold values from 0 to 127
- targets: int32 [32, 1024], P('dp', 'graph'), may hold values from 0 to 127
- edge_counts: int32 [32, 8], P('dp', 'graph'), may hold values from 8 to 128, as said below
- w_zero: bfloat16 [2, 896, 448], replicated, may hold values from -0.1875 to 0.1875
- w_one: bfloat16 [2, 768, 768], replicated, may hold values from -0.15625 to 0.15625
- w_two: bfloat16 [2, 640, 640], replicated, may hold values from -0.15625 to 0.15625
- radial: bfloat16 [2, 128, 2304], replicated, may hold values from -0.5 to 0.5
- query: bfloat16 [2, 128, 64], replicated, may hold values from -0.5 to 0.5
- w_out: bfloat16 [2, 7, 64, 128], replicated, may hold values from -0.75 to 0.75
- cotangent: bfloat16 [32, 128, 49, 128], P('dp', 'graph'), may hold values from -0.078125 to 0.078125
Outputs:
- out_features: bfloat16 [32, 128, 49, 128], P('dp', 'graph')
- grad_zero: float32 [2, 896, 448], P(None, 'graph', 'dp')
- grad_one: float32 [2, 768, 768], P(None, 'graph', 'dp')
- grad_two: float32 [2, 640, 640], P(None, 'graph', 'dp')
- grad_radial: float32 [2, 128, 2304], P(None, 'graph', 'dp')
- grad_query: float32 [2, 128, 64], P(None, 'graph', 'dp')
- grad_out: float32 [2, 7, 64, 128], P(None, None, 'dp', 'graph')
The draws below stay inside these ranges and needn't reach their ends.
Inputs may be any that keep to these rules, and one draw needn't show every extreme that they name: `sources`: node n of a graph belongs to shard n // 16; slots at or past a shard's edge count are padding and hold arbitrary node numbers. `targets`: same numbering as sources. `edge_counts`: in every graph at least one shard has all 128 slots live.
All inputs are finite; a program needn't handle non-finite values.
Results may differ from the reference program's by a relative error of at most 0.04.
Values may be sent and summed in bfloat16 or wider, within the bound.
No kernel may reach another device: no remote copies, remote signals or barrier semaphores. Data moves between devices by JAX's collectives and lax.ppermute only.
A program may use at most 128 MiB of HBM per device.

```python
import functools
import jax
import jax.numpy as jnp
import numpy as np
from jax import lax

CH = 128
HID = 64
ECH = 128
HEADS = 8
LMAX = 6
NODE_DEV = 16
EDGE_DEV = 128
LAYERS = 2
GRAPHS = 32
NODES_G = 128
EDGES_G = 1024
N_DP = 32
N_GRAPH = 8


def draw_edge_counts(key, part):
    key = jax.random.fold_in(key, 11)
    key_counts, key_full = jax.random.split(key)
    counts = jax.random.randint(key_counts, (GRAPHS, N_GRAPH), EDGE_DEV // 16, EDGE_DEV + 1)
    full_shard = jax.random.randint(key_full, (GRAPHS, 1), 0, N_GRAPH)
    slot_ids = jnp.arange(N_GRAPH)[None, :]
    return jnp.where(slot_ids == full_shard, EDGE_DEV, counts).astype(jnp.int32)


def with_ends(values, stream_key, low, largest):
    dims = values.shape
    place = [jax.random.randint(jax.random.fold_in(stream_key, axis), (), 0, dims[axis]) for axis in range(len(dims))]
    values = values.at[tuple(place)].set(low)
    longest = dims.index(max(dims))
    place[longest] = (place[longest] + 1) % dims[longest]
    return values.at[tuple(place)].set(largest)


def levels(stream_key, extent, cuts, least, high):
    def one(dim, parts):
        steps = jax.random.uniform(jax.random.fold_in(jax.random.fold_in(stream_key, 6), dim), (parts,), jnp.float32, least / len(cuts), high / len(cuts))
        return jnp.repeat(jnp.exp(steps), extent[dim] // parts).reshape((-1,) + (1,) * (len(extent) - dim - 1))

    gain = one(*cuts[0])
    for cut in cuts[1:]:
        gain = gain * one(*cut)
    return gain


def normal_values(rng, extent, spread, bound, cuts=(), held_as=jnp.bfloat16):
    level = levels(rng, extent, cuts, -0.22, 0.18) if cuts else 1.0
    values = jax.random.normal(rng, extent, jnp.float32) * spread * level
    return jnp.minimum(jnp.maximum(values, -bound), bound).astype(held_as)


def setup_inputs(seed: int = 0) -> dict:
    splits = jax.random.split(jax.random.key(seed), 13)
    return {
        "node_features": normal_values(splits[0], (GRAPHS, NODES_G, (LMAX + 1) ** 2, CH), 1.0, 6.0, ((0, 32), (1, 8))),
        "edge_embed": normal_values(splits[1], (GRAPHS, EDGES_G, ECH), 1.0, 6.0, ((0, 32), (1, 8))),
        "sources": with_ends(jax.random.randint(splits[2], (GRAPHS, EDGES_G), 0, NODES_G), jax.random.fold_in(splits[2], 1), 0, NODES_G - 1).astype(jnp.int32),
        "targets": with_ends(jax.random.randint(splits[3], (GRAPHS, EDGES_G), 0, NODES_G), jax.random.fold_in(splits[3], 1), 0, NODES_G - 1).astype(jnp.int32),
        "edge_counts": draw_edge_counts(jax.random.fold_in(splits[12], 71), 0),
        "w_zero": normal_values(splits[5], (LAYERS, (LMAX + 1) * CH, (LMAX + 1) * HID), ((LMAX + 1) * CH) ** -0.5, 0.1875),
        "w_one": normal_values(splits[6], (LAYERS, LMAX * CH, 2 * LMAX * HID), (2 * LMAX * CH) ** -0.5, 0.15625),
        "w_two": normal_values(splits[7], (LAYERS, (LMAX - 1) * CH, 2 * (LMAX - 1) * HID), (2 * (LMAX - 1) * CH) ** -0.5, 0.15625),
        "radial": normal_values(splits[8], (LAYERS, ECH, 3 * LMAX * CH), ECH ** -0.5, 0.5),
        "query": normal_values(splits[9], (LAYERS, CH, HID), CH ** -0.5, 0.5),
        "w_out": normal_values(splits[10], (LAYERS, LMAX + 1, HID, CH), HID ** -0.5, 0.75),
        "cotangent": normal_values(splits[11], (GRAPHS, NODES_G, (LMAX + 1) ** 2, CH), (1.0 / (EDGE_DEV * N_GRAPH * N_DP) ** 0.5), 0.078125, ((0, 32), (1, 8))),
    }


group_of_coef = np.array(list(range(7)) + list(range(7, 13)) * 2 + list(range(13, 18)) * 2, dtype=np.int32)
degree_of_coef = np.array(list(range(7)) + list(range(1, 7)) * 2 + list(range(2, 7)) * 2, dtype=np.int32)
group_table = np.asarray(group_of_coef[:, None] == np.arange(18)[None, :], dtype=np.float32)
degree_table = np.asarray(degree_of_coef[:, None] == np.arange(7)[None, :], dtype=np.float32)
norm_eps = 1e-06

def contract(left_side, right_side):
    return lax.dot_general(left_side, right_side, (((0,), (0,)), ((), ())), preferred_element_type=jnp.float32)

def contract_last(left_side, right_side):
    return lax.dot_general(left_side, right_side, (((1,), (1,)), ((), ())), preferred_element_type=jnp.float32)

def rounded(values):
    return lax.optimization_barrier(values.astype(jnp.bfloat16)).astype(jnp.float32)

def pair_forward(plus_part, minus_part, weight):
    edge_total = plus_part.shape[0]
    stacked = jnp.concatenate([plus_part.reshape(edge_total, -1), minus_part.reshape(edge_total, -1)], axis=0)
    product = jnp.dot(stacked, weight, preferred_element_type=jnp.float32)
    half_width = weight.shape[1] // 2
    plus_prod = product[:edge_total]
    minus_prod = product[edge_total:]
    out_plus = plus_prod[:, :half_width] - minus_prod[:, half_width:]
    out_minus = minus_prod[:, :half_width] + plus_prod[:, half_width:]
    unit_width = half_width // plus_part.shape[1]
    return (out_plus.reshape(edge_total, -1, unit_width), out_minus.reshape(edge_total, -1, unit_width))

def pair_backward(plus_part, minus_part, grad_plus, grad_minus, weight):
    edge_total = plus_part.shape[0]
    stacked = jnp.concatenate([plus_part.reshape(edge_total, -1), minus_part.reshape(edge_total, -1)], axis=0)
    flat_plus = grad_plus.reshape(edge_total, -1)
    flat_minus = grad_minus.reshape(edge_total, -1)
    grad_stack = jnp.concatenate([jnp.concatenate([flat_plus, flat_minus], axis=1), jnp.concatenate([flat_minus, -flat_plus], axis=1)], axis=0)
    weight_grad = contract(stacked, grad_stack)
    input_grad = contract_last(grad_stack, weight)
    coef_count = plus_part.shape[1]
    return (weight_grad, input_grad[:edge_total].reshape(edge_total, coef_count, -1), input_grad[edge_total:].reshape(edge_total, coef_count, -1))

def edge_forward(group_rows, edge_rows, source_ids, target_ids, live_mask, weight_zero, weight_one, weight_two, radial_weight, query_weight):
    edge_total = source_ids.shape[0]
    channels = group_rows.shape[2]
    hidden = query_weight.shape[1]
    head_width = hidden // HEADS
    radial_rows = jnp.dot(edge_rows, radial_weight, preferred_element_type=jnp.float32).reshape(edge_total, -1, channels)
    coef_scale = radial_rows[:, group_of_coef]
    source_rows = jnp.take(group_rows, source_ids, axis=0)
    scaled = (source_rows.astype(jnp.float32) * coef_scale).astype(jnp.bfloat16)
    value_zero = jnp.dot(scaled[:, :7].reshape(edge_total, -1), weight_zero, preferred_element_type=jnp.float32).reshape(edge_total, 7, hidden)
    one_plus, one_minus = pair_forward(scaled[:, 7:13], scaled[:, 13:19], weight_one)
    two_plus, two_minus = pair_forward(scaled[:, 19:24], scaled[:, 24:29], weight_two)
    values = jnp.concatenate([value_zero, one_plus, one_minus, two_plus, two_minus], axis=1)
    queries = jnp.dot(group_rows[:, 0], query_weight, preferred_element_type=jnp.float32)
    target_query = jnp.take(queries, target_ids, axis=0)
    logits = (values[:, 0] * target_query).reshape(edge_total, HEADS, head_width).sum(axis=-1) * head_width ** (-0.5)
    gate_values = jax.nn.sigmoid(logits)
    weights_live = gate_values * live_mask[:, None]
    messages = (values.reshape(edge_total, 29, HEADS, head_width) * weights_live[:, None, :, None]).reshape(edge_total, 29, hidden).astype(jnp.bfloat16)
    return (messages, (source_rows, coef_scale, scaled, values, target_query, gate_values, weights_live))

def edge_backward(grad_messages, kept_arrays, edge_rows, group_rows, source_ids, target_ids, live_mask, weight_zero, weight_one, weight_two, query_weight, with_source):
    source_rows, coef_scale, scaled, values, target_query, gate_values, weights_live = kept_arrays
    edge_total = source_ids.shape[0]
    hidden = values.shape[2]
    head_width = hidden // HEADS
    split_grad = grad_messages.reshape(edge_total, 29, HEADS, head_width)
    grad_weights = (split_grad * values.reshape(edge_total, 29, HEADS, head_width)).sum(axis=(1, 3))
    grad_values = (split_grad * weights_live[:, None, :, None]).reshape(edge_total, 29, hidden)
    grad_logits = grad_weights * gate_values * (1.0 - gate_values) * live_mask[:, None]
    per_channel = jnp.repeat(grad_logits, head_width, axis=1) * head_width ** (-0.5)
    grad_values = grad_values.at[:, 0].add(per_channel * target_query)
    grad_query_rows = (per_channel * values[:, 0]).astype(jnp.bfloat16)
    target_rows = jnp.take(group_rows[:, 0], target_ids, axis=0)
    query_grad = contract(target_rows, grad_query_rows)
    grad_rounded = grad_values.astype(jnp.bfloat16)
    flat_zero = grad_rounded[:, :7].reshape(edge_total, -1)
    zero_grad = contract(scaled[:, :7].reshape(edge_total, -1), flat_zero)
    grad_scaled_zero = contract_last(flat_zero, weight_zero).reshape(edge_total, 7, -1)
    one_grad, grad_one_plus, grad_one_minus = pair_backward(scaled[:, 7:13], scaled[:, 13:19], grad_rounded[:, 7:13], grad_rounded[:, 13:19], weight_one)
    two_grad, grad_two_plus, grad_two_minus = pair_backward(scaled[:, 19:24], scaled[:, 24:29], grad_rounded[:, 19:24], grad_rounded[:, 24:29], weight_two)
    grad_scaled = jnp.concatenate([grad_scaled_zero, grad_one_plus, grad_one_minus, grad_two_plus, grad_two_minus], axis=1)
    grad_scale = grad_scaled * source_rows.astype(jnp.float32)
    grad_groups = jnp.einsum('eic,ig->egc', grad_scale, jnp.asarray(group_table), precision=lax.Precision.HIGHEST).astype(jnp.bfloat16)
    radial_grad = contract(edge_rows, grad_groups.reshape(edge_total, -1))
    node_grad = None
    if with_source:
        node_total = group_rows.shape[0]
        node_grad = jax.ops.segment_sum(grad_scaled * coef_scale, source_ids, num_segments=node_total)
        query_back = contract_last(grad_query_rows, query_weight)
        node_grad = node_grad.at[:, 0].add(jax.ops.segment_sum(query_back, target_ids, num_segments=node_total))
    return ((zero_grad, one_grad, two_grad, radial_grad, query_grad), node_grad)

def node_update(aggregated, out_weight):
    expand = out_weight[degree_of_coef]
    return jnp.einsum('nid,idc->nic', aggregated.astype(jnp.float32), expand.astype(jnp.float32))

def out_partial(aggregated, grad_rows):
    per_coef = jnp.einsum('nid,nic->idc', aggregated.astype(jnp.float32), grad_rows.astype(jnp.float32))
    return jnp.einsum('idc,il->ldc', per_coef, jnp.asarray(degree_table), precision=lax.Precision.HIGHEST)

def reference(node_features, edge_embed, sources, targets, edge_counts, w_zero, w_one, w_two, radial, query, w_out, cotangent):
    shards = N_GRAPH
    forward_all = jax.vmap(edge_forward, in_axes=(None, 0, 0, 0, 0, None, None, None, None, None))

    def one_graph(totals, graph_items):
        features, embeds, source_ids, target_ids, counts, cot_rows = graph_items
        node_total = features.shape[0]
        embeds = embeds.reshape(shards, EDGE_DEV, -1)
        source_ids = source_ids.reshape(shards, EDGE_DEV)
        target_ids = target_ids.reshape(shards, EDGE_DEV)
        live_mask = (jnp.arange(EDGE_DEV)[None, :] < counts[:, None]).astype(jnp.float32)
        state = features.astype(jnp.float32)
        stored = []
        for layer_index in range(LAYERS):
            norm_scale = lax.rsqrt(lax.optimization_barrier(jnp.mean(state * state, axis=(1, 2))) + norm_eps)
            normed = (state * norm_scale[:, None, None])[:, :29].astype(jnp.bfloat16)
            messages, kept_arrays = forward_all(normed, embeds, source_ids, target_ids, live_mask, w_zero[layer_index], w_one[layer_index], w_two[layer_index], radial[layer_index], query[layer_index])
            summed = jax.ops.segment_sum(messages.reshape(-1, 29, messages.shape[-1]).astype(jnp.float32), target_ids.reshape(-1), num_segments=node_total)
            aggregated = summed.astype(jnp.bfloat16)
            stored.append((state, norm_scale, normed, aggregated, kept_arrays))
            state = jnp.concatenate([state[:, :29] + node_update(aggregated, w_out[layer_index]), state[:, 29:]], axis=1)
        result = state.astype(jnp.bfloat16)
        grad_state = cot_rows.astype(jnp.float32)
        layer_grads = []
        for layer_index in reversed(range(LAYERS)):
            state_in, norm_scale, normed, aggregated, kept_arrays = stored[layer_index]
            grad_rows = grad_state[:, :29].astype(jnp.bfloat16)
            out_part = jax.vmap(out_partial)(aggregated.reshape(shards, NODE_DEV, 29, -1), grad_rows.reshape(shards, NODE_DEV, 29, -1))
            expand = w_out[layer_index][degree_of_coef]
            grad_agg = jnp.einsum('nic,idc->nid', grad_rows.astype(jnp.float32), expand.astype(jnp.float32)).astype(jnp.bfloat16)
            grad_messages = jnp.take(grad_agg, target_ids, axis=0).astype(jnp.float32)
            backward_all = jax.vmap(functools.partial(edge_backward, with_source=layer_index > 0), in_axes=(0, 0, 0, None, 0, 0, 0, None, None, None, None))
            edge_part, node_grad = backward_all(grad_messages, kept_arrays, embeds, normed, source_ids, target_ids, live_mask, w_zero[layer_index], w_one[layer_index], w_two[layer_index], query[layer_index])
            if layer_index > 0:
                node_sum = node_grad.sum(axis=0)
                full_grad = jnp.concatenate([node_sum, jnp.zeros((node_total, state_in.shape[1] - 29, state_in.shape[2]), jnp.float32)], axis=1)
                inner = lax.optimization_barrier(jnp.sum(full_grad * state_in, axis=(1, 2)))
                entries = state_in.shape[1] * state_in.shape[2]
                grad_state = grad_state + norm_scale[:, None, None] * full_grad - state_in * (norm_scale ** 3 * inner / entries)[:, None, None]
            layer_grads.insert(0, tuple((rounded(piece).sum(axis=0) for piece in edge_part + (out_part,))))
        stacked = tuple((jnp.stack([layer_grads[layer_index][position] for layer_index in range(LAYERS)]) for position in range(6)))
        return (tuple((total + piece for total, piece in zip(totals, stacked))), result)
    initial = (jnp.zeros(w_zero.shape, jnp.float32), jnp.zeros(w_one.shape, jnp.float32), jnp.zeros(w_two.shape, jnp.float32), jnp.zeros(radial.shape, jnp.float32), jnp.zeros(query.shape, jnp.float32), jnp.zeros(w_out.shape, jnp.float32))
    totals, outputs = lax.scan(one_graph, initial, (node_features, edge_embed, sources, targets, edge_counts, cotangent))
    return (outputs, totals[0], totals[1], totals[2], totals[3], totals[4], totals[5])
```

```python
import functools

import jax
import jax.numpy as jnp
import numpy as np
from jax import lax
from jax.experimental import pallas as pl
from jax.experimental.pallas import tpu as pltpu
from jax.sharding import PartitionSpec as P

F32 = jnp.float32
BF16 = jnp.bfloat16
LOW = 29
CH = 128
NODES = 128
EDGES = 512
ENTRIES = 49 * 128
NORM_EPS = 1e-6
HEAD_SCALE = 8 ** -0.5
LIMIT = 56 * 1024 * 1024

SEGMENTS = (
    [(0, 2, 0), (2, 2, 2), (4, 2, 4), (6, 1, 6)]
    + [(7, 2, 7), (9, 2, 9), (11, 2, 11)]
    + [(13, 2, 7), (15, 2, 9), (17, 2, 11)]
    + [(19, 2, 13), (21, 2, 15), (23, 1, 17)]
    + [(24, 2, 13), (26, 2, 15), (28, 1, 17)]
)
PAIRS = [(0, 1), (2, 3), (4, 5), (6, None), (1, 2), (3, 4), (5, 6)]
PAIR_OF = [0, 1, 2, 3, 4, 5, 6, 4, 5, 6, 1, 2, 3, 1, 2, 3]

HEAD_FIRST = np.zeros((256, 128), np.float32)
HEAD_BOTH = np.zeros((256, 128), np.float32)
for c_row in range(256):
    for c_col in range(128):
        same = (c_row % 64) // 8 == (c_col % 64) // 8
        HEAD_BOTH[c_row, c_col] = same
        HEAD_FIRST[c_row, c_col] = same and (c_row % 128) < 64


def dot(a, b):
    return lax.dot_general(a, b, (((1,), (0,)), ((), ())), preferred_element_type=F32)


def dot_nt(a, b):
    return lax.dot_general(a, b, (((1,), (1,)), ((), ())), preferred_element_type=F32)


def dot_tn(a, b):
    return lax.dot_general(a, b, (((0,), (0,)), ((), ())), preferred_element_type=F32)


def split_hi_lo(a):
    hi = a.astype(BF16)
    return hi, (a - hi.astype(F32)).astype(BF16)


def swap16(a):
    rows = []
    for b in range(a.shape[0] // 16):
        rows.append(a[16 * (b ^ 1) : 16 * (b ^ 1) + 16])
    return jnp.concatenate(rows, axis=0)


def forward_edges(h_ref, s_ref, t_ref, tt_ref, ee_ref, w0_ref, w1_ref, w2_ref, rad_ref, q_ref, hf_ref,
                  u_ref, hs_ref, r_ref, v_ref, gate_ref, tq_ref, agg_store):
    s_mat = s_ref[...]
    ee = ee_ref[...]
    r_vals = {}
    for c0, n, g0 in SEGMENTS:
        w = 128 * n
        if g0 not in r_vals:
            r_vals[g0] = dot(ee, rad_ref[:, 128 * g0 : 128 * g0 + w])
            if r_ref is not None:
                r_ref[:, 128 * g0 : 128 * g0 + w] = r_vals[g0].astype(BF16)
        hs = dot(s_mat, h_ref[:, 128 * c0 : 128 * c0 + w])
        hs_ref[:, 128 * c0 : 128 * c0 + w] = hs.astype(BF16)
        u_ref[:, 128 * c0 : 128 * c0 + w] = (hs * r_vals[g0]).astype(BF16)
    v0 = dot(u_ref[:, 0:896], w0_ref[...])
    v_ref[:, 0:512] = v0.astype(BF16)
    q_hi, q_lo = split_hi_lo(dot(h_ref[:, 0:128], q_ref[...]))
    t_mat = t_ref[...]
    tq = dot(t_mat, jnp.concatenate([q_hi, q_lo], axis=1))
    tq = tq[:, :128] + tq[:, 128:]
    tq_ref[...] = tq
    p_hi, p_lo = split_hi_lo(v0[:, :128] * tq)
    logits = dot(jnp.concatenate([p_hi, p_lo], axis=1), hf_ref[...]) * HEAD_SCALE
    gate = jax.nn.sigmoid(logits)
    gate_ref[...] = gate
    tt = tt_ref[...]

    def send(values, col):
        n = values.shape[1] // 128
        msg = jnp.concatenate(
            [(values[:, 128 * b : 128 * b + 128] * gate).astype(BF16) for b in range(n)], axis=1
        )
        agg_store(col, dot(tt, msg))

    send(v0[:, 0:256], 0)
    send(v0[:, 256:512], 256)
    v1 = dot(u_ref[:, 896:2432], w1_ref[...])
    v_ref[:, 512:1280] = v1.astype(BF16)
    for b in range(3):
        send(v1[:, 256 * b : 256 * b + 256], 512 + 256 * b)
    v2 = dot(u_ref[:, 2432:3712], w2_ref[...])
    v_ref[:, 1280:2048] = v2.astype(BF16)
    for b in range(3):
        send(v2[:, 256 * b : 256 * b + 256], 1280 + 256 * b)


def select_rows(u_ref, sel0_ref, sel1_ref, sel2_ref, us_ref):
    us_ref[0] = dot(u_ref[:, 0:896], sel0_ref[...]).astype(BF16)
    us_ref[1] = dot(u_ref[:, 896:1664], sel1_ref[...]).astype(BF16)
    us_ref[2] = dot(u_ref[:, 1664:2432], sel1_ref[...]).astype(BF16)
    us_ref[3] = dot(u_ref[:, 2432:3072], sel2_ref[...]).astype(BF16)
    us_ref[4] = dot(u_ref[:, 3072:3712], sel2_ref[...]).astype(BF16)


def backward_edges(core, dagg_ref, dy_ref, agg_ref, h0, t_ref, tt_ref, ee_ref, w0_ref, w1_ref, w2_ref,
                   hb_ref, selq_ref, selr_ref, selp_ref, hs_ref, r_ref, v_ref, gate, tq, us_ref,
                   dv_ref, dr_ref, w_ref, gm_ref, gs_ref):
    t_mat = t_ref[...]
    acc = jnp.zeros((EDGES, 128), F32)
    first = None
    for p in range(8):
        dm = dot(t_mat, dagg_ref[:, 256 * p : 256 * p + 256])
        for b in range(2):
            col = 256 * p + 128 * b
            part = dm[:, 128 * b : 128 * b + 128]
            acc = acc + part * v_ref[:, col : col + 128].astype(F32)
            scaled = part * gate
            if col == 0:
                first = scaled
            else:
                dv_ref[:, col : col + 128] = scaled.astype(BF16)
    a_hi, a_lo = split_hi_lo(acc)
    dalpha = dot(jnp.concatenate([a_hi, a_lo], axis=1), hb_ref[...])
    per = dalpha * gate * (1.0 - gate) * HEAD_SCALE
    dv_ref[:, 0:128] = (first + per * tq).astype(BF16)
    lane = lax.broadcasted_iota(jnp.int32, (EDGES, 128), 1)
    dq = jnp.where(lane < 64, per * v_ref[:, 0:128].astype(F32), 0.0).astype(BF16)
    dqn = dot(tt_ref[...], dq)

    def grads_of(col, width, weight_ref, row):
        return dot_nt(dv_ref[:, col : col + width], weight_ref[row, :])

    plans = (
        (SEGMENTS[0:4], None, 0, 512, w0_ref, 0),
        (SEGMENTS[4:7], SEGMENTS[7:10], 512, 768, w1_ref, 768),
        (SEGMENTS[10:13], SEGMENTS[13:16], 1280, 768, w2_ref, 640),
    )
    for plus, minus, col, width, weight_ref, half in plans:
        base = plus[0][0]
        for k, (c0, n, g0) in enumerate(plus):
            w = 128 * n
            at = 128 * (c0 - base)
            du = grads_of(col, width, weight_ref, pl.ds(at, w))
            dr = du * hs_ref[:, 128 * c0 : 128 * c0 + w].astype(F32)
            if w_ref is not None:
                rg = r_ref[:, 128 * g0 : 128 * g0 + w].astype(F32)
                w_ref[:, 128 * c0 : 128 * c0 + w] = (du * rg).astype(BF16)
            if minus is not None:
                m0 = minus[k][0]
                dum = grads_of(col, width, weight_ref, pl.ds(half + at, w))
                dr = dr + dum * hs_ref[:, 128 * m0 : 128 * m0 + w].astype(F32)
                if w_ref is not None:
                    w_ref[:, 128 * m0 : 128 * m0 + w] = (dum * rg).astype(BF16)
            dr_ref[:, 128 * g0 : 128 * g0 + w] = dr.astype(BF16)

    def put(row, val):
        n = val.shape[0]
        lo, hi = val[:, :128], val[:, 128:]
        gm_ref[row : row + n, :] = jnp.where(core == 0, lo, hi)
        gs_ref[row : row + n, :] = jnp.where(core == 0, hi, lo).astype(BF16)

    sums = [None] * 7
    for k, (c0, n, _) in enumerate(SEGMENTS):
        degs = PAIRS[PAIR_OF[k]]
        sel = dot(dy_ref[:, 128 * c0 : 128 * c0 + 128 * n], selp_ref[0 : 128 * n, :]).astype(BF16)
        prod = dot_tn(agg_ref[:, 128 * k : 128 * k + 128], sel)
        for m in range(n):
            piece = prod[64 * m : 64 * m + 64, 256 * m : 256 * m + 256]
            d = degs[m]
            sums[d] = piece if sums[d] is None else sums[d] + piece
    extra = sums
    hsel = dot(h0, selq_ref[...]).astype(BF16)
    extra.append(dot_tn(dqn.astype(BF16), hsel)[0:64])
    dv0t = dv_ref[:, 0:512].T
    put(0, dot(dv0t, us_ref[0]) + jnp.concatenate(extra, axis=0))
    up, um = us_ref[1], us_ref[2]
    dpt = dv_ref[:, 512:896].T
    dmt = dv_ref[:, 896:1280].T
    put(512, dot(dpt, up) + dot(dmt, um))
    put(896, dot(dmt, up) - dot(dpt, um))
    up, um = us_ref[3], us_ref[4]
    dpt = dv_ref[:, 1280:1664].T
    dmt = dv_ref[:, 1664:2048].T
    put(1280, dot(dpt, up) + dot(dmt, um))
    put(1664, dot(dmt, up) - dot(dpt, um))
    ees = dot_nt(selr_ref[...], ee_ref[...]).astype(BF16)
    for p in range(9):
        pr = dot(ees, dr_ref[:, 256 * p : 256 * p + 256])
        mine = jnp.where(core == 0, pr[0:16], pr[16:32])
        theirs = jnp.where(core == 0, pr[16:32], pr[0:16]).astype(BF16)
        for b in range(2):
            row = 2048 + 16 * (2 * p + b)
            gm_ref[row : row + 16, :] = mine[:, 128 * b : 128 * b + 128]
            gs_ref[row : row + 16, :] = theirs[:, 128 * b : 128 * b + 128]
    return dqn


def node_block(bufs, i):
    return jnp.concatenate([b[i] for b in bufs], axis=0)


def kernel_first(pos_ref, b0, b1, b2, b3, b4, b5, b6, b7, w0_ref, w1_ref, w2_ref, rad_ref, q_ref, hf_ref,
                 sel0_ref, sel1_ref, sel2_ref,
                 agg_ref, s_ref, t_ref, tt_ref, st_ref, ee_ref, v_ref, gate_ref, tq_ref, hs_ref, us_ref, h0_ref,
                 h_ref, u_ref):
    bufs = [b0, b1, b2, b3, b4, b5, b6, b7]
    mask = 16 * pos_ref[0]
    iota = lax.broadcasted_iota(jnp.int32, (NODES, 128), 0)
    for k in range(4):
        buf = bufs[2 * k]
        ids = buf[38].astype(F32)
        src = ids[0:1].astype(jnp.int32) ^ mask
        tgt = ids[1:2].astype(jnp.int32) ^ mask
        s_hot = jnp.where(iota == src, 1.0, 0.0)
        t_hot = jnp.where(iota == tgt, 1.0, 0.0) * ids[2:3]
        st_ref[:, 128 * k : 128 * k + 128] = s_hot.astype(BF16)
        tt_ref[:, 128 * k : 128 * k + 128] = t_hot.astype(BF16)
        s_ref[128 * k : 128 * k + 128, :] = s_hot.T.astype(BF16)
        t_ref[128 * k : 128 * k + 128, :] = t_hot.T.astype(BF16)
        for m in range(8):
            ee_ref[128 * k + 16 * m : 128 * k + 16 * m + 16, :] = buf[30 + m]
    total = jnp.zeros((NODES, CH), F32)
    for i in range(LOW):
        x = node_block(bufs, i).astype(F32)
        total = total + x * x
    total = total + node_block(bufs, LOW).astype(F32)
    scale = lax.rsqrt(jnp.sum(total, axis=1, keepdims=True) * (1.0 / ENTRIES) + NORM_EPS)
    for i in range(LOW):
        h_ref[:, 128 * i : 128 * i + 128] = (node_block(bufs, i).astype(F32) * scale).astype(BF16)
    h0_ref[...] = h_ref[:, 0:128]

    def agg_store(col, val):
        agg_ref[:, col : col + 256] = val.astype(BF16)

    forward_edges(h_ref, s_ref, t_ref, tt_ref, ee_ref, w0_ref, w1_ref, w2_ref, rad_ref, q_ref, hf_ref,
                  u_ref, hs_ref, None, v_ref, gate_ref, tq_ref, agg_store)
    select_rows(u_ref, sel0_ref, sel1_ref, sel2_ref, us_ref)


def kernel_second(pos_ref, b0, b1, b2, b3, b4, b5, b6, b7, c0_, c1_, c2_, c3_, c4_, c5_, c6_, c7_,
                  agg0_ref, agg0p_ref, s_ref, t_ref, tt_ref, st_ref, ee_ref,
                  wd0_ref, wd1_ref, w0_ref, w1_ref, w2_ref, rad_ref, q_ref, hf_ref, hb_ref,
                  sel0_ref, sel1_ref, sel2_ref, selq_ref, selr_ref, selp_ref,
                  x1_ref, s1_ref, own_ref, snd_ref, dh_ref, gm_ref, gs_ref,
                  h_ref, u_ref, hs_ref, r_ref, v_ref, gate_ref, tq_ref, us_ref, agg1_ref, dy_ref, dagg_ref,
                  dv_ref, dr_ref, w_ref):
    core = pos_ref[0] & 1
    bufs = [b0, b1, b2, b3, b4, b5, b6, b7]
    cots = [c0_, c1_, c2_, c3_, c4_, c5_, c6_, c7_]
    total = node_block(bufs, LOW).astype(F32)
    for k, (c0, n, _) in enumerate(SEGMENTS):
        agg = agg0_ref[:, 128 * k : 128 * k + 128].astype(F32)
        agg = agg + swap16(agg0p_ref[:, 128 * k : 128 * k + 128]).astype(F32)
        out = dot(agg.astype(BF16), wd0_ref[PAIR_OF[k]])
        for m in range(n):
            x = node_block(bufs, c0 + m).astype(F32) + out[:, 128 * m : 128 * m + 128]
            x1_ref[:, 128 * (c0 + m) : 128 * (c0 + m) + 128] = x
            total = total + x * x
    scale = lax.rsqrt(jnp.sum(total, axis=1, keepdims=True) * (1.0 / ENTRIES) + NORM_EPS)
    s1_ref[...] = jnp.broadcast_to(scale, (NODES, 128))
    for i in range(LOW):
        h_ref[:, 128 * i : 128 * i + 128] = (x1_ref[:, 128 * i : 128 * i + 128] * scale).astype(BF16)

    def agg_store(col, val):
        agg1_ref[:, col : col + 256] = val.astype(BF16)
        own_ref[:, col : col + 256] = val[0:16]
        snd_ref[:, col : col + 256] = val[16:32].astype(BF16)

    forward_edges(h_ref, s_ref, t_ref, tt_ref, ee_ref, w0_ref, w1_ref, w2_ref, rad_ref, q_ref, hf_ref,
                  u_ref, hs_ref, r_ref, v_ref, gate_ref, tq_ref, agg_store)
    select_rows(u_ref, sel0_ref, sel1_ref, sel2_ref, us_ref)
    for i in range(LOW):
        dy_ref[:, 128 * i : 128 * i + 128] = node_block(cots, i)
    for k, (c0, n, _) in enumerate(SEGMENTS):
        w = 128 * n
        dagg_ref[:, 128 * k : 128 * k + 128] = dot_nt(
            dy_ref[:, 128 * c0 : 128 * c0 + w], wd1_ref[PAIR_OF[k], :, 0:w]
        ).astype(BF16)
    dqn = backward_edges(core, dagg_ref, dy_ref, agg1_ref, h_ref[:, 0:128], t_ref, tt_ref, ee_ref,
                         w0_ref, w1_ref, w2_ref, hb_ref, selq_ref, selr_ref, selp_ref, hs_ref, r_ref, v_ref,
                         gate_ref[...], tq_ref[...], us_ref, dv_ref, dr_ref, w_ref, gm_ref, gs_ref)
    st = st_ref[...]
    d_hi, d_lo = split_hi_lo(dqn)
    back = dot_nt(jnp.concatenate([d_hi, d_lo], axis=1), jnp.concatenate([q_ref[...], q_ref[...]], axis=1))
    for c0, n, _ in SEGMENTS:
        w = 128 * n
        val = dot(st, w_ref[:, 128 * c0 : 128 * c0 + w])
        if c0 == 0:
            val = val + jnp.concatenate([back, jnp.zeros((NODES, 128), F32)], axis=1)
        dh_ref[:, 128 * c0 : 128 * c0 + w] = val.astype(BF16)


def kernel_third(pos_ref, c0_, c1_, c2_, c3_, c4_, c5_, c6_, c7_, x1_ref, s1_ref, dh_ref, dhp_ref,
                 agg0_ref, t_ref, tt_ref, ee_ref, v_ref, gate_ref, tq_ref, hs_ref, us_ref, h0_ref,
                 wd0_ref, wd1_ref, w0_ref, w1_ref, w2_ref, hb_ref, selq_ref, selr_ref, selp_ref,
                 own_ref, rcv_ref,
                 gm_ref, gs_ref, x2_ref,
                 dy_ref, dagg_ref, dv_ref, dr_ref, full_ref):
    core = pos_ref[0] & 1
    cots = [c0_, c1_, c2_, c3_, c4_, c5_, c6_, c7_]
    inner = jnp.zeros((NODES, 128), F32)
    for i in range(LOW):
        cols = pl.ds(128 * i, 128)
        dh = dh_ref[:, cols].astype(F32) + swap16(dhp_ref[:, cols]).astype(F32)
        full_ref[:, cols] = dh
        inner = inner + dh * x1_ref[:, cols]
    s1 = s1_ref[...]
    coef = jnp.sum(inner, axis=1, keepdims=True) * (1.0 / ENTRIES) * (s1 * s1 * s1)
    for i in range(LOW):
        cols = pl.ds(128 * i, 128)
        dx = node_block(cots, i).astype(F32) + s1 * full_ref[:, cols] - x1_ref[:, cols] * coef
        dy_ref[:, cols] = dx.astype(BF16)
    for k, (c0, n, _) in enumerate(SEGMENTS):
        w = 128 * n
        dagg_ref[:, 128 * k : 128 * k + 128] = dot_nt(
            dy_ref[:, 128 * c0 : 128 * c0 + w], wd0_ref[PAIR_OF[k], :, 0:w]
        ).astype(BF16)
    backward_edges(core, dagg_ref, dy_ref, agg0_ref, h0_ref[...], t_ref, tt_ref, ee_ref,
                   w0_ref, w1_ref, w2_ref, hb_ref, selq_ref, selr_ref, selp_ref, hs_ref, None, v_ref,
                   gate_ref[...], tq_ref[...], us_ref, dv_ref, dr_ref, None, gm_ref, gs_ref)
    for k, (c0, n, _) in enumerate(SEGMENTS):
        w = 128 * n
        agg = own_ref[:, 128 * k : 128 * k + 128] + rcv_ref[:, 128 * k : 128 * k + 128].astype(F32)
        out = dot(agg.astype(BF16), wd1_ref[PAIR_OF[k], :, 0:w])
        x2_ref[:, 128 * c0 : 128 * c0 + w] = (x1_ref[0:16, 128 * c0 : 128 * c0 + w] + out).astype(BF16)


def kernel_pack(ma, pa, mb, pb, out_ref, g_ref, chunk_ref):
    lane14 = lax.broadcasted_iota(jnp.int32, (16, 128), 1)
    for layer, (mine, other) in enumerate(((ma, pa), (mb, pb))):
        g_ref[...] = mine[...] + other[...].astype(F32)
        base = 64 * layer
        for d in range(32):
            chunk_ref[d, base : base + 14, :] = g_ref[14 * d : 14 * d + 14, :]
            chunk_ref[d, base + 14 : base + 38, :] = g_ref[512 + 24 * d : 536 + 24 * d, :]
            row = 1280 + 20 * d + (64 if d >= 16 else 0)
            chunk_ref[d, base + 38 : base + 58, :] = g_ref[row : row + 20, :]
            chunk_ref[d, base + 58 : base + 64, :] = jnp.zeros((6, 128), F32)
            for q in range(7):
                chunk_ref[d, base + 2 * q : base + 2 * q + 2, 112:128] = g_ref[
                    64 * q + 2 * d : 64 * q + 2 * d + 2, 112:128
                ]
            chunk_ref[d, base + 14 : base + 16, 112:128] = g_ref[448 + 2 * d : 450 + 2 * d, 112:128]
            for start, width, at, to in ((72 * d, 48, 80, 38), (72 * d + 48, 24, 96, 16)):
                blk, off = start // 128, start % 128
                shift = (at - off) % 128
                left = g_ref[2048 + 16 * blk : 2064 + 16 * blk, :]
                win = pltpu.roll(left, shift, 1) if shift else left
                if off + width > 128:
                    right = g_ref[2064 + 16 * blk : 2080 + 16 * blk, :]
                    right = pltpu.roll(right, shift, 1) if shift else right
                    win = jnp.where(lane14 < at + 128 - off, win, right)
                chunk_ref[d, base + to : base + to + 16, at : at + width] = win[:, at : at + width]
    out_ref[...] = chunk_ref[...].astype(BF16)


def kernel_finish(in_ref, zero_ref, one_ref, two_ref, rad_ref, q_ref, out_ref):
    acc = in_ref[0].astype(F32)
    for d in range(1, 32):
        acc = acc + in_ref[d].astype(F32)
    lane = lax.broadcasted_iota(jnp.int32, (16, 128), 1)
    for layer in range(2):
        part = acc[64 * layer : 64 * layer + 64]
        flip = part.T
        zero_ref[layer] = flip[0:112, 0:14]
        one_ref[layer] = flip[0:96, 14:38]
        two_ref[layer] = flip[0:80, 38:58]
        q_ref[layer] = flip[112:128, 14:16]
        low = pltpu.roll(part[38:54], 48, 1)
        high = pltpu.roll(part[16:32], 80, 1)
        rad_ref[layer] = jnp.where(lane < 48, low, high)[:, 0:72]
        tail = pltpu.roll(part[0:16], 16, 1)
        for q in range(7):
            out_ref[layer, q] = tail[2 * q : 2 * q + 2, 0:16]


def call(body, outs, scratch, n_in):
    return pl.pallas_call(
        body,
        in_specs=[pl.BlockSpec(memory_space=pltpu.SMEM)] + [pl.BlockSpec(memory_space=pltpu.VMEM)] * (n_in - 1),
        out_specs=[pl.BlockSpec(memory_space=pltpu.VMEM)] * len(outs),
        out_shape=[jax.ShapeDtypeStruct(s, t) for s, t in outs],
        scratch_shapes=[pltpu.VMEM(s, t) for s, t in scratch],
        compiler_params=pltpu.CompilerParams(vmem_limit_bytes=LIMIT),
    )


def plain_call(body, outs, scratch):
    return pl.pallas_call(
        body,
        out_shape=[jax.ShapeDtypeStruct(s, t) for s, t in outs],
        scratch_shapes=[pltpu.VMEM(s, t) for s, t in scratch],
        compiler_params=pltpu.CompilerParams(vmem_limit_bytes=LIMIT),
    )


def swap(x, bits):
    return lax.ppermute(x, "graph", [(i, i ^ bits) for i in range(8)])


def exact_pieces(t):
    hi = lax.reduce_precision(t, 8, 7)
    mid = lax.reduce_precision(t - hi, 8, 7)
    return [hi, mid, t - hi - mid]


def shards(node_features, edge_embed, sources, targets, edge_counts, w_zero, w_one, w_two, radial, query, w_out, cotangent):
    pos = lax.axis_index("graph").astype(jnp.int32)
    z_lo = pos // 2
    pos_arr = pos[None]
    x0 = node_features[0]
    low = jnp.transpose(x0[:, :LOW], (1, 0, 2))
    tail = jnp.sum(jnp.square(x0[:, LOW:].astype(F32)), axis=(1, 2))
    tail_block = jnp.pad(jnp.stack(exact_pieces(tail), axis=1), ((0, 0), (0, 125))).astype(BF16)[None]
    live = (jnp.arange(128) < edge_counts[0, 0]).astype(BF16)
    ids = jnp.pad(
        jnp.stack([sources[0].astype(BF16), targets[0].astype(BF16), live]), ((0, 13), (0, 0))
    )[None]
    own = jnp.concatenate([low, tail_block, edge_embed[0].reshape(8, 16, 128), ids], axis=0)
    far = [swap(own, k) for k in (2, 4, 6)]
    pair = [swap(b, 1) for b in [own] + far]
    bufs = [own, pair[0], far[0], pair[1], far[1], pair[2], far[2], pair[3]]
    cot = jnp.transpose(cotangent[0][:, :LOW], (1, 0, 2))
    cot, _ = lax.optimization_barrier((cot, far[2][0, 0, 0]))
    cfar = [swap(cot, k) for k in (2, 4, 6)]
    cpair = [swap(b, 1) for b in [cot] + cfar]
    cots = [cot, cpair[0], cfar[0], cpair[1], cfar[1], cpair[2], cfar[2], cpair[3]]

    w0p = jnp.pad(w_zero, ((0, 0), (0, 0), (0, 64)))
    a1, b1 = w_one[:, :, :384], w_one[:, :, 384:]
    w1c = jnp.concatenate([jnp.concatenate([a1, b1], 2), jnp.concatenate([-b1, a1], 2)], 1)
    widen = ((0, 0), (0, 0), (0, 64))
    a2, b2 = jnp.pad(w_two[:, :, :320], widen), jnp.pad(w_two[:, :, 320:], widen)
    w2c = jnp.concatenate([jnp.concatenate([a2, b2], 2), jnp.concatenate([-b2, a2], 2)], 1)
    qp = jnp.pad(query, widen)
    blank = jnp.zeros((2, 64, 128), BF16)
    blocks = []
    for a, b in PAIRS:
        top = jnp.concatenate([w_out[:, a], blank], 2)
        bottom = jnp.concatenate([blank, blank if b is None else w_out[:, b]], 2)
        blocks.append(jnp.concatenate([top, bottom], 1))
    wd = jnp.stack(blocks, 1)

    def select(rows, width, first_lane, scale):
        k = lax.broadcasted_iota(jnp.int32, (rows, 256), 0)
        l = lax.broadcasted_iota(jnp.int32, (rows, 256), 1)
        m = l % 128 - first_lane
        hit = (m >= 0) & (m < width) & (k == scale * z_lo + width * (l // 128) + m)
        return hit.astype(BF16)

    sel0 = select(896, 112, 0, 224)
    sel1 = select(768, 96, 0, 192)
    sel2 = select(640, 80, 0, 160)
    selq = select(128, 16, 112, 32)
    zq = jnp.zeros((128, 256), BF16)
    selp = jnp.concatenate([jnp.concatenate([selq, zq], 1), jnp.concatenate([zq, selq], 1)], 0)
    rows = lax.broadcasted_iota(jnp.int32, (32, 128), 0)
    cols = lax.broadcasted_iota(jnp.int32, (32, 128), 1)
    selr = (cols == 32 * z_lo + rows).astype(BF16)
    hf = jnp.asarray(HEAD_FIRST, BF16)
    hb = jnp.asarray(HEAD_BOTH, BF16)

    big = (EDGES, LOW * CH)
    agg0, s_mat, t_mat, tt, st, ee, v0, gate0, tq0, hs0, us0, h00 = call(
        kernel_first,
        [((NODES, 2048), BF16), ((EDGES, 128), BF16), ((EDGES, 128), BF16), ((128, EDGES), BF16),
         ((128, EDGES), BF16), ((EDGES, 128), BF16), ((EDGES, 2048), BF16), ((EDGES, 128), F32),
         ((EDGES, 128), F32), (big, BF16), ((5, EDGES, 256), BF16), ((NODES, 128), BF16)],
        [((NODES, LOW * CH), BF16), (big, BF16)],
        18,
    )(pos_arr, *bufs, w0p[0], w1c[0], w2c[0], radial[0], qp[0], hf, sel0, sel1, sel2)
    agg0p = swap(agg0, 1)
    grad_rows = 2048 + 288
    x1, s1, own1, snd1, dh, gm1, gs1 = call(
        kernel_second,
        [((NODES, LOW * CH), F32), ((NODES, 128), F32), ((16, 2048), F32), ((16, 2048), BF16),
         ((NODES, LOW * CH), BF16), ((grad_rows, 128), F32), ((grad_rows, 128), BF16)],
        [((NODES, LOW * CH), BF16), (big, BF16), (big, BF16), ((EDGES, 2304), BF16), ((EDGES, 2048), BF16),
         ((EDGES, 128), F32), ((EDGES, 128), F32), ((5, EDGES, 256), BF16), ((NODES, 2048), BF16),
         ((NODES, LOW * CH), BF16), ((NODES, 2048), BF16), ((EDGES, 2048), BF16), ((EDGES, 2304), BF16),
         (big, BF16)],
        39,
    )(pos_arr, *bufs, *cots, agg0, agg0p, s_mat, t_mat, tt, st, ee, wd[0], wd[1], w0p[1], w1c[1], w2c[1],
      radial[1], qp[1], hf, hb, sel0, sel1, sel2, selq, selr, selp)
    dhp = swap(dh, 1)
    rcv1 = swap(snd1, 1)
    gp1 = swap(gs1, 1)
    gm0, gs0, x2 = call(
        kernel_third,
        [((grad_rows, 128), F32), ((grad_rows, 128), BF16), ((16, LOW * CH), BF16)],
        [((NODES, LOW * CH), BF16), ((NODES, 2048), BF16), ((EDGES, 2048), BF16), ((EDGES, 2304), BF16),
         ((NODES, LOW * CH), F32)],
        34,
    )(pos_arr, *cots, x1, s1, dh, dhp, agg0, t_mat, tt, ee, v0, gate0, tq0, hs0, us0, h00,
      wd[0], wd[1], w0p[0], w1c[0], w2c[0], hb, selq, selr, selp, own1, rcv1)
    gp0 = swap(gs0, 1)
    result = jnp.concatenate([x2.reshape(16, LOW, CH), x0[:, LOW:]], axis=1)[None]
    (packed,) = plain_call(
        kernel_pack, [((32, 128, 128), BF16)], [((grad_rows, 128), F32), ((32, 128, 128), F32)]
    )(gm0, gp0, gm1, gp1)
    moved = lax.all_to_all(packed, "dp", split_axis=0, concat_axis=0, tiled=True)
    grads = plain_call(
        kernel_finish,
        [((2, 112, 14), F32), ((2, 96, 24), F32), ((2, 80, 20), F32), ((2, 16, 72), F32),
         ((2, 16, 2), F32), ((2, 7, 2, 16), F32)],
        [],
    )(moved)
    return (result, *grads)


def solution(mesh):
    by_graph = P("dp", "graph")
    in_specs = (
        P("dp", "graph", None, None),
        P("dp", "graph", None),
        by_graph,
        by_graph,
        by_graph,
        P(),
        P(),
        P(),
        P(),
        P(),
        P(),
        P("dp", "graph", None, None),
    )
    out_specs = (
        P("dp", "graph", None, None),
        P(None, "graph", "dp"),
        P(None, "graph", "dp"),
        P(None, "graph", "dp"),
        P(None, "graph", "dp"),
        P(None, "graph", "dp"),
        P(None, None, "dp", "graph"),
    )
    return jax.shard_map(shards, mesh=mesh, in_specs=in_specs, out_specs=out_specs, check_vma=False)
```

```python
import functools

import jax
import jax.numpy as jnp
import numpy as np
from jax import lax
from jax.experimental import pallas as pl
from jax.experimental.pallas import tpu as pltpu
from jax.sharding import PartitionSpec as P

F32 = jnp.float32
BF16 = jnp.bfloat16
LOW = 29
CH = 128
NODES = 128
EDGES = 512
ENTRIES = 49 * 128
NORM_EPS = 1e-6
HEAD_SCALE = 8 ** -0.5
MIB = 1024 * 1024

SEGMENTS = (
    [(0, 2, 0), (2, 2, 2), (4, 2, 4), (6, 1, 6)]
    + [(7, 2, 7), (9, 2, 9), (11, 2, 11)]
    + [(13, 2, 7), (15, 2, 9), (17, 2, 11)]
    + [(19, 2, 13), (21, 2, 15), (23, 1, 17)]
    + [(24, 2, 13), (26, 2, 15), (28, 1, 17)]
)
PAIRS = [(0, 1), (2, 3), (4, 5), (6, None), (1, 2), (3, 4), (5, 6)]
PAIR_OF = [0, 1, 2, 3, 4, 5, 6, 4, 5, 6, 1, 2, 3, 1, 2, 3]

HEAD_FIRST = np.zeros((256, 128), np.float32)
HEAD_BOTH = np.zeros((256, 128), np.float32)
for c_row in range(256):
    for c_col in range(128):
        same = (c_row % 64) // 8 == (c_col % 64) // 8
        HEAD_BOTH[c_row, c_col] = same
        HEAD_FIRST[c_row, c_col] = same and (c_row % 128) < 64


def dot(a, b):
    return lax.dot_general(a, b, (((1,), (0,)), ((), ())), preferred_element_type=F32)


def dot_nt(a, b):
    return lax.dot_general(a, b, (((1,), (1,)), ((), ())), preferred_element_type=F32)


def dot_tn(a, b):
    return lax.dot_general(a, b, (((0,), (0,)), ((), ())), preferred_element_type=F32)


def split_hi_lo(a):
    hi = a.astype(BF16)
    return hi, (a - hi.astype(F32)).astype(BF16)


def swap16(a):
    rows = []
    for b in range(a.shape[0] // 16):
        rows.append(a[16 * (b ^ 1) : 16 * (b ^ 1) + 16])
    return jnp.concatenate(rows, axis=0)


def forward_edges(h_ref, s_ref, t_ref, tt_ref, ee_ref, w0_ref, w1_ref, w2_ref, rad_ref, q_ref, hf_ref,
                  u_ref, hs_ref, r_ref, v_ref, gate_ref, tq_ref, agg_store):
    s_mat = s_ref[...]
    ee = ee_ref[...]
    r_vals = {}
    for c0, n, g0 in SEGMENTS:
        w = 128 * n
        if g0 not in r_vals:
            r_vals[g0] = dot(ee, rad_ref[:, 128 * g0 : 128 * g0 + w])
            if r_ref is not None:
                r_ref[:, 128 * g0 : 128 * g0 + w] = r_vals[g0].astype(BF16)
        hs = dot(s_mat, h_ref[:, 128 * c0 : 128 * c0 + w])
        hs_ref[:, 128 * c0 : 128 * c0 + w] = hs.astype(BF16)
        u_ref[:, 128 * c0 : 128 * c0 + w] = (hs * r_vals[g0]).astype(BF16)
    v0 = dot_nt(u_ref[:, 0:896], w0_ref[...])
    v_ref[:, 0:512] = v0.astype(BF16)
    q_hi, q_lo = split_hi_lo(dot_nt(h_ref[:, 0:128], q_ref[...]))
    t_mat = t_ref[...]
    tq = dot(t_mat, jnp.concatenate([q_hi, q_lo], axis=1))
    tq = tq[:, :128] + tq[:, 128:]
    tq_ref[...] = tq
    p_hi, p_lo = split_hi_lo(v0[:, :128] * tq)
    logits = dot(jnp.concatenate([p_hi, p_lo], axis=1), hf_ref[...]) * HEAD_SCALE
    gate = jax.nn.sigmoid(logits)
    gate_ref[...] = gate
    tt = tt_ref[...]

    def send(values, col):
        n = values.shape[1] // 128
        msg = jnp.concatenate(
            [(values[:, 128 * b : 128 * b + 128] * gate).astype(BF16) for b in range(n)], axis=1
        )
        agg_store(col, dot(tt, msg))

    send(v0[:, 0:256], 0)
    send(v0[:, 256:512], 256)
    v1 = dot(u_ref[:, 896:2432], w1_ref[...])
    v_ref[:, 512:1280] = v1.astype(BF16)
    for b in range(3):
        send(v1[:, 256 * b : 256 * b + 256], 512 + 256 * b)
    v2 = dot(u_ref[:, 2432:3712], w2_ref[...])
    v_ref[:, 1280:2048] = v2.astype(BF16)
    for b in range(3):
        send(v2[:, 256 * b : 256 * b + 256], 1280 + 256 * b)


def select_rows(u_ref, sel0_ref, sel1_ref, sel2_ref, us_ref):
    us_ref[0] = dot(u_ref[:, 0:896], sel0_ref[...]).astype(BF16)
    us_ref[1] = dot(u_ref[:, 896:1664], sel1_ref[...]).astype(BF16)
    us_ref[2] = dot(u_ref[:, 1664:2432], sel1_ref[...]).astype(BF16)
    us_ref[3] = dot(u_ref[:, 2432:3072], sel2_ref[...]).astype(BF16)
    us_ref[4] = dot(u_ref[:, 3072:3712], sel2_ref[...]).astype(BF16)


def backward_edges(core, dagg_ref, dy_ref, agg_ref, h0, t_ref, tt_ref, ee_ref, w0_ref, w1_ref, w2_ref,
                   hb_ref, selq_ref, selr_ref, selp_ref, hs_ref, r_ref, v_ref, gate, tq, us_ref,
                   dv_ref, dr_ref, w_ref, gm_ref, gs_ref):
    t_mat = t_ref[...]
    acc = jnp.zeros((EDGES, 128), F32)
    first = None
    for p in range(8):
        dm = dot(t_mat, dagg_ref[:, 256 * p : 256 * p + 256])
        for b in range(2):
            col = 256 * p + 128 * b
            part = dm[:, 128 * b : 128 * b + 128]
            acc = acc + part * v_ref[:, col : col + 128].astype(F32)
            scaled = part * gate
            if col == 0:
                first = scaled
            else:
                dv_ref[:, col : col + 128] = scaled.astype(BF16)
    a_hi, a_lo = split_hi_lo(acc)
    dalpha = dot(jnp.concatenate([a_hi, a_lo], axis=1), hb_ref[...])
    per = dalpha * gate * (1.0 - gate) * HEAD_SCALE
    dv_ref[:, 0:128] = (first + per * tq).astype(BF16)
    lane = lax.broadcasted_iota(jnp.int32, (EDGES, 128), 1)
    dq = jnp.where(lane < 64, per * v_ref[:, 0:128].astype(F32), 0.0).astype(BF16)
    dqn = dot(tt_ref[...], dq)

    def grads_of(col, width, weight_ref, row):
        if col == 0:
            return dot(dv_ref[:, col : col + width], weight_ref[:, row])
        return dot_nt(dv_ref[:, col : col + width], weight_ref[row, :])

    plans = (
        (SEGMENTS[0:4], None, 0, 512, w0_ref, 0),
        (SEGMENTS[4:7], SEGMENTS[7:10], 512, 768, w1_ref, 768),
        (SEGMENTS[10:13], SEGMENTS[13:16], 1280, 768, w2_ref, 640),
    )
    for plus, minus, col, width, weight_ref, half in plans:
        base = plus[0][0]
        for k, (c0, n, g0) in enumerate(plus):
            w = 128 * n
            at = 128 * (c0 - base)
            du = grads_of(col, width, weight_ref, pl.ds(at, w))
            dr = du * hs_ref[:, 128 * c0 : 128 * c0 + w].astype(F32)
            if w_ref is not None:
                rg = r_ref[:, 128 * g0 : 128 * g0 + w].astype(F32)
                w_ref[:, 128 * c0 : 128 * c0 + w] = (du * rg).astype(BF16)
            if minus is not None:
                m0 = minus[k][0]
                dum = grads_of(col, width, weight_ref, pl.ds(half + at, w))
                dr = dr + dum * hs_ref[:, 128 * m0 : 128 * m0 + w].astype(F32)
                if w_ref is not None:
                    w_ref[:, 128 * m0 : 128 * m0 + w] = (dum * rg).astype(BF16)
            dr_ref[:, 128 * g0 : 128 * g0 + w] = dr.astype(BF16)

    def put(row, val):
        n = val.shape[0]
        lo, hi = val[:, :128], val[:, 128:]
        gm_ref[row : row + n, :] = jnp.where(core == 0, lo, hi)
        gs_ref[row : row + n, :] = jnp.where(core == 0, hi, lo).astype(BF16)

    sums = [None] * 7
    for k, (c0, n, _) in enumerate(SEGMENTS):
        degs = PAIRS[PAIR_OF[k]]
        sel = dot(dy_ref[:, 128 * c0 : 128 * c0 + 128 * n], selp_ref[0 : 128 * n, :]).astype(BF16)
        prod = dot_tn(agg_ref[:, 128 * k : 128 * k + 128], sel)
        for m in range(n):
            piece = prod[64 * m : 64 * m + 64, 256 * m : 256 * m + 256]
            d = degs[m]
            sums[d] = piece if sums[d] is None else sums[d] + piece
    extra = sums
    hsel = dot(h0, selq_ref[...]).astype(BF16)
    extra.append(dot_tn(dqn.astype(BF16), hsel)[0:64])
    dv0t = dv_ref[:, 0:512].T
    put(0, dot(dv0t, us_ref[0]) + jnp.concatenate(extra, axis=0))
    up, um = us_ref[1], us_ref[2]
    dpt = dv_ref[:, 512:896].T
    dmt = dv_ref[:, 896:1280].T
    put(512, dot(dpt, up) + dot(dmt, um))
    put(896, dot(dmt, up) - dot(dpt, um))
    up, um = us_ref[3], us_ref[4]
    dpt = dv_ref[:, 1280:1664].T
    dmt = dv_ref[:, 1664:2048].T
    put(1280, dot(dpt, up) + dot(dmt, um))
    put(1664, dot(dmt, up) - dot(dpt, um))
    ees = dot_nt(selr_ref[...], ee_ref[...]).astype(BF16)
    for p in range(9):
        pr = dot(ees, dr_ref[:, 256 * p : 256 * p + 256])
        mine = jnp.where(core == 0, pr[0:16], pr[16:32])
        theirs = jnp.where(core == 0, pr[16:32], pr[0:16]).astype(BF16)
        for b in range(2):
            row = 2048 + 16 * (2 * p + b)
            gm_ref[row : row + 16, :] = mine[:, 128 * b : 128 * b + 128]
            gs_ref[row : row + 16, :] = theirs[:, 128 * b : 128 * b + 128]
    return dqn


def node_block(bufs, i):
    return jnp.concatenate([b[i] for b in bufs], axis=0)


def kernel_first(pos_ref, b0, b1, b2, b3, b4, b5, b6, b7, w0_ref, w1_ref, w2_ref, rad_ref, q_ref, hf_ref,
                 sel0_ref, sel1_ref, sel2_ref,
                 agg_ref, s_ref, t_ref, tt_ref, st_ref, ee_ref, v_ref, gate_ref, tq_ref, hs_ref, us_ref, h0_ref,
                 h_ref, u_ref):
    bufs = [b0, b1, b2, b3, b4, b5, b6, b7]
    mask = 16 * pos_ref[0]
    iota = lax.broadcasted_iota(jnp.int32, (NODES, 128), 0)
    for k in range(4):
        buf = bufs[2 * k]
        ids = buf[38].astype(F32)
        src = ids[0:1].astype(jnp.int32) ^ mask
        tgt = ids[1:2].astype(jnp.int32) ^ mask
        s_hot = jnp.where(iota == src, 1.0, 0.0)
        t_hot = jnp.where(iota == tgt, 1.0, 0.0) * ids[2:3]
        st_ref[:, 128 * k : 128 * k + 128] = s_hot.astype(BF16)
        tt_ref[:, 128 * k : 128 * k + 128] = t_hot.astype(BF16)
        s_ref[128 * k : 128 * k + 128, :] = s_hot.T.astype(BF16)
        t_ref[128 * k : 128 * k + 128, :] = t_hot.T.astype(BF16)
        for m in range(8):
            ee_ref[128 * k + 16 * m : 128 * k + 16 * m + 16, :] = buf[30 + m]
    total = jnp.zeros((NODES, CH), F32)
    for i in range(LOW):
        x = node_block(bufs, i).astype(F32)
        total = total + x * x
    total = total + node_block(bufs, LOW).astype(F32)
    scale = lax.rsqrt(jnp.sum(total, axis=1, keepdims=True) * (1.0 / ENTRIES) + NORM_EPS)
    for i in range(LOW):
        h_ref[:, 128 * i : 128 * i + 128] = (node_block(bufs, i).astype(F32) * scale).astype(BF16)
    h0_ref[...] = h_ref[:, 0:128]

    def agg_store(col, val):
        agg_ref[:, col : col + 256] = val.astype(BF16)

    forward_edges(h_ref, s_ref, t_ref, tt_ref, ee_ref, w0_ref, w1_ref, w2_ref, rad_ref, q_ref, hf_ref,
                  u_ref, hs_ref, None, v_ref, gate_ref, tq_ref, agg_store)
    select_rows(u_ref, sel0_ref, sel1_ref, sel2_ref, us_ref)


def kernel_second(b0, b1, b2, b3, b4, b5, b6, b7, agg0_ref, agg0p_ref, s_ref, t_ref, tt_ref, ee_ref,
                  wd0_ref, w0_ref, w1_ref, w2_ref, rad_ref, q_ref, hf_ref, sel0_ref, sel1_ref, sel2_ref,
                  x1_ref, s1_ref, own_ref, snd_ref, agg1_ref, h0_ref, hs_ref, r_ref, v_ref, gate_ref, tq_ref, us_ref,
                  h_ref, u_ref):
    bufs = [b0, b1, b2, b3, b4, b5, b6, b7]
    total = node_block(bufs, LOW).astype(F32)
    for k, (c0, n, _) in enumerate(SEGMENTS):
        agg = agg0_ref[:, 128 * k : 128 * k + 128].astype(F32)
        agg = agg + swap16(agg0p_ref[:, 128 * k : 128 * k + 128]).astype(F32)
        out = dot(agg.astype(BF16), wd0_ref[PAIR_OF[k]])
        for m in range(n):
            x = node_block(bufs, c0 + m).astype(F32) + out[:, 128 * m : 128 * m + 128]
            x1_ref[:, 128 * (c0 + m) : 128 * (c0 + m) + 128] = x
            total = total + x * x
    scale = lax.rsqrt(jnp.sum(total, axis=1, keepdims=True) * (1.0 / ENTRIES) + NORM_EPS)
    s1_ref[...] = jnp.broadcast_to(scale, (NODES, 128))
    for i in range(LOW):
        h_ref[:, 128 * i : 128 * i + 128] = (x1_ref[:, 128 * i : 128 * i + 128] * scale).astype(BF16)
    h0_ref[...] = h_ref[:, 0:128]

    def agg_store(col, val):
        agg1_ref[:, col : col + 256] = val.astype(BF16)
        own_ref[:, col : col + 256] = val[0:16]
        snd_ref[:, col : col + 256] = val[16:32].astype(BF16)

    forward_edges(h_ref, s_ref, t_ref, tt_ref, ee_ref, w0_ref, w1_ref, w2_ref, rad_ref, q_ref, hf_ref,
                  u_ref, hs_ref, r_ref, v_ref, gate_ref, tq_ref, agg_store)
    select_rows(u_ref, sel0_ref, sel1_ref, sel2_ref, us_ref)


def kernel_back(pos_ref, c0_, c1_, c2_, c3_, c4_, c5_, c6_, c7_, agg1_ref, h0_ref, t_ref, tt_ref, st_ref, ee_ref,
                v_ref, gate_ref, tq_ref, hs_ref, r_ref, us_ref,
                wd1_ref, w0_ref, w1_ref, w2_ref, q_ref, hb_ref, selq_ref, selr_ref, selp_ref,
                dh_ref, gm_ref, gs_ref,
                dy_ref, dagg_ref, dv_ref, dr_ref, w_ref):
    core = pos_ref[0] & 1
    cots = [c0_, c1_, c2_, c3_, c4_, c5_, c6_, c7_]
    for i in range(LOW):
        dy_ref[:, 128 * i : 128 * i + 128] = node_block(cots, i)
    for k, (c0, n, _) in enumerate(SEGMENTS):
        w = 128 * n
        dagg_ref[:, 128 * k : 128 * k + 128] = dot_nt(
            dy_ref[:, 128 * c0 : 128 * c0 + w], wd1_ref[PAIR_OF[k], :, 0:w]
        ).astype(BF16)
    dqn = backward_edges(core, dagg_ref, dy_ref, agg1_ref, h0_ref[...], t_ref, tt_ref, ee_ref,
                         w0_ref, w1_ref, w2_ref, hb_ref, selq_ref, selr_ref, selp_ref, hs_ref, r_ref, v_ref,
                         gate_ref[...], tq_ref[...], us_ref, dv_ref, dr_ref, w_ref, gm_ref, gs_ref)
    st = st_ref[...]
    d_hi, d_lo = split_hi_lo(dqn)
    back = dot(jnp.concatenate([d_hi, d_lo], axis=1), jnp.concatenate([q_ref[...], q_ref[...]], axis=0))
    for c0, n, _ in SEGMENTS:
        w = 128 * n
        val = dot(st, w_ref[:, 128 * c0 : 128 * c0 + w])
        if c0 == 0:
            val = val + jnp.concatenate([back, jnp.zeros((NODES, 128), F32)], axis=1)
        dh_ref[:, 128 * c0 : 128 * c0 + w] = val.astype(BF16)


def kernel_third(pos_ref, c0_, c1_, c2_, c3_, c4_, c5_, c6_, c7_, x1_ref, s1_ref, dh_ref, dhp_ref,
                 agg0_ref, t_ref, tt_ref, ee_ref, v_ref, gate_ref, tq_ref, hs_ref, us_ref, h0_ref,
                 wd0_ref, wd1_ref, w0_ref, w1_ref, w2_ref, hb_ref, selq_ref, selr_ref, selp_ref,
                 own_ref, rcv_ref, nf_ref,
                 gm_ref, gs_ref, x2_ref,
                 dy_ref, dagg_ref, dv_ref, dr_ref, full_ref):
    core = pos_ref[0] & 1
    cots = [c0_, c1_, c2_, c3_, c4_, c5_, c6_, c7_]
    inner = jnp.zeros((NODES, 128), F32)
    for i in range(LOW):
        cols = pl.ds(128 * i, 128)
        dh = dh_ref[:, cols].astype(F32) + swap16(dhp_ref[:, cols]).astype(F32)
        full_ref[:, cols] = dh
        inner = inner + dh * x1_ref[:, cols]
    s1 = s1_ref[...]
    coef = jnp.sum(inner, axis=1, keepdims=True) * (1.0 / ENTRIES) * (s1 * s1 * s1)
    for i in range(LOW):
        cols = pl.ds(128 * i, 128)
        dx = node_block(cots, i).astype(F32) + s1 * full_ref[:, cols] - x1_ref[:, cols] * coef
        dy_ref[:, cols] = dx.astype(BF16)
    for k, (c0, n, _) in enumerate(SEGMENTS):
        w = 128 * n
        dagg_ref[:, 128 * k : 128 * k + 128] = dot_nt(
            dy_ref[:, 128 * c0 : 128 * c0 + w], wd0_ref[PAIR_OF[k], :, 0:w]
        ).astype(BF16)
    backward_edges(core, dagg_ref, dy_ref, agg0_ref, h0_ref[...], t_ref, tt_ref, ee_ref,
                   w0_ref, w1_ref, w2_ref, hb_ref, selq_ref, selr_ref, selp_ref, hs_ref, None, v_ref,
                   gate_ref[...], tq_ref[...], us_ref, dv_ref, dr_ref, None, gm_ref, gs_ref)
    for k, (c0, n, _) in enumerate(SEGMENTS):
        w = 128 * n
        agg = own_ref[:, 128 * k : 128 * k + 128] + rcv_ref[:, 128 * k : 128 * k + 128].astype(F32)
        out = dot(agg.astype(BF16), wd1_ref[PAIR_OF[k], :, 0:w])
        out = (x1_ref[0:16, 128 * c0 : 128 * c0 + w] + out).astype(BF16)
        for m in range(n):
            x2_ref[c0 + m] = out[:, 128 * m : 128 * m + 128]
    x2_ref[LOW:] = nf_ref[LOW:]


def kernel_pack(ma, pa, mb, pb, out_ref, g_ref, chunk_ref):
    lane14 = lax.broadcasted_iota(jnp.int32, (16, 128), 1)
    for layer, (mine, other) in enumerate(((ma, pa), (mb, pb))):
        g_ref[...] = mine[...] + other[...].astype(F32)
        base = 56 * layer
        for d in range(32):
            to_d, row0 = d % 16, 112 * (d // 16) + base
            chunk_ref[to_d, row0 : row0 + 14, :] = g_ref[14 * d : 14 * d + 14, :]
            chunk_ref[to_d, row0 + 14 : row0 + 38, :] = g_ref[512 + 24 * d : 536 + 24 * d, :]
            row = 1280 + 20 * d + (64 if d >= 16 else 0)
            chunk_ref[to_d, row0 + 38 : row0 + 56, :] = g_ref[row : row + 18, :]
            last = g_ref[row + 18 : row + 20, :]
            for k in range(3):
                chunk_ref[to_d, row0 + 32 + 2 * k : row0 + 34 + 2 * k, 96:128] = pltpu.roll(last, 96 - 32 * k, 1)[
                    :, 96:128
                ]
            for q in range(7):
                chunk_ref[to_d, row0 + 2 * q : row0 + 2 * q + 2, 112:128] = g_ref[
                    64 * q + 2 * d : 64 * q + 2 * d + 2, 112:128
                ]
            chunk_ref[to_d, row0 + 14 : row0 + 16, 112:128] = g_ref[448 + 2 * d : 450 + 2 * d, 112:128]
            for start, width, at, to in ((72 * d, 48, 80, 38), (72 * d + 48, 24, 96, 16)):
                blk, off = start // 128, start % 128
                shift = (at - off) % 128
                left = g_ref[2048 + 16 * blk : 2064 + 16 * blk, :]
                win = pltpu.roll(left, shift, 1) if shift else left
                if off + width > 128:
                    right = g_ref[2064 + 16 * blk : 2080 + 16 * blk, :]
                    right = pltpu.roll(right, shift, 1) if shift else right
                    win = jnp.where(lane14 < at + 128 - off, win, right)
                chunk_ref[to_d, row0 + to : row0 + to + 16, at : at + width] = win[:, at : at + width]
    out_ref[...] = chunk_ref[...].astype(BF16)


def kernel_plane(half_ref, in_ref, own_ref, snd_ref):
    for h in range(2):
        acc = in_ref[0, 112 * h : 112 * h + 112].astype(F32)
        for d in range(1, 16):
            acc = acc + in_ref[d, 112 * h : 112 * h + 112].astype(F32)

        @pl.when(half_ref[0] == h)
        def _():
            own_ref[...] = acc

        @pl.when(half_ref[0] != h)
        def _():
            snd_ref[...] = acc.astype(BF16)


def kernel_finish(in_ref, rcv_ref, zero_ref, one_ref, two_ref, rad_ref, q_ref, out_ref, acc_ref):
    acc_ref[...] = in_ref[...] + rcv_ref[...].astype(F32)
    lane = lax.broadcasted_iota(jnp.int32, (16, 128), 1)
    for layer in range(2):
        b = 56 * layer
        for r in range(14):
            zero_ref[r, layer : layer + 1, :] = acc_ref[b + r : b + r + 1, 0:112]
        one_ref[layer] = acc_ref[b + 14 : b + 38, 0:96]
        for r in range(18):
            two_ref[r, layer : layer + 1, :] = acc_ref[b + 38 + r : b + 39 + r, 0:80]
        first, second, third = [
            pltpu.roll(acc_ref[b + 32 + 2 * k : b + 34 + 2 * k, :], 32 + 32 * k, 1) for k in range(3)
        ]
        lane2 = lax.broadcasted_iota(jnp.int32, (2, 128), 1)
        last = jnp.where(lane2 < 32, first, jnp.where(lane2 < 64, second, third))
        for r in range(2):
            two_ref[18 + r, layer : layer + 1, :] = last[r : r + 1, 0:80]
        q_ref[layer] = pltpu.roll(acc_ref[b + 14 : b + 16, :], 16, 1)[:, 0:16]
        low = pltpu.roll(acc_ref[b + 38 : b + 54, :], 48, 1)
        high = pltpu.roll(acc_ref[b + 16 : b + 32, :], 80, 1)
        rad_ref[layer] = jnp.where(lane < 48, low, high)[:, 0:72]
        tail = pltpu.roll(acc_ref[b : b + 16, :], 16, 1)
        for q in range(7):
            out_ref[layer, q] = tail[2 * q : 2 * q + 2, 0:16]


def kernel_load(nf_ref, ee_ref, src_ref, tgt_ref, count_ref, cot_ref, own_ref, low_cot_ref,
                tail_ref, ids_ref, count_smem, sems):
    copies = [
        pltpu.make_async_copy(nf_ref.at[pl.ds(LOW, 20)], tail_ref, sems.at[0]),
        pltpu.make_async_copy(src_ref, ids_ref.at[0], sems.at[1]),
        pltpu.make_async_copy(tgt_ref, ids_ref.at[1], sems.at[2]),
        pltpu.make_async_copy(count_ref, count_smem, sems.at[3]),
        pltpu.make_async_copy(nf_ref.at[pl.ds(0, LOW)], own_ref.at[pl.ds(0, LOW)], sems.at[4]),
        pltpu.make_async_copy(ee_ref, own_ref.at[pl.ds(30, 8)], sems.at[5]),
        pltpu.make_async_copy(cot_ref.at[pl.ds(0, LOW)], low_cot_ref, sems.at[6]),
    ]
    for copy in copies:
        copy.start()
    copies[0].wait()
    tail = jnp.zeros((16, 128), F32)
    for i in range(20):
        x = tail_ref[i].astype(F32)
        tail = tail + x * x
    tail = jnp.broadcast_to(jnp.sum(tail, axis=1, keepdims=True), (16, 128))
    lane = lax.broadcasted_iota(jnp.int32, (16, 128), 1)
    hi = tail.astype(BF16).astype(F32)
    mid = (tail - hi).astype(BF16).astype(F32)
    pieces = jnp.where(lane == 0, hi, jnp.where(lane == 1, mid, jnp.where(lane == 2, tail - hi - mid, 0.0)))
    own_ref[LOW] = pieces.astype(BF16)
    for copy in copies[1:4]:
        copy.wait()
    row = lax.broadcasted_iota(jnp.int32, (16, 128), 0)
    live = jnp.where(lane < count_smem[0, 0], 1.0, 0.0)
    src = jnp.broadcast_to(ids_ref[0], (16, 128)).astype(F32)
    tgt = jnp.broadcast_to(ids_ref[1], (16, 128)).astype(F32)
    ids = jnp.where(row == 0, src, jnp.where(row == 1, tgt, jnp.where(row == 2, live, 0.0)))
    own_ref[38] = ids.astype(BF16)
    for copy in copies[4:]:
        copy.wait()


def kernel_weights(pos_ref, zero_ref, one_ref, two_ref, query_ref, out_ref,
                   w0_ref, w1_ref, w2_ref, q_ref, wd_ref, sel0_ref, sel1_ref, sel2_ref, selq_ref, selr_ref, selp_ref):
    z_lo = pos_ref[0] // 2
    for k in range(2):
        w0_ref[k, 0:448, :] = zero_ref[k]
        w0_ref[k, 448:512, :] = jnp.zeros((64, 896), BF16)
        a, b = one_ref[k, :, 0:384], one_ref[k, :, 384:768]
        w1_ref[k, 0:768, 0:384] = a
        w1_ref[k, 0:768, 384:768] = b
        w1_ref[k, 768:1536, 0:384] = -b
        w1_ref[k, 768:1536, 384:768] = a
        blank = jnp.zeros((640, 64), BF16)
        a = jnp.concatenate([two_ref[k, :, 0:320], blank], axis=1)
        b = jnp.concatenate([two_ref[k, :, 320:640], blank], axis=1)
        w2_ref[k, 0:640, 0:384] = a
        w2_ref[k, 0:640, 384:768] = b
        w2_ref[k, 640:1280, 0:384] = -b
        w2_ref[k, 640:1280, 384:768] = a
        q_ref[k, 0:64, :] = query_ref[k]
        q_ref[k, 64:128, :] = jnp.zeros((64, 128), BF16)
        none = jnp.zeros((64, 128), BF16)
        for p, (d, e) in enumerate(PAIRS):
            wd_ref[k, p, 0:64, 0:128] = out_ref[k, d]
            wd_ref[k, p, 0:64, 128:256] = none
            wd_ref[k, p, 64:128, 0:128] = none
            wd_ref[k, p, 64:128, 128:256] = none if e is None else out_ref[k, e]

    def select(rows, width, first_lane, scale):
        k = lax.broadcasted_iota(jnp.int32, (rows, 128), 0)
        m = lax.broadcasted_iota(jnp.int32, (rows, 128), 1) - first_lane
        live = (m >= 0) & (m < width)
        lo = jnp.where(live & (k == scale * z_lo + m), 1.0, 0.0)
        hi = jnp.where(live & (k == scale * z_lo + width + m), 1.0, 0.0)
        return jnp.concatenate([lo, hi], axis=1).astype(BF16)

    sel0_ref[...] = select(896, 112, 0, 224)
    sel1_ref[...] = select(768, 96, 0, 192)
    sel2_ref[...] = select(640, 80, 0, 160)
    selq = select(128, 16, 112, 32)
    selq_ref[...] = selq
    blank = jnp.zeros((128, 256), BF16)
    selp_ref[0:128, 0:256] = selq
    selp_ref[0:128, 256:512] = blank
    selp_ref[128:256, 0:256] = blank
    selp_ref[128:256, 256:512] = selq
    rows = lax.broadcasted_iota(jnp.int32, (32, 128), 0)
    cols = lax.broadcasted_iota(jnp.int32, (32, 128), 1)
    selr_ref[...] = jnp.where(cols == 32 * z_lo + rows, 1.0, 0.0).astype(BF16)


def call(body, outs, scratch, n_in, limit=16, cost=None):
    return pl.pallas_call(
        body,
        in_specs=[pl.BlockSpec(memory_space=pltpu.SMEM)] + [pl.BlockSpec(memory_space=pltpu.VMEM)] * (n_in - 1),
        out_specs=[pl.BlockSpec(memory_space=pltpu.VMEM)] * len(outs),
        out_shape=[jax.ShapeDtypeStruct(s, t) for s, t in outs],
        scratch_shapes=[pltpu.VMEM(s, t) for s, t in scratch],
        compiler_params=pltpu.CompilerParams(vmem_limit_bytes=limit * MIB),
        cost_estimate=cost,
    )


def plain_call(body, outs, scratch, limit=16):
    return pl.pallas_call(
        body,
        out_shape=[jax.ShapeDtypeStruct(s, t) for s, t in outs],
        scratch_shapes=[pltpu.VMEM(s, t) for s, t in scratch],
        compiler_params=pltpu.CompilerParams(vmem_limit_bytes=limit * MIB),
    )


def swap(x, bits):
    return lax.ppermute(x, "graph", [(i, i ^ bits) for i in range(8)])


def shards(node_features, edge_embed, sources, targets, edge_counts, w_zero, w_one, w_two, radial, query, w_out, cotangent):
    pos_arr = lax.axis_index("graph").astype(jnp.int32)[None]
    nf = jnp.transpose(node_features[0], (1, 0, 2))
    shard = (16, 128)
    own, cot = pl.pallas_call(
        kernel_load,
        in_specs=[pl.BlockSpec(memory_space=pltpu.HBM)] * 6,
        out_specs=[pl.BlockSpec(memory_space=pltpu.VMEM)] * 2,
        out_shape=[jax.ShapeDtypeStruct((39, *shard), BF16), jax.ShapeDtypeStruct((LOW, *shard), BF16)],
        scratch_shapes=[
            pltpu.VMEM((20, *shard), BF16), pltpu.VMEM((2, 1, 128), jnp.int32), pltpu.SMEM((1, 1), jnp.int32),
            pltpu.SemaphoreType.DMA((7,)),
        ],
        compiler_params=pltpu.CompilerParams(vmem_limit_bytes=56 * MIB),
    )(nf, edge_embed[0].reshape(8, 16, 128), sources, targets, edge_counts, jnp.transpose(cotangent[0], (1, 0, 2)))
    far = [swap(own, k) for k in (2, 4, 6)]
    pair = [swap(b, 1) for b in [own] + far]
    bufs = [own, pair[0], far[0], pair[1], far[1], pair[2], far[2], pair[3]]
    cfar = [swap(cot, k) for k in (2, 4, 6)]

    w0p, w1c, w2c, qp, wd, sel0, sel1, sel2, selq, selr, selp = call(
        kernel_weights,
        [((2, 512, 896), BF16), ((2, 1536, 768), BF16), ((2, 1280, 768), BF16), ((2, 128, 128), BF16),
         ((2, 7, 128, 256), BF16), ((896, 256), BF16), ((768, 256), BF16), ((640, 256), BF16),
         ((128, 256), BF16), ((32, 128), BF16), ((256, 512), BF16)],
        [],
        6,
    )(pos_arr, jnp.swapaxes(w_zero, 1, 2), w_one, w_two, jnp.swapaxes(query, 1, 2), w_out)
    hf = jnp.asarray(HEAD_FIRST, BF16)
    hb = jnp.asarray(HEAD_BOTH, BF16)

    big = (EDGES, LOW * CH)
    agg0, s_mat, t_mat, tt, st, ee, v0, gate0, tq0, hs0, us0, h00 = call(
        kernel_first,
        [((NODES, 2048), BF16), ((EDGES, 128), BF16), ((EDGES, 128), BF16), ((128, EDGES), BF16),
         ((128, EDGES), BF16), ((EDGES, 128), BF16), ((EDGES, 2048), BF16), ((EDGES, 128), F32),
         ((EDGES, 128), F32), (big, BF16), ((5, EDGES, 256), BF16), ((NODES, 128), BF16)],
        [((NODES, LOW * CH), BF16), (big, BF16)],
        18,
        20,
        pl.CostEstimate(flops=1, bytes_accessed=1, transcendentals=0),
    )(pos_arr, *bufs, w0p[0], w1c[0], w2c[0], radial[0], qp[0], hf, sel0, sel1, sel2)
    agg0p = swap(agg0, 1)
    grad_rows = 2048 + 288
    x1, s1, own1, snd1, agg1, h01, hs1, r1, v1, gate1, tq1, us1 = plain_call(
        kernel_second,
        [((NODES, LOW * CH), F32), ((NODES, 128), F32), ((16, 2048), F32), ((16, 2048), BF16),
         ((NODES, 2048), BF16), ((NODES, 128), BF16), (big, BF16), ((EDGES, 2304), BF16), ((EDGES, 2048), BF16),
         ((EDGES, 128), F32), ((EDGES, 128), F32), ((5, EDGES, 256), BF16)],
        [((NODES, LOW * CH), BF16), (big, BF16)],
        20,
    )(*bufs, agg0, agg0p, s_mat, t_mat, tt, ee, wd[0], w0p[1], w1c[1], w2c[1],
      radial[1], qp[1], hf, sel0, sel1, sel2)
    rcv1 = swap(snd1, 1)
    *cfar, agg1 = lax.optimization_barrier((*cfar, agg1))
    cpair = [swap(b, 1) for b in [cot] + cfar]
    cots = [cot, cpair[0], cfar[0], cpair[1], cfar[1], cpair[2], cfar[2], cpair[3]]
    dh, gm1, gs1 = call(
        kernel_back,
        [((NODES, LOW * CH), BF16), ((grad_rows, 128), F32), ((grad_rows, 128), BF16)],
        [((NODES, LOW * CH), BF16), ((NODES, 2048), BF16), ((EDGES, 2048), BF16), ((EDGES, 2304), BF16),
         (big, BF16)],
        30,
        20,
    )(pos_arr, *cots, agg1, h01, t_mat, tt, st, ee, v1, gate1, tq1, hs1, r1, us1,
      wd[1], w0p[1], w1c[1], w2c[1], qp[1], hb, selq, selr, selp)
    dhp = swap(dh, 1)
    gp1 = swap(gs1, 1)
    gm0, gs0, x2 = call(
        kernel_third,
        [((grad_rows, 128), F32), ((grad_rows, 128), BF16), ((49, 16, 128), BF16)],
        [((NODES, LOW * CH), BF16), ((NODES, 2048), BF16), ((EDGES, 2048), BF16), ((EDGES, 2304), BF16),
         ((NODES, LOW * CH), F32)],
        35,
        20,
    )(pos_arr, *cots, x1, s1, dh, dhp, agg0, t_mat, tt, ee, v0, gate0, tq0, hs0, us0, h00,
      wd[0], wd[1], w0p[0], w1c[0], w2c[0], hb, selq, selr, selp, own1, rcv1, nf)
    gp0 = swap(gs0, 1)
    result = jnp.transpose(x2, (1, 0, 2))[None]
    (packed,) = plain_call(
        kernel_pack, [((16, 224, 128), BF16)], [((grad_rows, 128), F32), ((16, 224, 128), F32)]
    )(gm0, gp0, gm1, gp1)
    planes = [[16 * h + a for a in range(16)] for h in range(2)]
    moved = lax.all_to_all(packed, "dp", split_axis=0, concat_axis=0, tiled=True, axis_index_groups=planes)
    half = (lax.axis_index("dp") // 16).astype(jnp.int32)[None]
    mine, theirs = call(kernel_plane, [((112, 128), F32), ((112, 128), BF16)], [], 2)(half, moved)
    theirs = lax.ppermute(theirs, "dp", [(i, i ^ 16) for i in range(32)])
    zero, one, two, rad, q, out = plain_call(
        kernel_finish,
        [((14, 2, 112), F32), ((2, 24, 96), F32), ((20, 2, 80), F32), ((2, 16, 72), F32),
         ((2, 2, 16), F32), ((2, 7, 2, 16), F32)],
        [((112, 128), F32)],
    )(mine, theirs)
    return (
        result,
        jnp.transpose(zero, (1, 2, 0)),
        jnp.transpose(one, (0, 2, 1)),
        jnp.transpose(two, (1, 2, 0)),
        rad,
        jnp.transpose(q, (0, 2, 1)),
        out,
    )


def solution(mesh):
    by_graph = P("dp", "graph")
    in_specs = (
        P("dp", "graph", None, None),
        P("dp", "graph", None),
        by_graph,
        by_graph,
        by_graph,
        P(),
        P(),
        P(),
        P(),
        P(),
        P(),
        P("dp", "graph", None, None),
    )
    out_specs = (
        P("dp", "graph", None, None),
        P(None, "graph", "dp"),
        P(None, "graph", "dp"),
        P(None, "graph", "dp"),
        P(None, "graph", "dp"),
        P(None, "graph", "dp"),
        P(None, None, "dp", "graph"),
    )
    return jax.shard_map(shards, mesh=mesh, in_specs=in_specs, out_specs=out_specs, check_vma=False)
```

```python
import functools

import jax
import jax.numpy as jnp
import numpy as np
from jax import lax
from jax.experimental import pallas as pl
from jax.experimental.pallas import tpu as pltpu
from jax.sharding import PartitionSpec as P

F32 = jnp.float32
BF16 = jnp.bfloat16
LOW = 29
CH = 128
NODES = 128
EDGES = 512
ENTRIES = 49 * 128
NORM_EPS = 1e-6
HEAD_SCALE = 8 ** -0.5
MIB = 1024 * 1024
LIM_A = 10
LIM_B = 10
LIM_C = 16
LIM_D = 12
LIM_E = 10

SEGMENTS = (
    [(0, 2, 0), (2, 2, 2), (4, 2, 4), (6, 1, 6)]
    + [(7, 2, 7), (9, 2, 9), (11, 2, 11)]
    + [(13, 2, 7), (15, 2, 9), (17, 2, 11)]
    + [(19, 2, 13), (21, 2, 15), (23, 1, 17)]
    + [(24, 2, 13), (26, 2, 15), (28, 1, 17)]
)
PAIRS = [(0, 1), (2, 3), (4, 5), (6, None), (1, 2), (3, 4), (5, 6)]
PAIR_OF = [0, 1, 2, 3, 4, 5, 6, 4, 5, 6, 1, 2, 3, 1, 2, 3]

HEAD_FIRST = np.zeros((256, 128), np.float32)
HEAD_BOTH = np.zeros((256, 128), np.float32)
for c_row in range(256):
    for c_col in range(128):
        same = (c_row % 64) // 8 == (c_col % 64) // 8
        HEAD_BOTH[c_row, c_col] = same
        HEAD_FIRST[c_row, c_col] = same and (c_row % 128) < 64


def dot(a, b):
    return lax.dot_general(a, b, (((1,), (0,)), ((), ())), preferred_element_type=F32)


def dot_nt(a, b):
    return lax.dot_general(a, b, (((1,), (1,)), ((), ())), preferred_element_type=F32)


def dot_tn(a, b):
    return lax.dot_general(a, b, (((0,), (0,)), ((), ())), preferred_element_type=F32)


def split_hi_lo(a):
    hi = a.astype(BF16)
    return hi, (a - hi.astype(F32)).astype(BF16)


def swap16(a):
    rows = []
    for b in range(a.shape[0] // 16):
        rows.append(a[16 * (b ^ 1) : 16 * (b ^ 1) + 16])
    return jnp.concatenate(rows, axis=0)


def forward_edges(h_ref, s_ref, t_ref, tt_ref, ee_ref, w0_ref, w1_ref, w2_ref, rad_ref, q_ref, hf_ref,
                  u_ref, hs_ref, r_ref, v_ref, gate_ref, tq_ref, agg_store):
    s_mat = s_ref[...]
    ee = ee_ref[...]
    r_vals = {}
    for c0, n, g0 in SEGMENTS:
        w = 128 * n
        if g0 not in r_vals:
            r_vals[g0] = dot(ee, rad_ref[:, 128 * g0 : 128 * g0 + w])
            if r_ref is not None:
                r_ref[:, 128 * g0 : 128 * g0 + w] = r_vals[g0].astype(BF16)
        hs = dot(s_mat, h_ref[:, 128 * c0 : 128 * c0 + w])
        hs_ref[:, 128 * c0 : 128 * c0 + w] = hs.astype(BF16)
        u_ref[:, 128 * c0 : 128 * c0 + w] = (hs * r_vals[g0]).astype(BF16)
    v0 = dot_nt(u_ref[:, 0:896], w0_ref[...])
    v_ref[:, 0:512] = v0.astype(BF16)
    q_hi, q_lo = split_hi_lo(dot_nt(h_ref[:, 0:128], q_ref[...]))
    t_mat = t_ref[...]
    tq = dot(t_mat, jnp.concatenate([q_hi, q_lo], axis=1))
    tq = tq[:, :128] + tq[:, 128:]
    tq_ref[...] = tq
    p_hi, p_lo = split_hi_lo(v0[:, :128] * tq)
    logits = dot(jnp.concatenate([p_hi, p_lo], axis=1), hf_ref[...]) * HEAD_SCALE
    gate = jax.nn.sigmoid(logits)
    gate_ref[...] = gate
    tt = tt_ref[...]

    def send(values, col):
        n = values.shape[1] // 128
        msg = jnp.concatenate(
            [(values[:, 128 * b : 128 * b + 128] * gate).astype(BF16) for b in range(n)], axis=1
        )
        agg_store(col, dot(tt, msg))

    send(v0[:, 0:256], 0)
    send(v0[:, 256:512], 256)
    v1 = dot(u_ref[:, 896:2432], w1_ref[...])
    v_ref[:, 512:1280] = v1.astype(BF16)
    for b in range(3):
        send(v1[:, 256 * b : 256 * b + 256], 512 + 256 * b)
    v2 = dot(u_ref[:, 2432:3712], w2_ref[...])
    v_ref[:, 1280:2048] = v2.astype(BF16)
    for b in range(3):
        send(v2[:, 256 * b : 256 * b + 256], 1280 + 256 * b)


def select_rows(u_ref, sel0_ref, sel1_ref, sel2_ref, us_ref):
    us_ref[0] = dot(u_ref[:, 0:896], sel0_ref[...]).astype(BF16)
    us_ref[1] = dot(u_ref[:, 896:1664], sel1_ref[...]).astype(BF16)
    us_ref[2] = dot(u_ref[:, 1664:2432], sel1_ref[...]).astype(BF16)
    us_ref[3] = dot(u_ref[:, 2432:3072], sel2_ref[...]).astype(BF16)
    us_ref[4] = dot(u_ref[:, 3072:3712], sel2_ref[...]).astype(BF16)


def backward_edges(dagg_ref, t_ref, tt_ref, w0_ref, w1_ref, w2_ref, hb_ref, hs_ref, r_ref, v_ref, gate, tq,
                   dv_ref, dr_ref, w_ref):
    t_mat = t_ref[...]
    acc = jnp.zeros((EDGES, 128), F32)
    first = None
    for p in range(8):
        dm = dot(t_mat, dagg_ref[:, 256 * p : 256 * p + 256])
        for b in range(2):
            col = 256 * p + 128 * b
            part = dm[:, 128 * b : 128 * b + 128]
            acc = acc + part * v_ref[:, col : col + 128].astype(F32)
            scaled = part * gate
            if col == 0:
                first = scaled
            else:
                dv_ref[:, col : col + 128] = scaled.astype(BF16)
    a_hi, a_lo = split_hi_lo(acc)
    dalpha = dot(jnp.concatenate([a_hi, a_lo], axis=1), hb_ref[...])
    per = dalpha * gate * (1.0 - gate) * HEAD_SCALE
    dv_ref[:, 0:128] = (first + per * tq).astype(BF16)
    lane = lax.broadcasted_iota(jnp.int32, (EDGES, 128), 1)
    dq = jnp.where(lane < 64, per * v_ref[:, 0:128].astype(F32), 0.0).astype(BF16)
    dqn = dot(tt_ref[...], dq)

    def grads_of(col, width, weight_ref, row):
        if col == 0:
            return dot(dv_ref[:, col : col + width], weight_ref[:, row])
        return dot_nt(dv_ref[:, col : col + width], weight_ref[row, :])

    plans = (
        (SEGMENTS[0:4], None, 0, 512, w0_ref, 0),
        (SEGMENTS[4:7], SEGMENTS[7:10], 512, 768, w1_ref, 768),
        (SEGMENTS[10:13], SEGMENTS[13:16], 1280, 768, w2_ref, 640),
    )
    for plus, minus, col, width, weight_ref, half in plans:
        base = plus[0][0]
        for k, (c0, n, g0) in enumerate(plus):
            w = 128 * n
            at = 128 * (c0 - base)
            du = grads_of(col, width, weight_ref, pl.ds(at, w))
            dr = du * hs_ref[:, 128 * c0 : 128 * c0 + w].astype(F32)
            if w_ref is not None:
                rg = r_ref[:, 128 * g0 : 128 * g0 + w].astype(F32)
                w_ref[:, 128 * c0 : 128 * c0 + w] = (du * rg).astype(BF16)
            if minus is not None:
                m0 = minus[k][0]
                dum = grads_of(col, width, weight_ref, pl.ds(half + at, w))
                dr = dr + dum * hs_ref[:, 128 * m0 : 128 * m0 + w].astype(F32)
                if w_ref is not None:
                    w_ref[:, 128 * m0 : 128 * m0 + w] = (dum * rg).astype(BF16)
            dr_ref[:, 128 * g0 : 128 * g0 + w] = dr.astype(BF16)
    return dqn


def weight_grads(core, dy_ref, agg_ref, h0, dqn, ee_ref, selq_ref, selr_ref, us_ref, dv_ref, dr_ref, gm_ref, gs_ref):
    def put(row, val):
        n = val.shape[0]
        lo, hi = val[:, :128], val[:, 128:]
        gm_ref[row : row + n, :] = jnp.where(core == 0, lo, hi)
        gs_ref[row : row + n, :] = jnp.where(core == 0, hi, lo).astype(BF16)

    sums = [None] * 7
    for k, (c0, n, _) in enumerate(SEGMENTS):
        degs = PAIRS[PAIR_OF[k]]
        prod = dot_tn(agg_ref[:, 128 * k : 128 * k + 128], dy_ref[:, 128 * c0 : 128 * c0 + 128 * n])
        for m in range(n):
            piece = prod[64 * m : 64 * m + 64, 128 * m : 128 * m + 128]
            d = degs[m]
            sums[d] = piece if sums[d] is None else sums[d] + piece
    sums.append(dot_tn(dqn.astype(BF16), h0)[0:64])
    e_hi, e_lo = split_hi_lo(jnp.concatenate(sums, axis=0))
    selq = selq_ref[...]
    extra = dot(jnp.concatenate([e_hi, e_lo], axis=1), jnp.concatenate([selq, selq], axis=0))
    dv0t = dv_ref[:, 0:512].T
    put(0, dot(dv0t, us_ref[0]) + extra)
    up, um = us_ref[1], us_ref[2]
    dpt = dv_ref[:, 512:896].T
    dmt = dv_ref[:, 896:1280].T
    put(512, dot(dpt, up) + dot(dmt, um))
    put(896, dot(dmt, up) - dot(dpt, um))
    up, um = us_ref[3], us_ref[4]
    dpt = dv_ref[:, 1280:1664].T
    dmt = dv_ref[:, 1664:2048].T
    put(1280, dot(dpt, up) + dot(dmt, um))
    put(1664, dot(dmt, up) - dot(dpt, um))
    ees = dot_nt(selr_ref[...], ee_ref[...]).astype(BF16)
    for p in range(9):
        pr = dot(ees, dr_ref[:, 256 * p : 256 * p + 256])
        mine = jnp.where(core == 0, pr[0:16], pr[16:32])
        theirs = jnp.where(core == 0, pr[16:32], pr[0:16]).astype(BF16)
        for b in range(2):
            row = 2048 + 16 * (2 * p + b)
            gm_ref[row : row + 16, :] = mine[:, 128 * b : 128 * b + 128]
            gs_ref[row : row + 16, :] = theirs[:, 128 * b : 128 * b + 128]


def node_block(bufs, i):
    return jnp.concatenate([b[i] for b in bufs], axis=0)


def kernel_first(pos_ref, b0, b1, b2, b3, b4, b5, b6, b7, w0_ref, w1_ref, w2_ref, rad_ref, q_ref, hf_ref,
                 agg_ref, s_ref, t_ref, tt_ref, st_ref, ee_ref, v_ref, gate_ref, tq_ref, hs_ref, u_ref, h0_ref,
                 h_ref):
    bufs = [b0, b1, b2, b3, b4, b5, b6, b7]
    mask = 16 * pos_ref[0]
    iota = lax.broadcasted_iota(jnp.int32, (NODES, 128), 0)
    for k in range(4):
        buf = bufs[2 * k]
        ids = buf[38].astype(F32)
        src = ids[0:1].astype(jnp.int32) ^ mask
        tgt = ids[1:2].astype(jnp.int32) ^ mask
        s_hot = jnp.where(iota == src, 1.0, 0.0)
        t_hot = jnp.where(iota == tgt, 1.0, 0.0) * ids[2:3]
        st_ref[:, 128 * k : 128 * k + 128] = s_hot.astype(BF16)
        tt_ref[:, 128 * k : 128 * k + 128] = t_hot.astype(BF16)
        s_ref[128 * k : 128 * k + 128, :] = s_hot.T.astype(BF16)
        t_ref[128 * k : 128 * k + 128, :] = t_hot.T.astype(BF16)
        for m in range(8):
            ee_ref[128 * k + 16 * m : 128 * k + 16 * m + 16, :] = buf[30 + m]
    total = jnp.zeros((NODES, CH), F32)
    for i in range(LOW):
        x = node_block(bufs, i).astype(F32)
        total = total + x * x
    total = total + node_block(bufs, LOW).astype(F32)
    scale = lax.rsqrt(jnp.sum(total, axis=1, keepdims=True) * (1.0 / ENTRIES) + NORM_EPS)
    for i in range(LOW):
        h_ref[:, 128 * i : 128 * i + 128] = (node_block(bufs, i).astype(F32) * scale).astype(BF16)
    h0_ref[...] = h_ref[:, 0:128]

    def agg_store(col, val):
        agg_ref[:, col : col + 256] = val.astype(BF16)

    forward_edges(h_ref, s_ref, t_ref, tt_ref, ee_ref, w0_ref, w1_ref, w2_ref, rad_ref.at[0], q_ref, hf_ref,
                  u_ref, hs_ref, None, v_ref, gate_ref, tq_ref, agg_store)


def kernel_second(b0, b1, b2, b3, b4, b5, b6, b7, agg0_ref, agg0p_ref, s_ref, t_ref, tt_ref, ee_ref,
                  wd0_ref, w0_ref, w1_ref, w2_ref, rad_ref, q_ref, hf_ref,
                  x1_ref, s1_ref, own_ref, snd_ref, agg1_ref, h0_ref, hs_ref, r_ref, v_ref, gate_ref, tq_ref, u_ref,
                  h_ref):
    bufs = [b0, b1, b2, b3, b4, b5, b6, b7]
    total = node_block(bufs, LOW).astype(F32)
    for k, (c0, n, _) in enumerate(SEGMENTS):
        agg = agg0_ref[:, 128 * k : 128 * k + 128].astype(F32)
        agg = agg + swap16(agg0p_ref[:, 128 * k : 128 * k + 128]).astype(F32)
        out = dot(agg.astype(BF16), wd0_ref[PAIR_OF[k]])
        for m in range(n):
            x = node_block(bufs, c0 + m).astype(F32) + out[:, 128 * m : 128 * m + 128]
            x1_ref[:, 128 * (c0 + m) : 128 * (c0 + m) + 128] = x
            total = total + x * x
    scale = lax.rsqrt(jnp.sum(total, axis=1, keepdims=True) * (1.0 / ENTRIES) + NORM_EPS)
    s1_ref[...] = jnp.broadcast_to(scale, (NODES, 128))
    for i in range(LOW):
        h_ref[:, 128 * i : 128 * i + 128] = (x1_ref[:, 128 * i : 128 * i + 128] * scale).astype(BF16)
    h0_ref[...] = h_ref[:, 0:128]

    def agg_store(col, val):
        agg1_ref[:, col : col + 256] = val.astype(BF16)
        own_ref[:, col : col + 256] = val[0:16]
        snd_ref[:, col : col + 256] = val[16:32].astype(BF16)

    forward_edges(h_ref, s_ref, t_ref, tt_ref, ee_ref, w0_ref, w1_ref, w2_ref, rad_ref.at[1], q_ref, hf_ref,
                  u_ref, hs_ref, r_ref, v_ref, gate_ref, tq_ref, agg_store)


def kernel_back(c0_, c1_, c2_, c3_, c4_, c5_, c6_, c7_, t_ref, tt_ref, st_ref, v_ref, gate_ref, tq_ref, hs_ref, r_ref,
                wd1_ref, w0_ref, w1_ref, w2_ref, q_ref, hb_ref,
                dh_ref, dy_ref, dv_ref, dr_ref, dqn_ref,
                dagg_ref, w_ref):
    cots = [c0_, c1_, c2_, c3_, c4_, c5_, c6_, c7_]
    for i in range(LOW):
        dy_ref[:, 128 * i : 128 * i + 128] = node_block(cots, i)
    for k, (c0, n, _) in enumerate(SEGMENTS):
        w = 128 * n
        dagg_ref[:, 128 * k : 128 * k + 128] = dot_nt(
            dy_ref[:, 128 * c0 : 128 * c0 + w], wd1_ref[PAIR_OF[k], :, 0:w]
        ).astype(BF16)
    dqn = backward_edges(dagg_ref, t_ref, tt_ref, w0_ref, w1_ref, w2_ref, hb_ref, hs_ref, r_ref, v_ref,
                         gate_ref[...], tq_ref[...], dv_ref, dr_ref, w_ref)
    dqn_ref[...] = dqn
    st = st_ref[...]
    d_hi, d_lo = split_hi_lo(dqn)
    back = dot(jnp.concatenate([d_hi, d_lo], axis=1), jnp.concatenate([q_ref[...], q_ref[...]], axis=0))
    for c0, n, _ in SEGMENTS:
        w = 128 * n
        val = dot(st, w_ref[:, 128 * c0 : 128 * c0 + w])
        if c0 == 0:
            val = val + jnp.concatenate([back, jnp.zeros((NODES, 128), F32)], axis=1)
        dh_ref[:, 128 * c0 : 128 * c0 + w] = val.astype(BF16)


def kernel_grads(pos_ref, dy_ref, agg_ref, h0_ref, dqn_ref, ee_ref, u_ref, dv_ref, dr_ref,
                 sel0_ref, sel1_ref, sel2_ref, selq_ref, selr_ref, gm_ref, gs_ref, us_ref):
    select_rows(u_ref, sel0_ref, sel1_ref, sel2_ref, us_ref)
    weight_grads(pos_ref[0] & 1, dy_ref, agg_ref, h0_ref[...], dqn_ref[...], ee_ref, selq_ref, selr_ref,
                 us_ref, dv_ref, dr_ref, gm_ref, gs_ref)


def kernel_third(pos_ref, c0_, c1_, c2_, c3_, c4_, c5_, c6_, c7_, x1_ref, s1_ref, dh_ref, dhp_ref,
                 agg0_ref, t_ref, tt_ref, ee_ref, v_ref, gate_ref, tq_ref, hs_ref, us_ref, h0_ref,
                 wd0_ref, w0_ref, w1_ref, w2_ref, hb_ref, selq_ref, selr_ref,
                 gm_ref, gs_ref,
                 dy_ref, dagg_ref, dv_ref, dr_ref, full_ref):
    cots = [c0_, c1_, c2_, c3_, c4_, c5_, c6_, c7_]
    inner = jnp.zeros((NODES, 128), F32)
    for i in range(LOW):
        cols = pl.ds(128 * i, 128)
        dh = dh_ref[:, cols].astype(F32) + swap16(dhp_ref[:, cols]).astype(F32)
        full_ref[:, cols] = dh
        inner = inner + dh * x1_ref[:, cols]
    s1 = s1_ref[...]
    coef = jnp.sum(inner, axis=1, keepdims=True) * (1.0 / ENTRIES) * (s1 * s1 * s1)
    for i in range(LOW):
        cols = pl.ds(128 * i, 128)
        dx = node_block(cots, i).astype(F32) + s1 * full_ref[:, cols] - x1_ref[:, cols] * coef
        dy_ref[:, cols] = dx.astype(BF16)
    for k, (c0, n, _) in enumerate(SEGMENTS):
        w = 128 * n
        dagg_ref[:, 128 * k : 128 * k + 128] = dot_nt(
            dy_ref[:, 128 * c0 : 128 * c0 + w], wd0_ref[PAIR_OF[k], :, 0:w]
        ).astype(BF16)
    dqn = backward_edges(dagg_ref, t_ref, tt_ref, w0_ref, w1_ref, w2_ref, hb_ref, hs_ref, None, v_ref,
                         gate_ref[...], tq_ref[...], dv_ref, dr_ref, None)
    weight_grads(pos_ref[0] & 1, dy_ref, agg0_ref, h0_ref[...], dqn, ee_ref, selq_ref, selr_ref,
                 us_ref, dv_ref, dr_ref, gm_ref, gs_ref)


def kernel_output(nf_ref, x1_ref, own_ref, rcv_ref, wd1_ref, x2_ref):
    for k, (c0, n, _) in enumerate(SEGMENTS):
        w = 128 * n
        agg = own_ref[:, 128 * k : 128 * k + 128] + rcv_ref[:, 128 * k : 128 * k + 128].astype(F32)
        out = dot(agg.astype(BF16), wd1_ref[PAIR_OF[k], :, 0:w])
        out = (x1_ref[0:16, 128 * c0 : 128 * c0 + w] + out).astype(BF16)
        for m in range(n):
            x2_ref[c0 + m] = out[:, 128 * m : 128 * m + 128]
    x2_ref[LOW:] = nf_ref[LOW:]


def kernel_chunks(mine, other, chunk_ref, g_ref):
    lane14 = lax.broadcasted_iota(jnp.int32, (16, 128), 1)
    g_ref[...] = mine[...] + other[...].astype(F32)
    for d in range(32):
        chunk_ref[d, 0:14, :] = g_ref[14 * d : 14 * d + 14, :]
        chunk_ref[d, 14:38, :] = g_ref[512 + 24 * d : 536 + 24 * d, :]
        row = 1280 + 20 * d + (64 if d >= 16 else 0)
        chunk_ref[d, 38:56, :] = g_ref[row : row + 18, :]
        last = g_ref[row + 18 : row + 20, :]
        for k in range(3):
            chunk_ref[d, 32 + 2 * k : 34 + 2 * k, 96:128] = pltpu.roll(last, 96 - 32 * k, 1)[:, 96:128]
        for q in range(7):
            chunk_ref[d, 2 * q : 2 * q + 2, 112:128] = g_ref[64 * q + 2 * d : 64 * q + 2 * d + 2, 112:128]
        chunk_ref[d, 14:16, 112:128] = g_ref[448 + 2 * d : 450 + 2 * d, 112:128]
        for start, width, at, to in ((72 * d, 48, 80, 38), (72 * d + 48, 24, 96, 16)):
            blk, off = start // 128, start % 128
            shift = (at - off) % 128
            left = g_ref[2048 + 16 * blk : 2064 + 16 * blk, :]
            win = pltpu.roll(left, shift, 1) if shift else left
            if off + width > 128:
                right = g_ref[2064 + 16 * blk : 2080 + 16 * blk, :]
                right = pltpu.roll(right, shift, 1) if shift else right
                win = jnp.where(lane14 < at + 128 - off, win, right)
            chunk_ref[d, to : to + 16, at : at + width] = win[:, at : at + width]


def kernel_pack(mine, other, late_ref, out_ref, g_ref, chunk_ref):
    kernel_chunks(mine, other, chunk_ref, g_ref)
    for d in range(32):
        both = jnp.concatenate([chunk_ref[d], late_ref[d]], axis=0)
        out_ref[d % 16, 112 * (d // 16) : 112 * (d // 16) + 112, :] = both.astype(BF16)


def kernel_plane(half_ref, in_ref, own_ref, snd_ref):
    for h in range(2):
        acc = in_ref[0, 112 * h : 112 * h + 112].astype(F32)
        for d in range(1, 16):
            acc = acc + in_ref[d, 112 * h : 112 * h + 112].astype(F32)

        @pl.when(half_ref[0] == h)
        def _():
            own_ref[...] = acc

        @pl.when(half_ref[0] != h)
        def _():
            snd_ref[...] = acc.astype(BF16)


def kernel_finish(in_ref, rcv_ref, zero_ref, one_ref, two_ref, rad_ref, q_ref, out_ref, acc_ref):
    acc_ref[...] = in_ref[...] + rcv_ref[...].astype(F32)
    lane = lax.broadcasted_iota(jnp.int32, (16, 128), 1)
    for layer in range(2):
        b = 56 * layer
        for r in range(14):
            zero_ref[r, layer : layer + 1, :] = acc_ref[b + r : b + r + 1, 0:112]
        one_ref[layer] = acc_ref[b + 14 : b + 38, 0:96]
        for r in range(18):
            two_ref[r, layer : layer + 1, :] = acc_ref[b + 38 + r : b + 39 + r, 0:80]
        first, second, third = [
            pltpu.roll(acc_ref[b + 32 + 2 * k : b + 34 + 2 * k, :], 32 + 32 * k, 1) for k in range(3)
        ]
        lane2 = lax.broadcasted_iota(jnp.int32, (2, 128), 1)
        last = jnp.where(lane2 < 32, first, jnp.where(lane2 < 64, second, third))
        for r in range(2):
            two_ref[18 + r, layer : layer + 1, :] = last[r : r + 1, 0:80]
        q_ref[layer] = pltpu.roll(acc_ref[b + 14 : b + 16, :], 16, 1)[:, 0:16]
        low = pltpu.roll(acc_ref[b + 38 : b + 54, :], 48, 1)
        high = pltpu.roll(acc_ref[b + 16 : b + 32, :], 80, 1)
        rad_ref[layer] = jnp.where(lane < 48, low, high)[:, 0:72]
        tail = pltpu.roll(acc_ref[b : b + 16, :], 16, 1)
        for q in range(7):
            out_ref[layer, q] = tail[2 * q : 2 * q + 2, 0:16]


def kernel_load(nf_ref, ee_ref, src_ref, tgt_ref, count_ref, cot_ref, own_ref, low_cot_ref,
                tail_ref, ids_ref, count_smem, sems):
    copies = [
        pltpu.make_async_copy(nf_ref.at[pl.ds(LOW, 20)], tail_ref, sems.at[0]),
        pltpu.make_async_copy(src_ref, ids_ref.at[0], sems.at[1]),
        pltpu.make_async_copy(tgt_ref, ids_ref.at[1], sems.at[2]),
        pltpu.make_async_copy(count_ref, count_smem, sems.at[3]),
        pltpu.make_async_copy(nf_ref.at[pl.ds(0, LOW)], own_ref.at[pl.ds(0, LOW)], sems.at[4]),
        pltpu.make_async_copy(ee_ref, own_ref.at[pl.ds(30, 8)], sems.at[5]),
        pltpu.make_async_copy(cot_ref.at[pl.ds(0, LOW)], low_cot_ref, sems.at[6]),
    ]
    for copy in copies:
        copy.start()
    copies[0].wait()
    tail = jnp.zeros((16, 128), F32)
    for i in range(20):
        x = tail_ref[i].astype(F32)
        tail = tail + x * x
    tail = jnp.broadcast_to(jnp.sum(tail, axis=1, keepdims=True), (16, 128))
    lane = lax.broadcasted_iota(jnp.int32, (16, 128), 1)
    hi = tail.astype(BF16).astype(F32)
    mid = (tail - hi).astype(BF16).astype(F32)
    pieces = jnp.where(lane == 0, hi, jnp.where(lane == 1, mid, jnp.where(lane == 2, tail - hi - mid, 0.0)))
    own_ref[LOW] = pieces.astype(BF16)
    for copy in copies[1:4]:
        copy.wait()
    row = lax.broadcasted_iota(jnp.int32, (16, 128), 0)
    live = jnp.where(lane < count_smem[0, 0], 1.0, 0.0)
    src = jnp.broadcast_to(ids_ref[0], (16, 128)).astype(F32)
    tgt = jnp.broadcast_to(ids_ref[1], (16, 128)).astype(F32)
    ids = jnp.where(row == 0, src, jnp.where(row == 1, tgt, jnp.where(row == 2, live, 0.0)))
    own_ref[38] = ids.astype(BF16)
    for copy in copies[4:]:
        copy.wait()


def kernel_weights(pos_ref, zero_ref, one_ref, two_ref, query_ref, out_ref, *outs):
    sel0_ref, sel1_ref, sel2_ref, selq_ref, selr_ref = outs[10:]
    z_lo = pos_ref[0] // 2
    for k in range(2):
        w0_ref, w1_ref, w2_ref, q_ref, wd_ref = outs[5 * k : 5 * k + 5]
        w0_ref[0:448, :] = zero_ref[k]
        w0_ref[448:512, :] = jnp.zeros((64, 896), BF16)
        a, b = one_ref[k, :, 0:384], one_ref[k, :, 384:768]
        w1_ref[0:768, 0:384] = a
        w1_ref[0:768, 384:768] = b
        w1_ref[768:1536, 0:384] = -b
        w1_ref[768:1536, 384:768] = a
        blank = jnp.zeros((640, 64), BF16)
        a = jnp.concatenate([two_ref[k, :, 0:320], blank], axis=1)
        b = jnp.concatenate([two_ref[k, :, 320:640], blank], axis=1)
        w2_ref[0:640, 0:384] = a
        w2_ref[0:640, 384:768] = b
        w2_ref[640:1280, 0:384] = -b
        w2_ref[640:1280, 384:768] = a
        q_ref[0:64, :] = query_ref[k]
        q_ref[64:128, :] = jnp.zeros((64, 128), BF16)
        none = jnp.zeros((64, 128), BF16)
        for p, (d, e) in enumerate(PAIRS):
            wd_ref[p, 0:64, 0:128] = out_ref[k, d]
            wd_ref[p, 0:64, 128:256] = none
            wd_ref[p, 64:128, 0:128] = none
            wd_ref[p, 64:128, 128:256] = none if e is None else out_ref[k, e]

    def select(rows, width, first_lane, scale):
        k = lax.broadcasted_iota(jnp.int32, (rows, 128), 0)
        m = lax.broadcasted_iota(jnp.int32, (rows, 128), 1) - first_lane
        live = (m >= 0) & (m < width)
        lo = jnp.where(live & (k == scale * z_lo + m), 1.0, 0.0)
        hi = jnp.where(live & (k == scale * z_lo + width + m), 1.0, 0.0)
        return jnp.concatenate([lo, hi], axis=1).astype(BF16)

    sel0_ref[...] = select(896, 112, 0, 224)
    sel1_ref[...] = select(768, 96, 0, 192)
    sel2_ref[...] = select(640, 80, 0, 160)
    selq = select(128, 16, 112, 32)
    selq_ref[...] = selq
    rows = lax.broadcasted_iota(jnp.int32, (32, 128), 0)
    cols = lax.broadcasted_iota(jnp.int32, (32, 128), 1)
    selr_ref[...] = jnp.where(cols == 32 * z_lo + rows, 1.0, 0.0).astype(BF16)


def call(body, outs, scratch, n_in, limit=16, cost=None):
    return pl.pallas_call(
        body,
        in_specs=[pl.BlockSpec(memory_space=pltpu.SMEM)] + [pl.BlockSpec(memory_space=pltpu.VMEM)] * (n_in - 1),
        out_specs=[pl.BlockSpec(memory_space=pltpu.VMEM)] * len(outs),
        out_shape=[jax.ShapeDtypeStruct(s, t) for s, t in outs],
        scratch_shapes=[pltpu.VMEM(s, t) for s, t in scratch],
        compiler_params=pltpu.CompilerParams(vmem_limit_bytes=limit * MIB),
        cost_estimate=cost,
    )


def plain_call(body, outs, scratch, limit=16):
    return pl.pallas_call(
        body,
        out_shape=[jax.ShapeDtypeStruct(s, t) for s, t in outs],
        scratch_shapes=[pltpu.VMEM(s, t) for s, t in scratch],
        compiler_params=pltpu.CompilerParams(vmem_limit_bytes=limit * MIB),
    )


def swap(x, bits):
    return lax.ppermute(x, "graph", [(i, i ^ bits) for i in range(8)])


def shards(node_features, edge_embed, sources, targets, edge_counts, w_zero, w_one, w_two, radial, query, w_out, cotangent):
    pos_arr = lax.axis_index("graph").astype(jnp.int32)[None]
    nf = jnp.transpose(node_features[0], (1, 0, 2))
    shard = (16, 128)
    own, cot = pl.pallas_call(
        kernel_load,
        in_specs=[pl.BlockSpec(memory_space=pltpu.HBM)] * 6,
        out_specs=[pl.BlockSpec(memory_space=pltpu.VMEM)] * 2,
        out_shape=[jax.ShapeDtypeStruct((39, *shard), BF16), jax.ShapeDtypeStruct((LOW, *shard), BF16)],
        scratch_shapes=[
            pltpu.VMEM((20, *shard), BF16), pltpu.VMEM((2, 1, 128), jnp.int32), pltpu.SMEM((1, 1), jnp.int32),
            pltpu.SemaphoreType.DMA((7,)),
        ],
        compiler_params=pltpu.CompilerParams(vmem_limit_bytes=56 * MIB),
    )(nf, edge_embed[0].reshape(8, 16, 128), sources, targets, edge_counts, jnp.transpose(cotangent[0], (1, 0, 2)))
    far = [swap(own, k) for k in (2, 4, 6)]

    forms = [((512, 896), BF16), ((1536, 768), BF16), ((1280, 768), BF16), ((128, 128), BF16), ((7, 128, 256), BF16)]
    *forms, sel0, sel1, sel2, selq, selr = call(
        kernel_weights,
        forms * 2 + [((896, 256), BF16), ((768, 256), BF16), ((640, 256), BF16), ((128, 256), BF16), ((32, 128), BF16)],
        [],
        6,
    )(pos_arr, jnp.swapaxes(w_zero, 1, 2), w_one, w_two, jnp.swapaxes(query, 1, 2), w_out)
    far = [lax.optimization_barrier((b, selr))[0] for b in far]
    pair = [swap(b, 1) for b in [own] + far]
    bufs = [own, pair[0], far[0], pair[1], far[1], pair[2], far[2], pair[3]]
    cfar = [swap(cot, k) for k in (2, 4, 6)]
    w0p, w1c, w2c, qp, wd = [[forms[m], forms[5 + m]] for m in range(5)]
    hf = jnp.asarray(HEAD_FIRST, BF16)
    hb = jnp.asarray(HEAD_BOTH, BF16)

    big = (EDGES, LOW * CH)
    agg0, s_mat, t_mat, tt, st, ee, v0, gate0, tq0, hs0, u0, h00 = call(
        kernel_first,
        [((NODES, 2048), BF16), ((EDGES, 128), BF16), ((EDGES, 128), BF16), ((128, EDGES), BF16),
         ((128, EDGES), BF16), ((EDGES, 128), BF16), ((EDGES, 2048), BF16), ((EDGES, 128), F32),
         ((EDGES, 128), F32), (big, BF16), (big, BF16), ((NODES, 128), BF16)],
        [((NODES, LOW * CH), BF16)],
        15,
        LIM_A,
    )(pos_arr, *bufs, w0p[0], w1c[0], w2c[0], radial, qp[0], hf)
    agg0p = swap(agg0, 1)
    (us0,) = plain_call(select_rows, [((5, EDGES, 256), BF16)], [], 8)(u0, sel0, sel1, sel2)
    agg0p, us0 = lax.optimization_barrier((agg0p, us0))
    grad_rows = 2048 + 288
    x1, s1, own1, snd1, agg1, h01, hs1, r1, v1, gate1, tq1, u1 = plain_call(
        kernel_second,
        [((NODES, LOW * CH), F32), ((NODES, 128), F32), ((16, 2048), F32), ((16, 2048), BF16),
         ((NODES, 2048), BF16), ((NODES, 128), BF16), (big, BF16), ((EDGES, 2304), BF16), ((EDGES, 2048), BF16),
         ((EDGES, 128), F32), ((EDGES, 128), F32), (big, BF16)],
        [((NODES, LOW * CH), BF16)],
        LIM_B,
    )(*bufs, agg0, agg0p, s_mat, t_mat, tt, ee, wd[0], w0p[1], w1c[1], w2c[1], radial, qp[1], hf)
    rcv1 = swap(snd1, 1)
    *cfar, agg1 = lax.optimization_barrier((*cfar, agg1))
    cpair = [swap(b, 1) for b in [cot] + cfar]
    cots = [cot, cpair[0], cfar[0], cpair[1], cfar[1], cpair[2], cfar[2], cpair[3]]
    dh, dy1, dv1, dr1, dqn1 = plain_call(
        kernel_back,
        [((NODES, LOW * CH), BF16), ((NODES, LOW * CH), BF16), ((EDGES, 2048), BF16), ((EDGES, 2304), BF16),
         ((NODES, 128), F32)],
        [((NODES, 2048), BF16), (big, BF16)],
        LIM_D,
    )(*cots, t_mat, tt, st, v1, gate1, tq1, hs1, r1, wd[1], w0p[1], w1c[1], w2c[1], qp[1], hb)
    dhp = swap(dh, 1)
    gm1, gs1 = call(
        kernel_grads,
        [((grad_rows, 128), F32), ((grad_rows, 128), BF16)],
        [((5, EDGES, 256), BF16)],
        14,
        LIM_E,
    )(pos_arr, dy1, agg1, h01, dqn1, ee, u1, dv1, dr1, sel0, sel1, sel2, selq, selr)
    gp1 = swap(gs1, 1)
    gm0, gs0 = call(
        kernel_third,
        [((grad_rows, 128), F32), ((grad_rows, 128), BF16)],
        [((NODES, LOW * CH), BF16), ((NODES, 2048), BF16), ((EDGES, 2048), BF16), ((EDGES, 2304), BF16),
         ((NODES, LOW * CH), F32)],
        30,
        LIM_C,
    )(pos_arr, *cots, x1, s1, dh, dhp, agg0, t_mat, tt, ee, v0, gate0, tq0, hs0, us0, h00,
      wd[0], w0p[0], w1c[0], w2c[0], hb, selq, selr)
    gp0 = swap(gs0, 1)
    gm1, gp1, own1, _ = lax.optimization_barrier((gm1, gp1, own1, gm0))
    (x2,) = plain_call(kernel_output, [((49, 16, 128), BF16)], [])(nf, x1, own1, rcv1, wd[1])
    result = jnp.transpose(x2, (1, 0, 2))[None]
    (late,) = plain_call(kernel_chunks, [((32, 56, 128), F32)], [((grad_rows, 128), F32)])(gm1, gp1)
    (packed,) = plain_call(
        kernel_pack, [((16, 224, 128), BF16)], [((grad_rows, 128), F32), ((32, 56, 128), F32)]
    )(gm0, gp0, late)
    planes = [[16 * h + a for a in range(16)] for h in range(2)]
    moved = lax.all_to_all(packed, "dp", split_axis=0, concat_axis=0, tiled=True, axis_index_groups=planes)
    half = (lax.axis_index("dp") // 16).astype(jnp.int32)[None]
    mine, theirs = call(kernel_plane, [((112, 128), F32), ((112, 128), BF16)], [], 2)(half, moved)
    theirs = lax.ppermute(theirs, "dp", [(i, i ^ 16) for i in range(32)])
    zero, one, two, rad, q, out = plain_call(
        kernel_finish,
        [((14, 2, 112), F32), ((2, 24, 96), F32), ((20, 2, 80), F32), ((2, 16, 72), F32),
         ((2, 2, 16), F32), ((2, 7, 2, 16), F32)],
        [((112, 128), F32)],
    )(mine, theirs)
    return (
        result,
        jnp.transpose(zero, (1, 2, 0)),
        jnp.transpose(one, (0, 2, 1)),
        jnp.transpose(two, (1, 2, 0)),
        rad,
        jnp.transpose(q, (0, 2, 1)),
        out,
    )


def solution(mesh):
    by_graph = P("dp", "graph")
    in_specs = (
        P("dp", "graph", None, None),
        P("dp", "graph", None),
        by_graph,
        by_graph,
        by_graph,
        P(),
        P(),
        P(),
        P(),
        P(),
        P(),
        P("dp", "graph", None, None),
    )
    out_specs = (
        P("dp", "graph", None, None),
        P(None, "graph", "dp"),
        P(None, "graph", "dp"),
        P(None, "graph", "dp"),
        P(None, "graph", "dp"),
        P(None, "graph", "dp"),
        P(None, None, "dp", "graph"),
    )
    return jax.shard_map(shards, mesh=mesh, in_specs=in_specs, out_specs=out_specs, check_vma=False)
```

```python
import functools

import jax
import jax.numpy as jnp
import numpy as np
from jax import lax
from jax.experimental import pallas as pl
from jax.experimental.pallas import tpu as pltpu
from jax.sharding import PartitionSpec as P

F32 = jnp.float32
BF16 = jnp.bfloat16
LOW = 29
CH = 128
NODES = 128
EDGES = 512
ENTRIES = 49 * 128
NORM_EPS = 1e-6
HEAD_SCALE = 8 ** -0.5
MIB = 1024 * 1024
LIM_A = 10
LIM_B = 10
LIM_C = 16
LIM_D = 12
LIM_E = 10

SEGMENTS = (
    [(0, 2, 0), (2, 2, 2), (4, 2, 4), (6, 1, 6)]
    + [(7, 2, 7), (9, 2, 9), (11, 2, 11)]
    + [(13, 2, 7), (15, 2, 9), (17, 2, 11)]
    + [(19, 2, 13), (21, 2, 15), (23, 1, 17)]
    + [(24, 2, 13), (26, 2, 15), (28, 1, 17)]
)
PAIRS = [(0, 1), (2, 3), (4, 5), (6, None), (1, 2), (3, 4), (5, 6)]
PAIR_OF = [0, 1, 2, 3, 4, 5, 6, 4, 5, 6, 1, 2, 3, 1, 2, 3]

HEAD_FIRST = np.zeros((256, 128), np.float32)
HEAD_BOTH = np.zeros((256, 128), np.float32)
for c_row in range(256):
    for c_col in range(128):
        same = (c_row % 64) // 8 == (c_col % 64) // 8
        HEAD_BOTH[c_row, c_col] = same
        HEAD_FIRST[c_row, c_col] = same and (c_row % 128) < 64


def dot(a, b):
    return lax.dot_general(a, b, (((1,), (0,)), ((), ())), preferred_element_type=F32)


def dot_nt(a, b):
    return lax.dot_general(a, b, (((1,), (1,)), ((), ())), preferred_element_type=F32)


def dot_tn(a, b):
    return lax.dot_general(a, b, (((0,), (0,)), ((), ())), preferred_element_type=F32)


def split_hi_lo(a):
    hi = a.astype(BF16)
    return hi, (a - hi.astype(F32)).astype(BF16)


def swap16(a):
    rows = []
    for b in range(a.shape[0] // 16):
        rows.append(a[16 * (b ^ 1) : 16 * (b ^ 1) + 16])
    return jnp.concatenate(rows, axis=0)


def forward_edges(h_ref, s_ref, t_ref, tt_ref, ee_ref, w0_ref, w1_ref, w2_ref, rad_ref, q_ref, hf_ref,
                  u_ref, hs_ref, r_ref, v_ref, gate_ref, tq_ref, agg_store):
    s_mat = s_ref[...]
    ee = ee_ref[...]
    r_vals = {}
    for c0, n, g0 in SEGMENTS:
        w = 128 * n
        if g0 not in r_vals:
            r_vals[g0] = dot(ee, rad_ref[:, 128 * g0 : 128 * g0 + w])
            if r_ref is not None:
                r_ref[:, 128 * g0 : 128 * g0 + w] = r_vals[g0].astype(BF16)
        hs = dot(s_mat, h_ref[:, 128 * c0 : 128 * c0 + w])
        hs_ref[:, 128 * c0 : 128 * c0 + w] = hs.astype(BF16)
        u_ref[:, 128 * c0 : 128 * c0 + w] = (hs * r_vals[g0]).astype(BF16)
    v0 = dot_nt(u_ref[:, 0:896], w0_ref[...])
    v_ref[:, 0:512] = v0.astype(BF16)
    q_hi, q_lo = split_hi_lo(dot_nt(h_ref[:, 0:128], q_ref[...]))
    t_mat = t_ref[...]
    tq = dot(t_mat, jnp.concatenate([q_hi, q_lo], axis=1))
    tq = tq[:, :128] + tq[:, 128:]
    tq_ref[...] = tq
    p_hi, p_lo = split_hi_lo(v0[:, :128] * tq)
    logits = dot(jnp.concatenate([p_hi, p_lo], axis=1), hf_ref[...]) * HEAD_SCALE
    gate = jax.nn.sigmoid(logits)
    gate_ref[...] = gate
    tt = tt_ref[...]

    def send(values, col):
        n = values.shape[1] // 128
        msg = jnp.concatenate(
            [(values[:, 128 * b : 128 * b + 128] * gate).astype(BF16) for b in range(n)], axis=1
        )
        agg_store(col, dot(tt, msg))

    send(v0[:, 0:256], 0)
    send(v0[:, 256:512], 256)
    v1 = dot(u_ref[:, 896:2432], w1_ref[...])
    v_ref[:, 512:1280] = v1.astype(BF16)
    for b in range(3):
        send(v1[:, 256 * b : 256 * b + 256], 512 + 256 * b)
    v2 = dot(u_ref[:, 2432:3712], w2_ref[...])
    v_ref[:, 1280:2048] = v2.astype(BF16)
    for b in range(3):
        send(v2[:, 256 * b : 256 * b + 256], 1280 + 256 * b)


def select_rows(pos_ref, u_ref, us_ref):
    for z in range(4):

        @pl.when(pos_ref[0] // 2 == z)
        def _():
            for part, (base, width) in enumerate(((0, 112), (896, 96), (1664, 96), (2432, 80), (3072, 80))):
                at = base + 2 * width * z
                blank = jnp.zeros((EDGES, 128 - width), BF16)
                us_ref[part, :, 0:128] = jnp.concatenate([u_ref[:, at : at + width], blank], axis=1)
                at = at + width
                us_ref[part, :, 128:256] = jnp.concatenate([u_ref[:, at : at + width], blank], axis=1)


def backward_edges(dagg_ref, t_ref, tt_ref, w0_ref, w1_ref, w2_ref, hb_ref, hs_ref, r_ref, v_ref, gate, tq,
                   dv_ref, dr_ref, w_ref):
    t_mat = t_ref[...]
    acc = jnp.zeros((EDGES, 128), F32)
    first = None
    for p in range(8):
        dm = dot(t_mat, dagg_ref[:, 256 * p : 256 * p + 256])
        for b in range(2):
            col = 256 * p + 128 * b
            part = dm[:, 128 * b : 128 * b + 128]
            acc = acc + part * v_ref[:, col : col + 128].astype(F32)
            scaled = part * gate
            if col == 0:
                first = scaled
            else:
                dv_ref[:, col : col + 128] = scaled.astype(BF16)
    a_hi, a_lo = split_hi_lo(acc)
    dalpha = dot(jnp.concatenate([a_hi, a_lo], axis=1), hb_ref[...])
    per = dalpha * gate * (1.0 - gate) * HEAD_SCALE
    dv_ref[:, 0:128] = (first + per * tq).astype(BF16)
    lane = lax.broadcasted_iota(jnp.int32, (EDGES, 128), 1)
    dq = jnp.where(lane < 64, per * v_ref[:, 0:128].astype(F32), 0.0).astype(BF16)
    dqn = dot(tt_ref[...], dq)

    def grads_of(col, width, weight_ref, row):
        if col == 0:
            return dot(dv_ref[:, col : col + width], weight_ref[:, row])
        return dot_nt(dv_ref[:, col : col + width], weight_ref[row, :])

    plans = (
        (SEGMENTS[0:4], None, 0, 512, w0_ref, 0),
        (SEGMENTS[4:7], SEGMENTS[7:10], 512, 768, w1_ref, 768),
        (SEGMENTS[10:13], SEGMENTS[13:16], 1280, 768, w2_ref, 640),
    )
    for plus, minus, col, width, weight_ref, half in plans:
        base = plus[0][0]
        for k, (c0, n, g0) in enumerate(plus):
            w = 128 * n
            at = 128 * (c0 - base)
            du = grads_of(col, width, weight_ref, pl.ds(at, w))
            dr = du * hs_ref[:, 128 * c0 : 128 * c0 + w].astype(F32)
            if w_ref is not None:
                rg = r_ref[:, 128 * g0 : 128 * g0 + w].astype(F32)
                w_ref[:, 128 * c0 : 128 * c0 + w] = (du * rg).astype(BF16)
            if minus is not None:
                m0 = minus[k][0]
                dum = grads_of(col, width, weight_ref, pl.ds(half + at, w))
                dr = dr + dum * hs_ref[:, 128 * m0 : 128 * m0 + w].astype(F32)
                if w_ref is not None:
                    w_ref[:, 128 * m0 : 128 * m0 + w] = (dum * rg).astype(BF16)
            dr_ref[:, 128 * g0 : 128 * g0 + w] = dr.astype(BF16)
    return dqn


def weight_grads(core, dy_ref, agg_ref, h0, dqn, ee_ref, selq_ref, selr_ref, us_ref, dv_ref, dr_ref, gm_ref, gs_ref):
    def put(row, val):
        n = val.shape[0]
        lo, hi = val[:, :128], val[:, 128:]
        gm_ref[row : row + n, :] = jnp.where(core == 0, lo, hi)
        gs_ref[row : row + n, :] = jnp.where(core == 0, hi, lo).astype(BF16)

    sums = [None] * 7
    for k, (c0, n, _) in enumerate(SEGMENTS):
        degs = PAIRS[PAIR_OF[k]]
        prod = dot_tn(agg_ref[:, 128 * k : 128 * k + 128], dy_ref[:, 128 * c0 : 128 * c0 + 128 * n])
        for m in range(n):
            piece = prod[64 * m : 64 * m + 64, 128 * m : 128 * m + 128]
            d = degs[m]
            sums[d] = piece if sums[d] is None else sums[d] + piece
    sums.append(dot_tn(dqn.astype(BF16), h0)[0:64])
    e_hi, e_lo = split_hi_lo(jnp.concatenate(sums, axis=0))
    selq = selq_ref[...]
    extra = dot(jnp.concatenate([e_hi, e_lo], axis=1), jnp.concatenate([selq, selq], axis=0))
    dv0t = dv_ref[:, 0:512].T
    put(0, dot(dv0t, us_ref[0]) + extra)
    up, um = us_ref[1], us_ref[2]
    dpt = dv_ref[:, 512:896].T
    dmt = dv_ref[:, 896:1280].T
    put(512, dot(dpt, up) + dot(dmt, um))
    put(896, dot(dmt, up) - dot(dpt, um))
    up, um = us_ref[3], us_ref[4]
    dpt = dv_ref[:, 1280:1664].T
    dmt = dv_ref[:, 1664:2048].T
    put(1280, dot(dpt, up) + dot(dmt, um))
    put(1664, dot(dmt, up) - dot(dpt, um))
    ees = dot_nt(selr_ref[...], ee_ref[...]).astype(BF16)
    for p in range(9):
        pr = dot(ees, dr_ref[:, 256 * p : 256 * p + 256])
        mine = jnp.where(core == 0, pr[0:16], pr[16:32])
        theirs = jnp.where(core == 0, pr[16:32], pr[0:16]).astype(BF16)
        for b in range(2):
            row = 2048 + 16 * (2 * p + b)
            gm_ref[row : row + 16, :] = mine[:, 128 * b : 128 * b + 128]
            gs_ref[row : row + 16, :] = theirs[:, 128 * b : 128 * b + 128]


def node_block(bufs, i):
    return jnp.concatenate([b[i] for b in bufs], axis=0)


def kernel_first(pos_ref, b0, b1, b2, b3, b4, b5, b6, b7, w0_ref, w1_ref, w2_ref, rad_ref, q_ref, hf_ref,
                 agg_ref, s_ref, t_ref, tt_ref, st_ref, ee_ref, v_ref, gate_ref, tq_ref, hs_ref, u_ref, h0_ref,
                 h_ref):
    bufs = [b0, b1, b2, b3, b4, b5, b6, b7]
    mask = 16 * pos_ref[0]
    iota = lax.broadcasted_iota(jnp.int32, (NODES, 128), 0)
    for k in range(4):
        buf = bufs[2 * k]
        ids = buf[38].astype(F32)
        src = ids[0:1].astype(jnp.int32) ^ mask
        tgt = ids[1:2].astype(jnp.int32) ^ mask
        s_hot = jnp.where(iota == src, 1.0, 0.0)
        t_hot = jnp.where(iota == tgt, 1.0, 0.0) * ids[2:3]
        st_ref[:, 128 * k : 128 * k + 128] = s_hot.astype(BF16)
        tt_ref[:, 128 * k : 128 * k + 128] = t_hot.astype(BF16)
        s_ref[128 * k : 128 * k + 128, :] = s_hot.T.astype(BF16)
        t_ref[128 * k : 128 * k + 128, :] = t_hot.T.astype(BF16)
        for m in range(8):
            ee_ref[128 * k + 16 * m : 128 * k + 16 * m + 16, :] = buf[30 + m]
    total = jnp.zeros((NODES, CH), F32)
    for i in range(LOW):
        x = node_block(bufs, i).astype(F32)
        total = total + x * x
    total = total + node_block(bufs, LOW).astype(F32)
    scale = lax.rsqrt(jnp.sum(total, axis=1, keepdims=True) * (1.0 / ENTRIES) + NORM_EPS)
    for i in range(LOW):
        h_ref[:, 128 * i : 128 * i + 128] = (node_block(bufs, i).astype(F32) * scale).astype(BF16)
    h0_ref[...] = h_ref[:, 0:128]

    def agg_store(col, val):
        agg_ref[:, col : col + 256] = val.astype(BF16)

    forward_edges(h_ref, s_ref, t_ref, tt_ref, ee_ref, w0_ref, w1_ref, w2_ref, rad_ref.at[0], q_ref, hf_ref,
                  u_ref, hs_ref, None, v_ref, gate_ref, tq_ref, agg_store)


def kernel_second(b0, b1, b2, b3, b4, b5, b6, b7, agg0_ref, agg0p_ref, s_ref, t_ref, tt_ref, ee_ref,
                  wd0_ref, w0_ref, w1_ref, w2_ref, rad_ref, q_ref, hf_ref,
                  x1_ref, s1_ref, own_ref, snd_ref, agg1_ref, h0_ref, hs_ref, r_ref, v_ref, gate_ref, tq_ref, u_ref,
                  h_ref):
    bufs = [b0, b1, b2, b3, b4, b5, b6, b7]
    total = node_block(bufs, LOW).astype(F32)
    for k, (c0, n, _) in enumerate(SEGMENTS):
        agg = agg0_ref[:, 128 * k : 128 * k + 128].astype(F32)
        agg = agg + swap16(agg0p_ref[:, 128 * k : 128 * k + 128]).astype(F32)
        out = dot(agg.astype(BF16), wd0_ref[PAIR_OF[k]])
        for m in range(n):
            x = node_block(bufs, c0 + m).astype(F32) + out[:, 128 * m : 128 * m + 128]
            x1_ref[:, 128 * (c0 + m) : 128 * (c0 + m) + 128] = x
            total = total + x * x
    scale = lax.rsqrt(jnp.sum(total, axis=1, keepdims=True) * (1.0 / ENTRIES) + NORM_EPS)
    s1_ref[...] = jnp.broadcast_to(scale, (NODES, 128))
    for i in range(LOW):
        h_ref[:, 128 * i : 128 * i + 128] = (x1_ref[:, 128 * i : 128 * i + 128] * scale).astype(BF16)
    h0_ref[...] = h_ref[:, 0:128]

    def agg_store(col, val):
        agg1_ref[:, col : col + 256] = val.astype(BF16)
        own_ref[:, col : col + 256] = val[0:16]
        snd_ref[:, col : col + 256] = val[16:32].astype(BF16)

    forward_edges(h_ref, s_ref, t_ref, tt_ref, ee_ref, w0_ref, w1_ref, w2_ref, rad_ref.at[1], q_ref, hf_ref,
                  u_ref, hs_ref, r_ref, v_ref, gate_ref, tq_ref, agg_store)


def kernel_back(c0_, c1_, c2_, c3_, c4_, c5_, c6_, c7_, t_ref, tt_ref, st_ref, v_ref, gate_ref, tq_ref, hs_ref, r_ref,
                wd1_ref, w0_ref, w1_ref, w2_ref, q_ref, hb_ref,
                dh_ref, dy_ref, dv_ref, dr_ref, dqn_ref,
                dagg_ref, w_ref):
    cots = [c0_, c1_, c2_, c3_, c4_, c5_, c6_, c7_]
    for i in range(LOW):
        dy_ref[:, 128 * i : 128 * i + 128] = node_block(cots, i)
    for k, (c0, n, _) in enumerate(SEGMENTS):
        w = 128 * n
        dagg_ref[:, 128 * k : 128 * k + 128] = dot_nt(
            dy_ref[:, 128 * c0 : 128 * c0 + w], wd1_ref[PAIR_OF[k], :, 0:w]
        ).astype(BF16)
    dqn = backward_edges(dagg_ref, t_ref, tt_ref, w0_ref, w1_ref, w2_ref, hb_ref, hs_ref, r_ref, v_ref,
                         gate_ref[...], tq_ref[...], dv_ref, dr_ref, w_ref)
    dqn_ref[...] = dqn
    st = st_ref[...]
    d_hi, d_lo = split_hi_lo(dqn)
    back = dot(jnp.concatenate([d_hi, d_lo], axis=1), jnp.concatenate([q_ref[...], q_ref[...]], axis=0))
    for c0, n, _ in SEGMENTS:
        w = 128 * n
        val = dot(st, w_ref[:, 128 * c0 : 128 * c0 + w])
        if c0 == 0:
            val = val + jnp.concatenate([back, jnp.zeros((NODES, 128), F32)], axis=1)
        dh_ref[:, 128 * c0 : 128 * c0 + w] = val.astype(BF16)


def kernel_grads(pos_ref, dy_ref, agg_ref, h0_ref, dqn_ref, ee_ref, us_ref, dv_ref, dr_ref,
                 selq_ref, selr_ref, gm_ref, gs_ref):
    weight_grads(pos_ref[0] & 1, dy_ref, agg_ref, h0_ref[...], dqn_ref[...], ee_ref, selq_ref, selr_ref,
                 us_ref, dv_ref, dr_ref, gm_ref, gs_ref)


def kernel_third(pos_ref, c0_, c1_, c2_, c3_, c4_, c5_, c6_, c7_, x1_ref, s1_ref, dh_ref, dhp_ref,
                 agg0_ref, t_ref, tt_ref, ee_ref, v_ref, gate_ref, tq_ref, hs_ref, us_ref, h0_ref,
                 wd0_ref, w0_ref, w1_ref, w2_ref, hb_ref, selq_ref, selr_ref,
                 gm_ref, gs_ref,
                 dy_ref, dagg_ref, dv_ref, dr_ref, full_ref):
    cots = [c0_, c1_, c2_, c3_, c4_, c5_, c6_, c7_]
    inner = jnp.zeros((NODES, 128), F32)
    for i in range(LOW):
        cols = pl.ds(128 * i, 128)
        dh = dh_ref[:, cols].astype(F32) + swap16(dhp_ref[:, cols]).astype(F32)
        full_ref[:, cols] = dh
        inner = inner + dh * x1_ref[:, cols]
    s1 = s1_ref[...]
    coef = jnp.sum(inner, axis=1, keepdims=True) * (1.0 / ENTRIES) * (s1 * s1 * s1)
    for i in range(LOW):
        cols = pl.ds(128 * i, 128)
        dx = node_block(cots, i).astype(F32) + s1 * full_ref[:, cols] - x1_ref[:, cols] * coef
        dy_ref[:, cols] = dx.astype(BF16)
    for k, (c0, n, _) in enumerate(SEGMENTS):
        w = 128 * n
        dagg_ref[:, 128 * k : 128 * k + 128] = dot_nt(
            dy_ref[:, 128 * c0 : 128 * c0 + w], wd0_ref[PAIR_OF[k], :, 0:w]
        ).astype(BF16)
    dqn = backward_edges(dagg_ref, t_ref, tt_ref, w0_ref, w1_ref, w2_ref, hb_ref, hs_ref, None, v_ref,
                         gate_ref[...], tq_ref[...], dv_ref, dr_ref, None)
    weight_grads(pos_ref[0] & 1, dy_ref, agg0_ref, h0_ref[...], dqn, ee_ref, selq_ref, selr_ref,
                 us_ref, dv_ref, dr_ref, gm_ref, gs_ref)


def kernel_output(nf_ref, x1_ref, own_ref, rcv_ref, wd1_ref, x2_ref):
    for k, (c0, n, _) in enumerate(SEGMENTS):
        w = 128 * n
        agg = own_ref[:, 128 * k : 128 * k + 128] + rcv_ref[:, 128 * k : 128 * k + 128].astype(F32)
        out = dot(agg.astype(BF16), wd1_ref[PAIR_OF[k], :, 0:w])
        out = (x1_ref[0:16, 128 * c0 : 128 * c0 + w] + out).astype(BF16)
        for m in range(n):
            x2_ref[c0 + m] = out[:, 128 * m : 128 * m + 128]
    x2_ref[LOW:] = nf_ref[LOW:]


def kernel_chunks(mine, other, chunk_ref, g_ref):
    lane14 = lax.broadcasted_iota(jnp.int32, (16, 128), 1)
    g_ref[...] = mine[...] + other[...].astype(F32)
    for d in range(32):
        chunk_ref[d, 0:14, :] = g_ref[14 * d : 14 * d + 14, :]
        chunk_ref[d, 14:38, :] = g_ref[512 + 24 * d : 536 + 24 * d, :]
        row = 1280 + 20 * d + (64 if d >= 16 else 0)
        chunk_ref[d, 38:56, :] = g_ref[row : row + 18, :]
        last = g_ref[row + 18 : row + 20, :]
        for k in range(3):
            chunk_ref[d, 32 + 2 * k : 34 + 2 * k, 96:128] = pltpu.roll(last, 96 - 32 * k, 1)[:, 96:128]
        for q in range(7):
            chunk_ref[d, 2 * q : 2 * q + 2, 112:128] = g_ref[64 * q + 2 * d : 64 * q + 2 * d + 2, 112:128]
        chunk_ref[d, 14:16, 112:128] = g_ref[448 + 2 * d : 450 + 2 * d, 112:128]
        for start, width, at, to in ((72 * d, 48, 80, 38), (72 * d + 48, 24, 96, 16)):
            blk, off = start // 128, start % 128
            shift = (at - off) % 128
            left = g_ref[2048 + 16 * blk : 2064 + 16 * blk, :]
            win = pltpu.roll(left, shift, 1) if shift else left
            if off + width > 128:
                right = g_ref[2064 + 16 * blk : 2080 + 16 * blk, :]
                right = pltpu.roll(right, shift, 1) if shift else right
                win = jnp.where(lane14 < at + 128 - off, win, right)
            chunk_ref[d, to : to + 16, at : at + width] = win[:, at : at + width]


def kernel_pack(mine, other, late_ref, out_ref, g_ref, chunk_ref):
    kernel_chunks(mine, other, chunk_ref, g_ref)
    for d in range(32):
        both = jnp.concatenate([chunk_ref[d], late_ref[d]], axis=0)
        out_ref[d % 16, 112 * (d // 16) : 112 * (d // 16) + 112, :] = both.astype(BF16)


def kernel_plane(half_ref, in_ref, own_ref, snd_ref):
    for h in range(2):
        acc = in_ref[0, 112 * h : 112 * h + 112].astype(F32)
        for d in range(1, 16):
            acc = acc + in_ref[d, 112 * h : 112 * h + 112].astype(F32)

        @pl.when(half_ref[0] == h)
        def _():
            own_ref[...] = acc

        @pl.when(half_ref[0] != h)
        def _():
            snd_ref[...] = acc.astype(BF16)


def kernel_finish(in_ref, rcv_ref, zero_ref, one_ref, two_ref, rad_ref, q_ref, out_ref, acc_ref):
    acc_ref[...] = in_ref[...] + rcv_ref[...].astype(F32)
    lane = lax.broadcasted_iota(jnp.int32, (16, 128), 1)
    for layer in range(2):
        b = 56 * layer
        for r in range(14):
            zero_ref[r, layer : layer + 1, :] = acc_ref[b + r : b + r + 1, 0:112]
        one_ref[layer] = acc_ref[b + 14 : b + 38, 0:96]
        for r in range(18):
            two_ref[r, layer : layer + 1, :] = acc_ref[b + 38 + r : b + 39 + r, 0:80]
        first, second, third = [
            pltpu.roll(acc_ref[b + 32 + 2 * k : b + 34 + 2 * k, :], 32 + 32 * k, 1) for k in range(3)
        ]
        lane2 = lax.broadcasted_iota(jnp.int32, (2, 128), 1)
        last = jnp.where(lane2 < 32, first, jnp.where(lane2 < 64, second, third))
        for r in range(2):
            two_ref[18 + r, layer : layer + 1, :] = last[r : r + 1, 0:80]
        q_ref[layer] = pltpu.roll(acc_ref[b + 14 : b + 16, :], 16, 1)[:, 0:16]
        low = pltpu.roll(acc_ref[b + 38 : b + 54, :], 48, 1)
        high = pltpu.roll(acc_ref[b + 16 : b + 32, :], 80, 1)
        rad_ref[layer] = jnp.where(lane < 48, low, high)[:, 0:72]
        tail = pltpu.roll(acc_ref[b : b + 16, :], 16, 1)
        for q in range(7):
            out_ref[layer, q] = tail[2 * q : 2 * q + 2, 0:16]


def kernel_load(nf_ref, ee_ref, src_ref, tgt_ref, count_ref, cot_ref, own_ref, low_cot_ref,
                tail_ref, ids_ref, count_smem, sems):
    copies = [
        pltpu.make_async_copy(nf_ref.at[pl.ds(LOW, 20)], tail_ref, sems.at[0]),
        pltpu.make_async_copy(src_ref, ids_ref.at[0], sems.at[1]),
        pltpu.make_async_copy(tgt_ref, ids_ref.at[1], sems.at[2]),
        pltpu.make_async_copy(count_ref, count_smem, sems.at[3]),
        pltpu.make_async_copy(nf_ref.at[pl.ds(0, LOW)], own_ref.at[pl.ds(0, LOW)], sems.at[4]),
        pltpu.make_async_copy(ee_ref, own_ref.at[pl.ds(30, 8)], sems.at[5]),
        pltpu.make_async_copy(cot_ref.at[pl.ds(0, LOW)], low_cot_ref, sems.at[6]),
    ]
    for copy in copies:
        copy.start()
    copies[0].wait()
    tail = jnp.zeros((16, 128), F32)
    for i in range(20):
        x = tail_ref[i].astype(F32)
        tail = tail + x * x
    tail = jnp.broadcast_to(jnp.sum(tail, axis=1, keepdims=True), (16, 128))
    lane = lax.broadcasted_iota(jnp.int32, (16, 128), 1)
    hi = tail.astype(BF16).astype(F32)
    mid = (tail - hi).astype(BF16).astype(F32)
    pieces = jnp.where(lane == 0, hi, jnp.where(lane == 1, mid, jnp.where(lane == 2, tail - hi - mid, 0.0)))
    own_ref[LOW] = pieces.astype(BF16)
    for copy in copies[1:4]:
        copy.wait()
    row = lax.broadcasted_iota(jnp.int32, (16, 128), 0)
    live = jnp.where(lane < count_smem[0, 0], 1.0, 0.0)
    src = jnp.broadcast_to(ids_ref[0], (16, 128)).astype(F32)
    tgt = jnp.broadcast_to(ids_ref[1], (16, 128)).astype(F32)
    ids = jnp.where(row == 0, src, jnp.where(row == 1, tgt, jnp.where(row == 2, live, 0.0)))
    own_ref[38] = ids.astype(BF16)
    for copy in copies[4:]:
        copy.wait()


def kernel_weights(pos_ref, zero_ref, one_ref, two_ref, query_ref, out_ref, *outs):
    selq_ref, selr_ref = outs[10:]
    z_lo = pos_ref[0] // 2
    for k in range(2):
        w0_ref, w1_ref, w2_ref, q_ref, wd_ref = outs[5 * k : 5 * k + 5]
        w0_ref[0:448, :] = zero_ref[k]
        w0_ref[448:512, :] = jnp.zeros((64, 896), BF16)
        a, b = one_ref[k, :, 0:384], one_ref[k, :, 384:768]
        w1_ref[0:768, 0:384] = a
        w1_ref[0:768, 384:768] = b
        w1_ref[768:1536, 0:384] = -b
        w1_ref[768:1536, 384:768] = a
        blank = jnp.zeros((640, 64), BF16)
        a = jnp.concatenate([two_ref[k, :, 0:320], blank], axis=1)
        b = jnp.concatenate([two_ref[k, :, 320:640], blank], axis=1)
        w2_ref[0:640, 0:384] = a
        w2_ref[0:640, 384:768] = b
        w2_ref[640:1280, 0:384] = -b
        w2_ref[640:1280, 384:768] = a
        q_ref[0:64, :] = query_ref[k]
        q_ref[64:128, :] = jnp.zeros((64, 128), BF16)
        none = jnp.zeros((64, 128), BF16)
        for p, (d, e) in enumerate(PAIRS):
            wd_ref[p, 0:64, 0:128] = out_ref[k, d]
            wd_ref[p, 0:64, 128:256] = none
            wd_ref[p, 64:128, 0:128] = none
            wd_ref[p, 64:128, 128:256] = none if e is None else out_ref[k, e]

    def select(rows, width, first_lane, scale):
        k = lax.broadcasted_iota(jnp.int32, (rows, 128), 0)
        m = lax.broadcasted_iota(jnp.int32, (rows, 128), 1) - first_lane
        live = (m >= 0) & (m < width)
        lo = jnp.where(live & (k == scale * z_lo + m), 1.0, 0.0)
        hi = jnp.where(live & (k == scale * z_lo + width + m), 1.0, 0.0)
        return jnp.concatenate([lo, hi], axis=1).astype(BF16)

    selq = select(128, 16, 112, 32)
    selq_ref[...] = selq
    rows = lax.broadcasted_iota(jnp.int32, (32, 128), 0)
    cols = lax.broadcasted_iota(jnp.int32, (32, 128), 1)
    selr_ref[...] = jnp.where(cols == 32 * z_lo + rows, 1.0, 0.0).astype(BF16)


def call(body, outs, scratch, n_in, limit=16, cost=None):
    return pl.pallas_call(
        body,
        in_specs=[pl.BlockSpec(memory_space=pltpu.SMEM)] + [pl.BlockSpec(memory_space=pltpu.VMEM)] * (n_in - 1),
        out_specs=[pl.BlockSpec(memory_space=pltpu.VMEM)] * len(outs),
        out_shape=[jax.ShapeDtypeStruct(s, t) for s, t in outs],
        scratch_shapes=[pltpu.VMEM(s, t) for s, t in scratch],
        compiler_params=pltpu.CompilerParams(vmem_limit_bytes=limit * MIB),
        cost_estimate=cost,
    )


def plain_call(body, outs, scratch, limit=16):
    return pl.pallas_call(
        body,
        out_shape=[jax.ShapeDtypeStruct(s, t) for s, t in outs],
        scratch_shapes=[pltpu.VMEM(s, t) for s, t in scratch],
        compiler_params=pltpu.CompilerParams(vmem_limit_bytes=limit * MIB),
    )


def swap(x, bits):
    return lax.ppermute(x, "graph", [(i, i ^ bits) for i in range(8)])


def shards(node_features, edge_embed, sources, targets, edge_counts, w_zero, w_one, w_two, radial, query, w_out, cotangent):
    pos_arr = lax.axis_index("graph").astype(jnp.int32)[None]
    nf = jnp.transpose(node_features[0], (1, 0, 2))
    shard = (16, 128)
    own, cot = pl.pallas_call(
        kernel_load,
        in_specs=[pl.BlockSpec(memory_space=pltpu.HBM)] * 6,
        out_specs=[pl.BlockSpec(memory_space=pltpu.VMEM)] * 2,
        out_shape=[jax.ShapeDtypeStruct((39, *shard), BF16), jax.ShapeDtypeStruct((LOW, *shard), BF16)],
        scratch_shapes=[
            pltpu.VMEM((20, *shard), BF16), pltpu.VMEM((2, 1, 128), jnp.int32), pltpu.SMEM((1, 1), jnp.int32),
            pltpu.SemaphoreType.DMA((7,)),
        ],
        compiler_params=pltpu.CompilerParams(vmem_limit_bytes=56 * MIB),
    )(nf, edge_embed[0].reshape(8, 16, 128), sources, targets, edge_counts, jnp.transpose(cotangent[0], (1, 0, 2)))
    far = [swap(own, k) for k in (2, 4, 6)]

    forms = [((512, 896), BF16), ((1536, 768), BF16), ((1280, 768), BF16), ((128, 128), BF16), ((7, 128, 256), BF16)]
    *forms, selq, selr = call(
        kernel_weights,
        forms * 2 + [((128, 256), BF16), ((32, 128), BF16)],
        [],
        6,
    )(pos_arr, jnp.swapaxes(w_zero, 1, 2), w_one, w_two, jnp.swapaxes(query, 1, 2), w_out)
    far = [lax.optimization_barrier((b, selr))[0] for b in far]
    pair = [swap(b, 1) for b in [own] + far]
    bufs = [own, pair[0], far[0], pair[1], far[1], pair[2], far[2], pair[3]]
    cfar = [swap(cot, k) for k in (2, 4, 6)]
    w0p, w1c, w2c, qp, wd = [[forms[m], forms[5 + m]] for m in range(5)]
    hf = jnp.asarray(HEAD_FIRST, BF16)
    hb = jnp.asarray(HEAD_BOTH, BF16)

    big = (EDGES, LOW * CH)
    agg0, s_mat, t_mat, tt, st, ee, v0, gate0, tq0, hs0, u0, h00 = call(
        kernel_first,
        [((NODES, 2048), BF16), ((EDGES, 128), BF16), ((EDGES, 128), BF16), ((128, EDGES), BF16),
         ((128, EDGES), BF16), ((EDGES, 128), BF16), ((EDGES, 2048), BF16), ((EDGES, 128), F32),
         ((EDGES, 128), F32), (big, BF16), (big, BF16), ((NODES, 128), BF16)],
        [((NODES, LOW * CH), BF16)],
        15,
        LIM_A,
    )(pos_arr, *bufs, w0p[0], w1c[0], w2c[0], radial, qp[0], hf)
    agg0p = swap(agg0, 1)
    (us0,) = call(select_rows, [((5, EDGES, 256), BF16)], [], 2, 8)(pos_arr, u0)
    agg0p, us0 = lax.optimization_barrier((agg0p, us0))
    grad_rows = 2048 + 288
    x1, s1, own1, snd1, agg1, h01, hs1, r1, v1, gate1, tq1, u1 = plain_call(
        kernel_second,
        [((NODES, LOW * CH), F32), ((NODES, 128), F32), ((16, 2048), F32), ((16, 2048), BF16),
         ((NODES, 2048), BF16), ((NODES, 128), BF16), (big, BF16), ((EDGES, 2304), BF16), ((EDGES, 2048), BF16),
         ((EDGES, 128), F32), ((EDGES, 128), F32), (big, BF16)],
        [((NODES, LOW * CH), BF16)],
        LIM_B,
    )(*bufs, agg0, agg0p, s_mat, t_mat, tt, ee, wd[0], w0p[1], w1c[1], w2c[1], radial, qp[1], hf)
    rcv1 = swap(snd1, 1)
    *cfar, agg1 = lax.optimization_barrier((*cfar, agg1))
    cpair = [swap(b, 1) for b in [cot] + cfar]
    cots = [cot, cpair[0], cfar[0], cpair[1], cfar[1], cpair[2], cfar[2], cpair[3]]
    (us1,) = call(select_rows, [((5, EDGES, 256), BF16)], [], 2, 8)(pos_arr, u1)
    cpair[2], us1 = lax.optimization_barrier((cpair[2], us1))
    cots[5] = cpair[2]
    dh, dy1, dv1, dr1, dqn1 = plain_call(
        kernel_back,
        [((NODES, LOW * CH), BF16), ((NODES, LOW * CH), BF16), ((EDGES, 2048), BF16), ((EDGES, 2304), BF16),
         ((NODES, 128), F32)],
        [((NODES, 2048), BF16), (big, BF16)],
        LIM_D,
    )(*cots, t_mat, tt, st, v1, gate1, tq1, hs1, r1, wd[1], w0p[1], w1c[1], w2c[1], qp[1], hb)
    dhp = swap(dh, 1)
    gm1, gs1 = call(
        kernel_grads,
        [((grad_rows, 128), F32), ((grad_rows, 128), BF16)],
        [],
        11,
        LIM_E,
    )(pos_arr, dy1, agg1, h01, dqn1, ee, us1, dv1, dr1, selq, selr)
    gp1 = swap(gs1, 1)
    gm0, gs0 = call(
        kernel_third,
        [((grad_rows, 128), F32), ((grad_rows, 128), BF16)],
        [((NODES, LOW * CH), BF16), ((NODES, 2048), BF16), ((EDGES, 2048), BF16), ((EDGES, 2304), BF16),
         ((NODES, LOW * CH), F32)],
        30,
        LIM_C,
    )(pos_arr, *cots, x1, s1, dh, dhp, agg0, t_mat, tt, ee, v0, gate0, tq0, hs0, us0, h00,
      wd[0], w0p[0], w1c[0], w2c[0], hb, selq, selr)
    gp0 = swap(gs0, 1)
    gm1, gp1, own1, _ = lax.optimization_barrier((gm1, gp1, own1, gm0))
    (x2,) = plain_call(kernel_output, [((49, 16, 128), BF16)], [])(nf, x1, own1, rcv1, wd[1])
    result = jnp.transpose(x2, (1, 0, 2))[None]
    (late,) = plain_call(kernel_chunks, [((32, 56, 128), F32)], [((grad_rows, 128), F32)])(gm1, gp1)
    (packed,) = plain_call(
        kernel_pack, [((16, 224, 128), BF16)], [((grad_rows, 128), F32), ((32, 56, 128), F32)]
    )(gm0, gp0, late)
    planes = [[16 * h + a for a in range(16)] for h in range(2)]
    moved = lax.all_to_all(packed, "dp", split_axis=0, concat_axis=0, tiled=True, axis_index_groups=planes)
    half = (lax.axis_index("dp") // 16).astype(jnp.int32)[None]
    mine, theirs = call(kernel_plane, [((112, 128), F32), ((112, 128), BF16)], [], 2)(half, moved)
    theirs = lax.ppermute(theirs, "dp", [(i, i ^ 16) for i in range(32)])
    zero, one, two, rad, q, out = plain_call(
        kernel_finish,
        [((14, 2, 112), F32), ((2, 24, 96), F32), ((20, 2, 80), F32), ((2, 16, 72), F32),
         ((2, 2, 16), F32), ((2, 7, 2, 16), F32)],
        [((112, 128), F32)],
    )(mine, theirs)
    return (
        result,
        jnp.transpose(zero, (1, 2, 0)),
        jnp.transpose(one, (0, 2, 1)),
        jnp.transpose(two, (1, 2, 0)),
        rad,
        jnp.transpose(q, (0, 2, 1)),
        out,
    )


def solution(mesh):
    by_graph = P("dp", "graph")
    in_specs = (
        P("dp", "graph", None, None),
        P("dp", "graph", None),
        by_graph,
        by_graph,
        by_graph,
        P(),
        P(),
        P(),
        P(),
        P(),
        P(),
        P("dp", "graph", None, None),
    )
    out_specs = (
        P("dp", "graph", None, None),
        P(None, "graph", "dp"),
        P(None, "graph", "dp"),
        P(None, "graph", "dp"),
        P(None, "graph", "dp"),
        P(None, "graph", "dp"),
        P(None, None, "dp", "graph"),
    )
    return jax.shard_map(shards, mesh=mesh, in_specs=in_specs, out_specs=out_specs, check_vma=False)
```

```python
import functools

import jax
import jax.numpy as jnp
import numpy as np
from jax import lax
from jax.experimental import pallas as pl
from jax.experimental.pallas import tpu as pltpu
from jax.sharding import PartitionSpec as P

F32 = jnp.float32
BF16 = jnp.bfloat16
LOW = 29
CH = 128
NODES = 128
EDGES = 512
ENTRIES = 49 * 128
NORM_EPS = 1e-6
HEAD_SCALE = 8 ** -0.5
MIB = 1024 * 1024
LIM_A = 10
LIM_B = 10
LIM_C = 16
LIM_D = 12
LIM_E = 10

SEGMENTS = (
    [(0, 2, 0), (2, 2, 2), (4, 2, 4), (6, 1, 6)]
    + [(7, 2, 7), (9, 2, 9), (11, 2, 11)]
    + [(13, 2, 7), (15, 2, 9), (17, 2, 11)]
    + [(19, 2, 13), (21, 2, 15), (23, 1, 17)]
    + [(24, 2, 13), (26, 2, 15), (28, 1, 17)]
)
PAIRS = [(0, 1), (2, 3), (4, 5), (6, None), (1, 2), (3, 4), (5, 6)]
PAIR_OF = [0, 1, 2, 3, 4, 5, 6, 4, 5, 6, 1, 2, 3, 1, 2, 3]

HEAD_FIRST = np.zeros((256, 128), np.float32)
HEAD_BOTH = np.zeros((256, 128), np.float32)
for c_row in range(256):
    for c_col in range(128):
        same = (c_row % 64) // 8 == (c_col % 64) // 8
        HEAD_BOTH[c_row, c_col] = same
        HEAD_FIRST[c_row, c_col] = same and (c_row % 128) < 64


def dot(a, b):
    return lax.dot_general(a, b, (((1,), (0,)), ((), ())), preferred_element_type=F32)


def dot_nt(a, b):
    return lax.dot_general(a, b, (((1,), (1,)), ((), ())), preferred_element_type=F32)


def dot_tn(a, b):
    return lax.dot_general(a, b, (((0,), (0,)), ((), ())), preferred_element_type=F32)


def split_hi_lo(a):
    hi = a.astype(BF16)
    return hi, (a - hi.astype(F32)).astype(BF16)


def swap16(a):
    rows = []
    for b in range(a.shape[0] // 16):
        rows.append(a[16 * (b ^ 1) : 16 * (b ^ 1) + 16])
    return jnp.concatenate(rows, axis=0)


def forward_edges(h_ref, s_ref, t_ref, tt_ref, ee_ref, w0_ref, w1_ref, w2_ref, rad_ref, q_ref, hf_ref,
                  u_ref, hs_ref, r_ref, v_ref, gate_ref, tq_ref, agg_store):
    s_mat = s_ref[...]
    ee = ee_ref[...]
    r_vals = {}
    for c0, n, g0 in SEGMENTS:
        w = 128 * n
        if g0 not in r_vals:
            r_vals[g0] = dot(ee, rad_ref[:, 128 * g0 : 128 * g0 + w])
            if r_ref is not None:
                r_ref[:, 128 * g0 : 128 * g0 + w] = r_vals[g0].astype(BF16)
        hs = dot(s_mat, h_ref[:, 128 * c0 : 128 * c0 + w])
        hs_ref[:, 128 * c0 : 128 * c0 + w] = hs.astype(BF16)
        u_ref[:, 128 * c0 : 128 * c0 + w] = (hs * r_vals[g0]).astype(BF16)
    v0 = dot_nt(u_ref[:, 0:896], w0_ref[...])
    v_ref[:, 0:512] = v0.astype(BF16)
    q_hi, q_lo = split_hi_lo(dot_nt(h_ref[:, 0:128], q_ref[...]))
    t_mat = t_ref[...]
    tq = dot(t_mat, jnp.concatenate([q_hi, q_lo], axis=1))
    tq = tq[:, :128] + tq[:, 128:]
    tq_ref[...] = tq
    p_hi, p_lo = split_hi_lo(v0[:, :128] * tq)
    logits = dot(jnp.concatenate([p_hi, p_lo], axis=1), hf_ref[...]) * HEAD_SCALE
    gate = jax.nn.sigmoid(logits)
    gate_ref[...] = gate
    tt = tt_ref[...]

    def send(values, col):
        n = values.shape[1] // 128
        msg = jnp.concatenate(
            [(values[:, 128 * b : 128 * b + 128] * gate).astype(BF16) for b in range(n)], axis=1
        )
        agg_store(col, dot(tt, msg))

    send(v0[:, 0:256], 0)
    send(v0[:, 256:512], 256)
    v1 = dot(u_ref[:, 896:2432], w1_ref[...])
    v_ref[:, 512:1280] = v1.astype(BF16)
    for b in range(3):
        send(v1[:, 256 * b : 256 * b + 256], 512 + 256 * b)
    v2 = dot(u_ref[:, 2432:3712], w2_ref[...])
    v_ref[:, 1280:2048] = v2.astype(BF16)
    for b in range(3):
        send(v2[:, 256 * b : 256 * b + 256], 1280 + 256 * b)


def select_rows(pos_ref, u_ref, us_ref):
    for z in range(4):

        @pl.when(pos_ref[0] // 2 == z)
        def _():
            for part, (base, width) in enumerate(((0, 112), (896, 96), (1664, 96), (2432, 80), (3072, 80))):
                at = base + 2 * width * z
                blank = jnp.zeros((EDGES, 128 - width), BF16)
                us_ref[part, :, 0:128] = jnp.concatenate([u_ref[:, at : at + width], blank], axis=1)
                at = at + width
                us_ref[part, :, 128:256] = jnp.concatenate([u_ref[:, at : at + width], blank], axis=1)


def backward_edges(dagg_ref, t_ref, tt_ref, w0_ref, w1_ref, w2_ref, hb_ref, hs_ref, r_ref, v_ref, gate, tq,
                   dv_ref, dr_ref, w_ref):
    t_mat = t_ref[...]
    acc = jnp.zeros((EDGES, 128), F32)
    first = None
    for p in range(8):
        dm = dot(t_mat, dagg_ref[:, 256 * p : 256 * p + 256])
        for b in range(2):
            col = 256 * p + 128 * b
            part = dm[:, 128 * b : 128 * b + 128]
            acc = acc + part * v_ref[:, col : col + 128].astype(F32)
            scaled = part * gate
            if col == 0:
                first = scaled
            else:
                dv_ref[:, col : col + 128] = scaled.astype(BF16)
    a_hi, a_lo = split_hi_lo(acc)
    dalpha = dot(jnp.concatenate([a_hi, a_lo], axis=1), hb_ref[...])
    per = dalpha * gate * (1.0 - gate) * HEAD_SCALE
    dv_ref[:, 0:128] = (first + per * tq).astype(BF16)
    lane = lax.broadcasted_iota(jnp.int32, (EDGES, 128), 1)
    dq = jnp.where(lane < 64, per * v_ref[:, 0:128].astype(F32), 0.0).astype(BF16)
    dqn = dot(tt_ref[...], dq)

    def grads_of(col, width, weight_ref, row):
        if col == 0:
            return dot(dv_ref[:, col : col + width], weight_ref[:, row])
        return dot_nt(dv_ref[:, col : col + width], weight_ref[row, :])

    plans = (
        (SEGMENTS[0:4], None, 0, 512, w0_ref, 0),
        (SEGMENTS[4:7], SEGMENTS[7:10], 512, 768, w1_ref, 768),
        (SEGMENTS[10:13], SEGMENTS[13:16], 1280, 768, w2_ref, 640),
    )
    for plus, minus, col, width, weight_ref, half in plans:
        base = plus[0][0]
        for k, (c0, n, g0) in enumerate(plus):
            w = 128 * n
            at = 128 * (c0 - base)
            du = grads_of(col, width, weight_ref, pl.ds(at, w))
            dr = du * hs_ref[:, 128 * c0 : 128 * c0 + w].astype(F32)
            if w_ref is not None:
                rg = r_ref[:, 128 * g0 : 128 * g0 + w].astype(F32)
                w_ref[:, 128 * c0 : 128 * c0 + w] = (du * rg).astype(BF16)
            if minus is not None:
                m0 = minus[k][0]
                dum = grads_of(col, width, weight_ref, pl.ds(half + at, w))
                dr = dr + dum * hs_ref[:, 128 * m0 : 128 * m0 + w].astype(F32)
                if w_ref is not None:
                    w_ref[:, 128 * m0 : 128 * m0 + w] = (dum * rg).astype(BF16)
            dr_ref[:, 128 * g0 : 128 * g0 + w] = dr.astype(BF16)
    return dqn


def weight_grads(core, dy_ref, agg_ref, h0, dqn, ee_ref, selq_ref, selr_ref, us_ref, dv_ref, dr_ref, gm_ref, gs_ref):
    def put(row, val):
        n = val.shape[0]
        lo, hi = val[:, :128], val[:, 128:]
        gm_ref[row : row + n, :] = jnp.where(core == 0, lo, hi)
        gs_ref[row : row + n, :] = jnp.where(core == 0, hi, lo).astype(BF16)

    sums = [None] * 7
    for k, (c0, n, _) in enumerate(SEGMENTS):
        degs = PAIRS[PAIR_OF[k]]
        prod = dot_tn(agg_ref[:, 128 * k : 128 * k + 128], dy_ref[:, 128 * c0 : 128 * c0 + 128 * n])
        for m in range(n):
            piece = prod[64 * m : 64 * m + 64, 128 * m : 128 * m + 128]
            d = degs[m]
            sums[d] = piece if sums[d] is None else sums[d] + piece
    sums.append(dot_tn(dqn.astype(BF16), h0)[0:64])
    e_hi, e_lo = split_hi_lo(jnp.concatenate(sums, axis=0))
    selq = selq_ref[...]
    extra = dot(jnp.concatenate([e_hi, e_lo], axis=1), jnp.concatenate([selq, selq], axis=0))
    dv0t = dv_ref[:, 0:512].T
    put(0, dot(dv0t, us_ref[0]) + extra)
    up, um = us_ref[1], us_ref[2]
    dpt = dv_ref[:, 512:896].T
    dmt = dv_ref[:, 896:1280].T
    put(512, dot(dpt, up) + dot(dmt, um))
    put(896, dot(dmt, up) - dot(dpt, um))
    up, um = us_ref[3], us_ref[4]
    dpt = dv_ref[:, 1280:1664].T
    dmt = dv_ref[:, 1664:2048].T
    put(1280, dot(dpt, up) + dot(dmt, um))
    put(1664, dot(dmt, up) - dot(dpt, um))
    ees = dot_nt(selr_ref[...], ee_ref[...]).astype(BF16)
    for p in range(9):
        pr = dot(ees, dr_ref[:, 256 * p : 256 * p + 256])
        mine = jnp.where(core == 0, pr[0:16], pr[16:32])
        theirs = jnp.where(core == 0, pr[16:32], pr[0:16]).astype(BF16)
        for b in range(2):
            row = 2048 + 16 * (2 * p + b)
            gm_ref[row : row + 16, :] = mine[:, 128 * b : 128 * b + 128]
            gs_ref[row : row + 16, :] = theirs[:, 128 * b : 128 * b + 128]


def cot_block(cots, core, i):
    own, pair, near, near_pair, wide, wide_pair = cots
    m0, m1 = wide[0, i].astype(F32), wide[1, i].astype(F32)
    p0, p1 = wide_pair[0, i].astype(F32), wide_pair[1, i].astype(F32)
    rows = [r[i].astype(F32) for r in (own, pair, near, near_pair)]
    rows += [jnp.where(core == 0, a, b) for a, b in ((m0, p1), (m1, p0), (p1, m0), (p0, m1))]
    return jnp.concatenate(rows, axis=0)


def node_block(bufs, i):
    return jnp.concatenate([b[i] for b in bufs], axis=0)


def kernel_first(pos_ref, b0, b1, b2, b3, b4, b5, b6, b7, w0_ref, w1_ref, w2_ref, rad_ref, q_ref, hf_ref,
                 agg_ref, s_ref, t_ref, tt_ref, st_ref, ee_ref, v_ref, gate_ref, tq_ref, hs_ref, u_ref, h0_ref,
                 h_ref):
    bufs = [b0, b1, b2, b3, b4, b5, b6, b7]
    mask = 16 * pos_ref[0]
    iota = lax.broadcasted_iota(jnp.int32, (NODES, 128), 0)
    for k in range(4):
        buf = bufs[2 * k]
        ids = buf[38].astype(F32)
        src = ids[0:1].astype(jnp.int32) ^ mask
        tgt = ids[1:2].astype(jnp.int32) ^ mask
        s_hot = jnp.where(iota == src, 1.0, 0.0)
        t_hot = jnp.where(iota == tgt, 1.0, 0.0) * ids[2:3]
        st_ref[:, 128 * k : 128 * k + 128] = s_hot.astype(BF16)
        tt_ref[:, 128 * k : 128 * k + 128] = t_hot.astype(BF16)
        s_ref[128 * k : 128 * k + 128, :] = s_hot.T.astype(BF16)
        t_ref[128 * k : 128 * k + 128, :] = t_hot.T.astype(BF16)
        for m in range(8):
            ee_ref[128 * k + 16 * m : 128 * k + 16 * m + 16, :] = buf[30 + m]
    total = jnp.zeros((NODES, CH), F32)
    for i in range(LOW):
        x = node_block(bufs, i).astype(F32)
        total = total + x * x
    total = total + node_block(bufs, LOW).astype(F32)
    scale = lax.rsqrt(jnp.sum(total, axis=1, keepdims=True) * (1.0 / ENTRIES) + NORM_EPS)
    for i in range(LOW):
        h_ref[:, 128 * i : 128 * i + 128] = (node_block(bufs, i).astype(F32) * scale).astype(BF16)
    h0_ref[...] = h_ref[:, 0:128]

    def agg_store(col, val):
        agg_ref[:, col : col + 256] = val.astype(BF16)

    forward_edges(h_ref, s_ref, t_ref, tt_ref, ee_ref, w0_ref, w1_ref, w2_ref, rad_ref.at[0], q_ref, hf_ref,
                  u_ref, hs_ref, None, v_ref, gate_ref, tq_ref, agg_store)


def kernel_second(b0, b1, b2, b3, b4, b5, b6, b7, agg0_ref, agg0p_ref, s_ref, t_ref, tt_ref, ee_ref,
                  wd0_ref, w0_ref, w1_ref, w2_ref, rad_ref, q_ref, hf_ref,
                  x1_ref, s1_ref, own_ref, snd_ref, agg1_ref, h0_ref, hs_ref, r_ref, v_ref, gate_ref, tq_ref, u_ref,
                  h_ref):
    bufs = [b0, b1, b2, b3, b4, b5, b6, b7]
    total = node_block(bufs, LOW).astype(F32)
    for k, (c0, n, _) in enumerate(SEGMENTS):
        agg = agg0_ref[:, 128 * k : 128 * k + 128].astype(F32)
        agg = agg + swap16(agg0p_ref[:, 128 * k : 128 * k + 128]).astype(F32)
        out = dot(agg.astype(BF16), wd0_ref[PAIR_OF[k]])
        for m in range(n):
            x = node_block(bufs, c0 + m).astype(F32) + out[:, 128 * m : 128 * m + 128]
            x1_ref[:, 128 * (c0 + m) : 128 * (c0 + m) + 128] = x
            total = total + x * x
    scale = lax.rsqrt(jnp.sum(total, axis=1, keepdims=True) * (1.0 / ENTRIES) + NORM_EPS)
    s1_ref[...] = jnp.broadcast_to(scale, (NODES, 128))
    for i in range(LOW):
        h_ref[:, 128 * i : 128 * i + 128] = (x1_ref[:, 128 * i : 128 * i + 128] * scale).astype(BF16)
    h0_ref[...] = h_ref[:, 0:128]

    def agg_store(col, val):
        agg1_ref[:, col : col + 256] = val.astype(BF16)
        own_ref[:, col : col + 256] = val[0:16]
        snd_ref[:, col : col + 256] = val[16:32].astype(BF16)

    forward_edges(h_ref, s_ref, t_ref, tt_ref, ee_ref, w0_ref, w1_ref, w2_ref, rad_ref.at[1], q_ref, hf_ref,
                  u_ref, hs_ref, r_ref, v_ref, gate_ref, tq_ref, agg_store)


def kernel_back(pos_ref, c0_, c1_, c2_, c3_, c4_, c5_, t_ref, tt_ref, st_ref, v_ref, gate_ref, tq_ref, hs_ref, r_ref,
                wd1_ref, w0_ref, w1_ref, w2_ref, q_ref, hb_ref,
                dh_ref, dy_ref, dv_ref, dr_ref, dqn_ref,
                dagg_ref, w_ref):
    core = pos_ref[0] & 1
    cots = [c0_, c1_, c2_, c3_, c4_, c5_]
    for i in range(LOW):
        dy_ref[:, 128 * i : 128 * i + 128] = cot_block(cots, core, i).astype(BF16)
    for k, (c0, n, _) in enumerate(SEGMENTS):
        w = 128 * n
        dagg_ref[:, 128 * k : 128 * k + 128] = dot_nt(
            dy_ref[:, 128 * c0 : 128 * c0 + w], wd1_ref[PAIR_OF[k], :, 0:w]
        ).astype(BF16)
    dqn = backward_edges(dagg_ref, t_ref, tt_ref, w0_ref, w1_ref, w2_ref, hb_ref, hs_ref, r_ref, v_ref,
                         gate_ref[...], tq_ref[...], dv_ref, dr_ref, w_ref)
    dqn_ref[...] = dqn
    st = st_ref[...]
    d_hi, d_lo = split_hi_lo(dqn)
    back = dot(jnp.concatenate([d_hi, d_lo], axis=1), jnp.concatenate([q_ref[...], q_ref[...]], axis=0))
    for c0, n, _ in SEGMENTS:
        w = 128 * n
        val = dot(st, w_ref[:, 128 * c0 : 128 * c0 + w])
        if c0 == 0:
            val = val + jnp.concatenate([back, jnp.zeros((NODES, 128), F32)], axis=1)
        dh_ref[:, 128 * c0 : 128 * c0 + w] = val.astype(BF16)


def kernel_grads(pos_ref, dy_ref, agg_ref, h0_ref, dqn_ref, ee_ref, us_ref, dv_ref, dr_ref,
                 selq_ref, selr_ref, gm_ref, gs_ref):
    weight_grads(pos_ref[0] & 1, dy_ref, agg_ref, h0_ref[...], dqn_ref[...], ee_ref, selq_ref, selr_ref,
                 us_ref, dv_ref, dr_ref, gm_ref, gs_ref)


def kernel_third(pos_ref, c0_, c1_, c2_, c3_, c4_, c5_, x1_ref, s1_ref, dh_ref, dhp_ref,
                 agg0_ref, t_ref, tt_ref, ee_ref, v_ref, gate_ref, tq_ref, hs_ref, us_ref, h0_ref,
                 wd0_ref, w0_ref, w1_ref, w2_ref, hb_ref, selq_ref, selr_ref,
                 gm_ref, gs_ref,
                 dy_ref, dagg_ref, dv_ref, dr_ref, full_ref):
    core = pos_ref[0] & 1
    cots = [c0_, c1_, c2_, c3_, c4_, c5_]
    inner = jnp.zeros((NODES, 128), F32)
    for i in range(LOW):
        cols = pl.ds(128 * i, 128)
        dh = dh_ref[:, cols].astype(F32) + swap16(dhp_ref[:, cols]).astype(F32)
        full_ref[:, cols] = dh
        inner = inner + dh * x1_ref[:, cols]
    s1 = s1_ref[...]
    coef = jnp.sum(inner, axis=1, keepdims=True) * (1.0 / ENTRIES) * (s1 * s1 * s1)
    for i in range(LOW):
        cols = pl.ds(128 * i, 128)
        dx = cot_block(cots, core, i) + s1 * full_ref[:, cols] - x1_ref[:, cols] * coef
        dy_ref[:, cols] = dx.astype(BF16)
    for k, (c0, n, _) in enumerate(SEGMENTS):
        w = 128 * n
        dagg_ref[:, 128 * k : 128 * k + 128] = dot_nt(
            dy_ref[:, 128 * c0 : 128 * c0 + w], wd0_ref[PAIR_OF[k], :, 0:w]
        ).astype(BF16)
    dqn = backward_edges(dagg_ref, t_ref, tt_ref, w0_ref, w1_ref, w2_ref, hb_ref, hs_ref, None, v_ref,
                         gate_ref[...], tq_ref[...], dv_ref, dr_ref, None)
    weight_grads(pos_ref[0] & 1, dy_ref, agg0_ref, h0_ref[...], dqn, ee_ref, selq_ref, selr_ref,
                 us_ref, dv_ref, dr_ref, gm_ref, gs_ref)


def kernel_output(nf_ref, x1_ref, own_ref, rcv_ref, wd1_ref, x2_ref):
    for k, (c0, n, _) in enumerate(SEGMENTS):
        w = 128 * n
        agg = own_ref[:, 128 * k : 128 * k + 128] + rcv_ref[:, 128 * k : 128 * k + 128].astype(F32)
        out = dot(agg.astype(BF16), wd1_ref[PAIR_OF[k], :, 0:w])
        out = (x1_ref[0:16, 128 * c0 : 128 * c0 + w] + out).astype(BF16)
        for m in range(n):
            x2_ref[c0 + m] = out[:, 128 * m : 128 * m + 128]
    x2_ref[LOW:] = nf_ref[LOW:]


def kernel_chunks(mine, other, chunk_ref, g_ref):
    lane14 = lax.broadcasted_iota(jnp.int32, (16, 128), 1)
    g_ref[...] = mine[...] + other[...].astype(F32)
    for d in range(32):
        chunk_ref[d, 0:14, :] = g_ref[14 * d : 14 * d + 14, :]
        chunk_ref[d, 14:38, :] = g_ref[512 + 24 * d : 536 + 24 * d, :]
        row = 1280 + 20 * d + (64 if d >= 16 else 0)
        chunk_ref[d, 38:56, :] = g_ref[row : row + 18, :]
        last = g_ref[row + 18 : row + 20, :]
        for k in range(3):
            chunk_ref[d, 32 + 2 * k : 34 + 2 * k, 96:128] = pltpu.roll(last, 96 - 32 * k, 1)[:, 96:128]
        for q in range(7):
            chunk_ref[d, 2 * q : 2 * q + 2, 112:128] = g_ref[64 * q + 2 * d : 64 * q + 2 * d + 2, 112:128]
        chunk_ref[d, 14:16, 112:128] = g_ref[448 + 2 * d : 450 + 2 * d, 112:128]
        for start, width, at, to in ((72 * d, 48, 80, 38), (72 * d + 48, 24, 96, 16)):
            blk, off = start // 128, start % 128
            shift = (at - off) % 128
            left = g_ref[2048 + 16 * blk : 2064 + 16 * blk, :]
            win = pltpu.roll(left, shift, 1) if shift else left
            if off + width > 128:
                right = g_ref[2064 + 16 * blk : 2080 + 16 * blk, :]
                right = pltpu.roll(right, shift, 1) if shift else right
                win = jnp.where(lane14 < at + 128 - off, win, right)
            chunk_ref[d, to : to + 16, at : at + width] = win[:, at : at + width]


def kernel_pack(mine, other, late_ref, out_ref, g_ref, chunk_ref):
    kernel_chunks(mine, other, chunk_ref, g_ref)
    for d in range(32):
        both = jnp.concatenate([chunk_ref[d], late_ref[d]], axis=0)
        out_ref[d % 16, 112 * (d // 16) : 112 * (d // 16) + 112, :] = both.astype(BF16)


def kernel_plane(half_ref, in_ref, own_ref, snd_ref):
    for h in range(2):
        acc = in_ref[0, 112 * h : 112 * h + 112].astype(F32)
        for d in range(1, 16):
            acc = acc + in_ref[d, 112 * h : 112 * h + 112].astype(F32)

        @pl.when(half_ref[0] == h)
        def _():
            own_ref[...] = acc

        @pl.when(half_ref[0] != h)
        def _():
            snd_ref[...] = acc.astype(BF16)


def kernel_finish(in_ref, rcv_ref, zero_ref, one_ref, two_ref, rad_ref, q_ref, out_ref, acc_ref):
    acc_ref[...] = in_ref[...] + rcv_ref[...].astype(F32)
    lane = lax.broadcasted_iota(jnp.int32, (16, 128), 1)
    for layer in range(2):
        b = 56 * layer
        for r in range(14):
            zero_ref[r, layer : layer + 1, :] = acc_ref[b + r : b + r + 1, 0:112]
        one_ref[layer] = acc_ref[b + 14 : b + 38, 0:96]
        for r in range(18):
            two_ref[r, layer : layer + 1, :] = acc_ref[b + 38 + r : b + 39 + r, 0:80]
        first, second, third = [
            pltpu.roll(acc_ref[b + 32 + 2 * k : b + 34 + 2 * k, :], 32 + 32 * k, 1) for k in range(3)
        ]
        lane2 = lax.broadcasted_iota(jnp.int32, (2, 128), 1)
        last = jnp.where(lane2 < 32, first, jnp.where(lane2 < 64, second, third))
        for r in range(2):
            two_ref[18 + r, layer : layer + 1, :] = last[r : r + 1, 0:80]
        q_ref[layer] = pltpu.roll(acc_ref[b + 14 : b + 16, :], 16, 1)[:, 0:16]
        low = pltpu.roll(acc_ref[b + 38 : b + 54, :], 48, 1)
        high = pltpu.roll(acc_ref[b + 16 : b + 32, :], 80, 1)
        rad_ref[layer] = jnp.where(lane < 48, low, high)[:, 0:72]
        tail = pltpu.roll(acc_ref[b : b + 16, :], 16, 1)
        for q in range(7):
            out_ref[layer, q] = tail[2 * q : 2 * q + 2, 0:16]


def kernel_load(nf_ref, ee_ref, src_ref, tgt_ref, count_ref, cot_ref, own_ref, low_cot_ref,
                tail_ref, ids_ref, count_smem, sems):
    copies = [
        pltpu.make_async_copy(nf_ref.at[pl.ds(LOW, 20)], tail_ref, sems.at[0]),
        pltpu.make_async_copy(src_ref, ids_ref.at[0], sems.at[1]),
        pltpu.make_async_copy(tgt_ref, ids_ref.at[1], sems.at[2]),
        pltpu.make_async_copy(count_ref, count_smem, sems.at[3]),
        pltpu.make_async_copy(nf_ref.at[pl.ds(0, LOW)], own_ref.at[pl.ds(0, LOW)], sems.at[4]),
        pltpu.make_async_copy(ee_ref, own_ref.at[pl.ds(30, 8)], sems.at[5]),
        pltpu.make_async_copy(cot_ref.at[pl.ds(0, LOW)], low_cot_ref, sems.at[6]),
    ]
    for copy in copies:
        copy.start()
    copies[0].wait()
    tail = jnp.zeros((16, 128), F32)
    for i in range(20):
        x = tail_ref[i].astype(F32)
        tail = tail + x * x
    tail = jnp.broadcast_to(jnp.sum(tail, axis=1, keepdims=True), (16, 128))
    lane = lax.broadcasted_iota(jnp.int32, (16, 128), 1)
    hi = tail.astype(BF16).astype(F32)
    mid = (tail - hi).astype(BF16).astype(F32)
    pieces = jnp.where(lane == 0, hi, jnp.where(lane == 1, mid, jnp.where(lane == 2, tail - hi - mid, 0.0)))
    own_ref[LOW] = pieces.astype(BF16)
    for copy in copies[1:4]:
        copy.wait()
    row = lax.broadcasted_iota(jnp.int32, (16, 128), 0)
    live = jnp.where(lane < count_smem[0, 0], 1.0, 0.0)
    src = jnp.broadcast_to(ids_ref[0], (16, 128)).astype(F32)
    tgt = jnp.broadcast_to(ids_ref[1], (16, 128)).astype(F32)
    ids = jnp.where(row == 0, src, jnp.where(row == 1, tgt, jnp.where(row == 2, live, 0.0)))
    own_ref[38] = ids.astype(BF16)
    for copy in copies[4:]:
        copy.wait()


def kernel_weights(pos_ref, zero_ref, one_ref, two_ref, query_ref, out_ref, *outs):
    selq_ref, selr_ref = outs[10:]
    z_lo = pos_ref[0] // 2
    for k in range(2):
        w0_ref, w1_ref, w2_ref, q_ref, wd_ref = outs[5 * k : 5 * k + 5]
        w0_ref[0:448, :] = zero_ref[k]
        w0_ref[448:512, :] = jnp.zeros((64, 896), BF16)
        a, b = one_ref[k, :, 0:384], one_ref[k, :, 384:768]
        w1_ref[0:768, 0:384] = a
        w1_ref[0:768, 384:768] = b
        w1_ref[768:1536, 0:384] = -b
        w1_ref[768:1536, 384:768] = a
        blank = jnp.zeros((640, 64), BF16)
        a = jnp.concatenate([two_ref[k, :, 0:320], blank], axis=1)
        b = jnp.concatenate([two_ref[k, :, 320:640], blank], axis=1)
        w2_ref[0:640, 0:384] = a
        w2_ref[0:640, 384:768] = b
        w2_ref[640:1280, 0:384] = -b
        w2_ref[640:1280, 384:768] = a
        q_ref[0:64, :] = query_ref[k]
        q_ref[64:128, :] = jnp.zeros((64, 128), BF16)
        none = jnp.zeros((64, 128), BF16)
        for p, (d, e) in enumerate(PAIRS):
            wd_ref[p, 0:64, 0:128] = out_ref[k, d]
            wd_ref[p, 0:64, 128:256] = none
            wd_ref[p, 64:128, 0:128] = none
            wd_ref[p, 64:128, 128:256] = none if e is None else out_ref[k, e]

    def select(rows, width, first_lane, scale):
        k = lax.broadcasted_iota(jnp.int32, (rows, 128), 0)
        m = lax.broadcasted_iota(jnp.int32, (rows, 128), 1) - first_lane
        live = (m >= 0) & (m < width)
        lo = jnp.where(live & (k == scale * z_lo + m), 1.0, 0.0)
        hi = jnp.where(live & (k == scale * z_lo + width + m), 1.0, 0.0)
        return jnp.concatenate([lo, hi], axis=1).astype(BF16)

    selq = select(128, 16, 112, 32)
    selq_ref[...] = selq
    rows = lax.broadcasted_iota(jnp.int32, (32, 128), 0)
    cols = lax.broadcasted_iota(jnp.int32, (32, 128), 1)
    selr_ref[...] = jnp.where(cols == 32 * z_lo + rows, 1.0, 0.0).astype(BF16)


def call(body, outs, scratch, n_in, limit=16, cost=None):
    return pl.pallas_call(
        body,
        in_specs=[pl.BlockSpec(memory_space=pltpu.SMEM)] + [pl.BlockSpec(memory_space=pltpu.VMEM)] * (n_in - 1),
        out_specs=[pl.BlockSpec(memory_space=pltpu.VMEM)] * len(outs),
        out_shape=[jax.ShapeDtypeStruct(s, t) for s, t in outs],
        scratch_shapes=[pltpu.VMEM(s, t) for s, t in scratch],
        compiler_params=pltpu.CompilerParams(vmem_limit_bytes=limit * MIB),
        cost_estimate=cost,
    )


def plain_call(body, outs, scratch, limit=16):
    return pl.pallas_call(
        body,
        out_shape=[jax.ShapeDtypeStruct(s, t) for s, t in outs],
        scratch_shapes=[pltpu.VMEM(s, t) for s, t in scratch],
        compiler_params=pltpu.CompilerParams(vmem_limit_bytes=limit * MIB),
    )


def swap(x, bits):
    return lax.ppermute(x, "graph", [(i, i ^ bits) for i in range(8)])


def shards(node_features, edge_embed, sources, targets, edge_counts, w_zero, w_one, w_two, radial, query, w_out, cotangent):
    pos_arr = lax.axis_index("graph").astype(jnp.int32)[None]
    nf = jnp.transpose(node_features[0], (1, 0, 2))
    shard = (16, 128)
    own, cot = pl.pallas_call(
        kernel_load,
        in_specs=[pl.BlockSpec(memory_space=pltpu.HBM)] * 6,
        out_specs=[pl.BlockSpec(memory_space=pltpu.VMEM)] * 2,
        out_shape=[jax.ShapeDtypeStruct((39, *shard), BF16), jax.ShapeDtypeStruct((LOW, *shard), BF16)],
        scratch_shapes=[
            pltpu.VMEM((20, *shard), BF16), pltpu.VMEM((2, 1, 128), jnp.int32), pltpu.SMEM((1, 1), jnp.int32),
            pltpu.SemaphoreType.DMA((7,)),
        ],
        compiler_params=pltpu.CompilerParams(vmem_limit_bytes=56 * MIB),
    )(nf, edge_embed[0].reshape(8, 16, 128), sources, targets, edge_counts, jnp.transpose(cotangent[0], (1, 0, 2)))
    far = [swap(own, k) for k in (2, 4, 6)]

    forms = [((512, 896), BF16), ((1536, 768), BF16), ((1280, 768), BF16), ((128, 128), BF16), ((7, 128, 256), BF16)]
    *forms, selq, selr = call(
        kernel_weights,
        forms * 2 + [((128, 256), BF16), ((32, 128), BF16)],
        [],
        6,
    )(pos_arr, jnp.swapaxes(w_zero, 1, 2), w_one, w_two, jnp.swapaxes(query, 1, 2), w_out)
    cot_pair = swap(cot, 1)
    both = jnp.stack([cot, cot_pair])
    far = [lax.optimization_barrier((b, selr, both))[0] for b in far]
    pair = [swap(b, 1) for b in [own] + far]
    bufs = [own, pair[0], far[0], pair[1], far[1], pair[2], far[2], pair[3]]
    near = swap(cot, 2)
    wide = lax.ppermute(both, "graph", [(i, i ^ (6 if i % 2 else 4)) for i in range(8)])
    w0p, w1c, w2c, qp, wd = [[forms[m], forms[5 + m]] for m in range(5)]
    hf = jnp.asarray(HEAD_FIRST, BF16)
    hb = jnp.asarray(HEAD_BOTH, BF16)

    big = (EDGES, LOW * CH)
    agg0, s_mat, t_mat, tt, st, ee, v0, gate0, tq0, hs0, u0, h00 = call(
        kernel_first,
        [((NODES, 2048), BF16), ((EDGES, 128), BF16), ((EDGES, 128), BF16), ((128, EDGES), BF16),
         ((128, EDGES), BF16), ((EDGES, 128), BF16), ((EDGES, 2048), BF16), ((EDGES, 128), F32),
         ((EDGES, 128), F32), (big, BF16), (big, BF16), ((NODES, 128), BF16)],
        [((NODES, LOW * CH), BF16)],
        15,
        LIM_A,
    )(pos_arr, *bufs, w0p[0], w1c[0], w2c[0], radial, qp[0], hf)
    agg0p = swap(agg0, 1)
    (us0,) = call(select_rows, [((5, EDGES, 256), BF16)], [], 2, 8)(pos_arr, u0)
    agg0p, us0 = lax.optimization_barrier((agg0p, us0))
    grad_rows = 2048 + 288
    x1, s1, own1, snd1, agg1, h01, hs1, r1, v1, gate1, tq1, u1 = plain_call(
        kernel_second,
        [((NODES, LOW * CH), F32), ((NODES, 128), F32), ((16, 2048), F32), ((16, 2048), BF16),
         ((NODES, 2048), BF16), ((NODES, 128), BF16), (big, BF16), ((EDGES, 2304), BF16), ((EDGES, 2048), BF16),
         ((EDGES, 128), F32), ((EDGES, 128), F32), (big, BF16)],
        [((NODES, LOW * CH), BF16)],
        LIM_B,
    )(*bufs, agg0, agg0p, s_mat, t_mat, tt, ee, wd[0], w0p[1], w1c[1], w2c[1], radial, qp[1], hf)
    rcv1 = swap(snd1, 1)
    near, wide, agg1 = lax.optimization_barrier((near, wide, agg1))
    cots = [cot, cot_pair, near, swap(near, 1), wide, swap(wide, 1)]
    (us1,) = call(select_rows, [((5, EDGES, 256), BF16)], [], 2, 8)(pos_arr, u1)
    cots[5], us1 = lax.optimization_barrier((cots[5], us1))
    dh, dy1, dv1, dr1, dqn1 = call(
        kernel_back,
        [((NODES, LOW * CH), BF16), ((NODES, LOW * CH), BF16), ((EDGES, 2048), BF16), ((EDGES, 2304), BF16),
         ((NODES, 128), F32)],
        [((NODES, 2048), BF16), (big, BF16)],
        21,
        LIM_D,
    )(pos_arr, *cots, t_mat, tt, st, v1, gate1, tq1, hs1, r1, wd[1], w0p[1], w1c[1], w2c[1], qp[1], hb)
    dhp = swap(dh, 1)
    gm1, gs1 = call(
        kernel_grads,
        [((grad_rows, 128), F32), ((grad_rows, 128), BF16)],
        [],
        11,
        LIM_E,
    )(pos_arr, dy1, agg1, h01, dqn1, ee, us1, dv1, dr1, selq, selr)
    gp1 = swap(gs1, 1)
    gm0, gs0 = call(
        kernel_third,
        [((grad_rows, 128), F32), ((grad_rows, 128), BF16)],
        [((NODES, LOW * CH), BF16), ((NODES, 2048), BF16), ((EDGES, 2048), BF16), ((EDGES, 2304), BF16),
         ((NODES, LOW * CH), F32)],
        28,
        LIM_C,
    )(pos_arr, *cots, x1, s1, dh, dhp, agg0, t_mat, tt, ee, v0, gate0, tq0, hs0, us0, h00,
      wd[0], w0p[0], w1c[0], w2c[0], hb, selq, selr)
    gp0 = swap(gs0, 1)
    gm1, gp1, own1, _ = lax.optimization_barrier((gm1, gp1, own1, gm0))
    (x2,) = plain_call(kernel_output, [((49, 16, 128), BF16)], [])(nf, x1, own1, rcv1, wd[1])
    (late,) = plain_call(kernel_chunks, [((32, 56, 128), F32)], [((grad_rows, 128), F32)])(gm1, gp1)
    (packed,) = plain_call(
        kernel_pack, [((16, 224, 128), BF16)], [((grad_rows, 128), F32), ((32, 56, 128), F32)]
    )(gm0, gp0, late)
    planes = [[16 * h + a for a in range(16)] for h in range(2)]
    moved = lax.all_to_all(packed, "dp", split_axis=0, concat_axis=0, tiled=True, axis_index_groups=planes)
    moved, x2 = lax.optimization_barrier((moved, x2))
    half = (lax.axis_index("dp") // 16).astype(jnp.int32)[None]
    mine, theirs = call(kernel_plane, [((112, 128), F32), ((112, 128), BF16)], [], 2)(half, moved)
    theirs = lax.ppermute(theirs, "dp", [(i, i ^ 16) for i in range(32)])
    result = jnp.transpose(x2, (1, 0, 2))[None]
    zero, one, two, rad, q, out = plain_call(
        kernel_finish,
        [((14, 2, 112), F32), ((2, 24, 96), F32), ((20, 2, 80), F32), ((2, 16, 72), F32),
         ((2, 2, 16), F32), ((2, 7, 2, 16), F32)],
        [((112, 128), F32)],
    )(mine, theirs)
    return (
        result,
        jnp.transpose(zero, (1, 2, 0)),
        jnp.transpose(one, (0, 2, 1)),
        jnp.transpose(two, (1, 2, 0)),
        rad,
        jnp.transpose(q, (0, 2, 1)),
        out,
    )


def solution(mesh):
    by_graph = P("dp", "graph")
    in_specs = (
        P("dp", "graph", None, None),
        P("dp", "graph", None),
        by_graph,
        by_graph,
        by_graph,
        P(),
        P(),
        P(),
        P(),
        P(),
        P(),
        P("dp", "graph", None, None),
    )
    out_specs = (
        P("dp", "graph", None, None),
        P(None, "graph", "dp"),
        P(None, "graph", "dp"),
        P(None, "graph", "dp"),
        P(None, "graph", "dp"),
        P(None, "graph", "dp"),
        P(None, None, "dp", "graph"),
    )
    return jax.shard_map(shards, mesh=mesh, in_specs=in_specs, out_specs=out_specs, check_vma=False)
```
